128 devices in a mesh: shot: 4 (over x), gx: 4 (over y_lo, core), gy: 8 (over y_hi, z).
Axes of the slice: x: 4, y: 4 (y_hi: 2, y_lo: 2; y = y_hi * 2 + y_lo), z: 4, core: 2. Of those that a mesh axis runs over, the one named last changes fastest.
Arguments:
- velocity: float32 [256, 512, 128], P(('shot', 'gx'), 'gy'), may hold values from 1.5 to 4.5
- density: float32 [256, 512, 128], P(('shot', 'gx'), 'gy'), may hold values from 1 to 3
- offsets: int32 [4, 2], replicated, may hold values from 0 to 256, as said below
- pressure: float32 [4, 128, 256, 128], P('shot', 'gx', 'gy'), may hold values from -6 to 6
- vel_x: float32 [4, 128, 256, 128], P('shot', 'gx', 'gy'), may hold values from -0.6 to 0.6
- vel_y: float32 [4, 128, 256, 128], P('shot', 'gx', 'gy'), may hold values from -0.6 to 0.6
- vel_z: float32 [4, 128, 256, 128], P('shot', 'gx', 'gy'), may hold values from -0.6 to 0.6
- source_cells: int32 [4, 3], replicated, may hold values from 0 to 255, as said below
- wavelet: float32 [4, 4], replicated, may hold values from -120 to 120
Outputs:
- pressure_out: float32 [4, 128, 256, 128], P('shot', 'gx', 'gy')
- vel_x_out: float32 [4, 128, 256, 128], P('shot', 'gx', 'gy')
- vel_y_out: float32 [4, 128, 256, 128], P('shot', 'gx', 'gy')
- vel_z_out: float32 [4, 128, 256, 128], P('shot', 'gx', 'gy')
The draws below stay inside these ranges and needn't reach their ends.
Inputs may be any that keep to these rules, and one draw needn't show every extreme that they name: `offsets`: every aperture lies inside the model: x corner at most 128, y corner at most 256; one shot's x corner and another's y corner are at those ends. `source_cells`: every source cell lies inside its aperture: x below 128, y below 256, depth below 128; some shots' sources lie on the far ends of x, y and depth.
All inputs are finite; a program needn't handle non-finite values.
Results may differ from the reference program's by a relative error of at most 0.0003.
Values sent between devices are 32-bit elements; how exact they have to be, the bound alone decides.
No kernel may reach another device: no remote copies, remote signals or barrier semaphores. Data moves between devices by JAX's collectives and lax.ppermute only.
A program may use at most 128 MiB of HBM per device.

```python
import math
import jax
import jax.numpy as jnp
from jax import lax

NZ = 128
STEPS = 4
MX = 256
MY = 512
AX = 128
AY = 256
N_SHOT = 4


def draw_offsets(key, part):
    key = jax.random.fold_in(key, 11)
    keys = jax.random.split(key, 3)
    order = jax.random.permutation(keys[0], N_SHOT)
    across = jax.random.randint(keys[1], (N_SHOT,), 0, MX - AX + 1)
    along = jax.random.randint(keys[2], (N_SHOT,), 0, MY - AY + 1)
    shots = jnp.arange(N_SHOT)
    across = jnp.where(shots == order[0], MX - AX, across)
    along = jnp.where(shots == order[1], MY - AY, along)
    return jnp.stack([across, along], axis=1).astype(jnp.int32)


def draw_source_cells(key, part):
    key = jax.random.fold_in(key, 23)
    keys = jax.random.split(key, 4)
    order = jax.random.permutation(keys[0], N_SHOT)
    across = jax.random.randint(keys[1], (N_SHOT,), 0, AX)
    along = jax.random.randint(keys[2], (N_SHOT,), 0, AY)
    depth = jax.random.randint(keys[3], (N_SHOT,), 0, NZ)
    shots = jnp.arange(N_SHOT)
    across = jnp.where(shots == order[0], AX - 1, across)
    along = jnp.where(shots == order[1], AY - 1, along)
    depth = jnp.where(shots == order[2], NZ - 1, depth)
    return jnp.stack([across, along, depth], axis=1).astype(jnp.int32)


def block_levels(own_key, shape, cuts, least, high):
    def one(axis_at, shards_of):
        steps = jax.random.uniform(jax.random.fold_in(jax.random.fold_in(own_key, 6), axis_at), (shards_of,), jnp.float32, least / len(cuts), high / len(cuts))
        return jnp.repeat(jnp.exp(steps), shape[axis_at] // shards_of).reshape((-1,) + (1,) * (len(shape) - axis_at - 1))

    factor_of = one(*cuts[0])
    for cut in cuts[1:]:
        factor_of = factor_of * one(*cut)
    return factor_of


def gaussian(own_key, shape, scale, most, cuts=(), kind=jnp.bfloat16):
    result = jax.random.normal(own_key, shape, jnp.float32) * scale
    if len(cuts) > 0:
        result = block_levels(own_key, shape, cuts, -0.22, 0.18) * result
    return jnp.clip(result, min=-most, max=most).astype(kind)


def setup_inputs(seed: int = 0) -> dict:
    key_of = jax.random.split(jax.random.key(seed), 10)
    return {
        "velocity": jnp.clip(1.5 + 3.0 * jax.random.uniform(key_of[0], (MX, MY, NZ), jnp.float32) ** block_levels(key_of[0], (MX, MY, NZ), ((0, 16), (1, 8)), -0.2, 0.2), 1.5, 4.5),
        "density": jnp.clip(jnp.exp(math.log(3.0) - 1.0986123 * jax.random.uniform(key_of[1], (MX, MY, NZ), jnp.float32) ** block_levels(key_of[1], (MX, MY, NZ), ((0, 16), (1, 8)), -0.2, 0.2)), 1.0, 3.0),
        "offsets": draw_offsets(jax.random.fold_in(key_of[9], 71), 0),
        "pressure": gaussian(key_of[3], (N_SHOT, AX, AY, NZ), 1.0, 6.0, ((0, 4), (1, 4), (2, 8)), jnp.float32),
        "vel_x": gaussian(key_of[4], (N_SHOT, AX, AY, NZ), 0.1, 0.6, ((0, 4), (1, 4), (2, 8)), jnp.float32),
        "vel_y": gaussian(key_of[5], (N_SHOT, AX, AY, NZ), 0.1, 0.6, ((0, 4), (1, 4), (2, 8)), jnp.float32),
        "vel_z": gaussian(key_of[6], (N_SHOT, AX, AY, NZ), 0.1, 0.6, ((0, 4), (1, 4), (2, 8)), jnp.float32),
        "source_cells": draw_source_cells(jax.random.fold_in(key_of[9], 71), 0),
        "wavelet": gaussian(key_of[8], (N_SHOT, STEPS), 20.0, 120.0, (), jnp.float32),
    }


coefs = (1225.0 / 1024.0, -245.0 / 3072.0, 49.0 / 5120.0, -5.0 / 7168.0)
time_step = 0.09


def stencil(padded, axis, count):
    total = None
    for reach in range(1, 5):
        upper = lax.slice_in_dim(padded, 3 + reach, 3 + reach + count, axis=axis)
        lower = lax.slice_in_dim(padded, 4 - reach, 4 - reach + count, axis=axis)
        term = coefs[reach - 1] * (upper - lower)
        total = term if total is None else total + term
    return total


def pad_axis(field, axis, before, after):
    widths = [(0, 0), (0, 0), (0, 0)]
    widths[axis] = (before, after)
    return jnp.pad(field, widths)


def reference(velocity, density, offsets, pressure, vel_x, vel_y, vel_z, source_cells, wavelet):
    def one_shot(index):
        corner = offsets[index].astype(jnp.int32)
        start = (corner[0], corner[1], jnp.int32(0))
        speed = lax.dynamic_slice(velocity, start, (AX, AY, NZ))
        rho = lax.dynamic_slice(density, start, (AX, AY, NZ))
        buoyancy = 1.0 / rho
        modulus = rho * speed * speed
        source = source_cells[index]
        amplitude = wavelet[index]
        across = jnp.arange(AX, dtype=jnp.int32)
        along = jnp.arange(AY, dtype=jnp.int32)
        depth = jnp.arange(NZ, dtype=jnp.int32)
        hit = (across == source[0])[:, None, None] & (along == source[1])[None, :, None] & (depth == source[2])[None, None, :]
        inject = jnp.where(hit, jnp.float32(1.0), jnp.float32(0.0))
        pres = pressure[index]
        flow_x = vel_x[index]
        flow_y = vel_y[index]
        flow_z = vel_z[index]
        for step in range(STEPS):
            grad_x = stencil(pad_axis(pres, 0, 3, 4), 0, AX)
            grad_y = stencil(pad_axis(pres, 1, 3, 4), 1, AY)
            grad_z = stencil(pad_axis(pres, 2, 3, 4), 2, NZ)
            flow_x = flow_x - time_step * buoyancy * grad_x
            flow_y = flow_y - time_step * buoyancy * grad_y
            flow_z = flow_z - time_step * buoyancy * grad_z
            spread = stencil(pad_axis(flow_x, 0, 4, 3), 0, AX) + stencil(pad_axis(flow_y, 1, 4, 3), 1, AY) + stencil(pad_axis(flow_z, 2, 4, 3), 2, NZ)
            pres = pres - time_step * modulus * spread + time_step * amplitude[step] * inject
        return pres, flow_x, flow_y, flow_z

    results = lax.map(one_shot, jnp.arange(N_SHOT, dtype=jnp.int32))
    return (results[0], results[1], results[2], results[3])
```

```python
import functools

import jax
import jax.numpy as jnp
import numpy as np
from jax import lax
from jax.experimental import pallas as pl
from jax.experimental.pallas import tpu as pltpu
from jax.sharding import PartitionSpec as P

CX = 32
CY = 32
STEPS = 4
HALO = 7
WIDE = 40
PAD = 48
LINE = 80
DEVICES = ("shot", "gx", "gy")

coefs = (1225.0 / 1024.0, -245.0 / 3072.0, 49.0 / 5120.0, -5.0 / 7168.0)
time_step = 0.09

f32 = jnp.float32
bf16 = jnp.bfloat16


def depth_matrices():
    out = []
    for lead in (0, 1):
        full = np.zeros((128, 128), np.float32)
        for reach in range(1, 5):
            for k in range(128):
                up, down = k + reach - lead, k - reach + 1 - lead
                if up < 128:
                    full[up, k] += np.float32(coefs[reach - 1])
                if down >= 0:
                    full[down, k] -= np.float32(coefs[reach - 1])
        high = full.astype(jnp.bfloat16)
        low = (full - high.astype(np.float32)).astype(jnp.bfloat16)
        out.append(np.concatenate([high, high, low], axis=0))
    return out


def depth_difference(values, mat_ref):
    high = values.astype(bf16)
    low = (values - high.astype(f32)).astype(bf16)
    main = jnp.dot(
        jnp.concatenate([high, low], axis=1), mat_ref[0:256, :], preferred_element_type=f32
    )
    return main + jnp.dot(high, mat_ref[256:384, :], preferred_element_type=f32)


def forward(taps, at):
    total = None
    for reach in range(1, 5):
        term = coefs[reach - 1] * (taps[at + 3 + reach] - taps[at + 4 - reach])
        total = term if total is None else total + term
    return total


def backward(taps, at):
    total = None
    for reach in range(1, 5):
        term = coefs[reach - 1] * (taps[at + 3 + reach] - taps[at + 4 - reach])
        total = term if total is None else total + term
    return total


def every(ref, start, step):
    return ref[pl.ds(start, 8, stride=step), :]


def put_every(ref, start, step, value):
    ref[pl.ds(start, 8, stride=step), :] = value


def send_faces(info, field, x_pair, y_pair, base, count):
    odd_x, odd_y = info[8], info[9]
    for which, ref in enumerate(x_pair):
        high = (odd_x == 0) if which == 0 else (odd_x == 1)
        start = pl.multiple_of(jnp.where(high, (CX - count[0]) * CY, 0), 32)
        rows = max(count)
        if count[0] != count[1]:
            start = pl.multiple_of(jnp.where(high, (CX - count[0]) * CY, 0), 32)
        ref[base * 32 : (base + rows) * 32, :] = field[pl.ds(start, rows * 32), :]
    for which, ref in enumerate(y_pair):
        high = (odd_y == 0) if which == 0 else (odd_y == 1)
        start = jnp.where(high, CY - count[0], 0)
        for c in range(max(count)):
            for part in range(4):
                at = (base + c) * 32 + part * 8
                ref[at : at + 8, :] = every(field, part * 8 * CY + start + c, CY)


def pack_kernel(info, vel, den, pres, flow_x, flow_y, deal, gx_a, gx_b, gy_a, gy_b):
    for row in range(16):
        for cls in range(8):
            at = (row * 8 + cls) * 16
            deal[at : at + 8, :] = every(vel, row * 64 + cls, 8)
            deal[at + 8 : at + 16, :] = every(den, row * 64 + cls, 8)
    send_faces(info, pres, (gx_a, gx_b), (gy_a, gy_b), 0, (HALO, HALO))
    send_faces(info, flow_x, (gx_a, gx_b), (), HALO, (4, 4))
    send_faces(info, flow_y, (), (gy_a, gy_b), HALO, (4, 4))


def cut_kernel(info, corners, dealt, out, rho_lines, vel_lines):
    row_class, col_class = info[3], info[2]
    for t in range(16):
        for part in range(8):
            src = (t * 8 + part) * 16
            dst = t * LINE + 8 + part * 8
            vel_lines[dst : dst + 8, :] = dealt[src : src + 8, :]
            rho_lines[dst : dst + 8, :] = dealt[src + 8 : src + 16, :]

    def block(index, carry):
        shot = index // 4
        corner_x = corners[shot * 2] + (index % 4) * CX
        corner_y = corners[shot * 2 + 1]
        wide_row = lax.shift_right_arithmetic(corner_x - 4 - row_class + 15, 4)
        row = lax.shift_right_arithmetic(corner_x - row_class + 15, 4)
        for h in range(8):
            base = (index * 8 + h) * 24
            wide_col = lax.shift_right_arithmetic(corner_y + h * CY - 4 - col_class + 7, 3)
            col = lax.shift_right_arithmetic(corner_y + h * CY - col_class + 7, 3)
            for k in range(3):
                line = jnp.clip(wide_row + k, 0, 15)
                out[pl.ds(base + 5 * k, 5), :] = rho_lines[
                    pl.ds(line * LINE + 8 + wide_col, 5), :
                ]
            for k in range(2):
                out[pl.ds(base + 16 + 4 * k, 4), :] = vel_lines[
                    pl.ds((row + k) * LINE + 8 + col, 4), :
                ]
        return carry

    lax.fori_loop(0, 16, block, 0)


def unpack_model(info, corners, window, buoy, modu, rho, vel):
    shot, g, h = info[0], info[1], info[2]
    corner_x = corners[shot * 2] + g * CX
    corner_y = corners[shot * 2 + 1] + h * CY
    turn = lax.rem(8 - lax.rem(corner_y + 4, 8), 8)
    wide_turn = turn
    turn = lax.rem(8 - lax.rem(corner_y, 8), 8)
    sub = lax.broadcasted_iota(jnp.int32, (8, 128), 0)
    for w in range(WIDE):
        cls = lax.rem(corner_x + 12 + w, 16)
        row_in = (g * CX + w - 4 >= 0) & (g * CX + w - 4 < 4 * CX)
        for n in range(5):
            got = every(window, cls * 192 + 5 * (w // 16) + n, 24)
            got = pltpu.roll(got, wide_turn, 0)
            at = w * WIDE + n * 8
            rho[at : at + 8, :] = got
            col = sub + (h * CY + n * 8 - 4)
            inside = (col >= 0) & (col < 8 * CY) & row_in
            buoy[at : at + 8, :] = jnp.where(inside, time_step * (1.0 / got), 0.0)
    for w in range(CX):
        cls = lax.rem(corner_x + w, 16)
        for n in range(4):
            got = every(window, cls * 192 + 16 + 4 * (w // 16) + n, 24)
            at = w * CY + n * 8
            vel[at : at + 8, :] = pltpu.roll(got, turn, 0)
    for w in range(CX):
        for j in range(4):
            speed = every(vel, w * CY + j, 4)
            dens = every(rho, (w + 4) * WIDE + 4 + j, 4)
            put_every(modu, w * CY + j, 4, time_step * (dens * speed * speed))


def receive_faces(info, x_pair, y_pair, padded):
    odd_x, odd_y, end_x, end_y = info[8], info[9], info[10], info[11]
    for which, ref in enumerate(x_pair):
        high = (odd_x == 0) if which == 0 else (odd_x == 1)
        start = jnp.where(high, CX, -HALO)
        for i in range(HALO):
            value = ref[i * 32 : (i + 1) * 32, :]
            if which == 1:
                value = jnp.where(end_x == 1, 0.0, value)
            padded[pl.ds(pl.multiple_of((start + i + 8) * PAD + 8, 8), 32), :] = value
    for which, ref in enumerate(y_pair):
        high = (odd_y == 0) if which == 0 else (odd_y == 1)
        start = jnp.where(high, CY, -HALO)
        for c in range(HALO):
            for part in range(4):
                value = ref[c * 32 + part * 8 : c * 32 + part * 8 + 8, :]
                if which == 1:
                    value = jnp.where(end_y == 1, 0.0, value)
                put_every(padded, (part * 8 + 8) * PAD + start + c + 8, PAD, value)


def step_kernel(step, *refs):
    first, last = step == 0, step == STEPS - 1
    info, corners, amps, mat_f, mat_b, pres, gx_a, gx_b, gy_a, gy_b = refs[:10]
    rest = list(refs[10:])
    if first:
        window, in_x, in_y, in_z = rest[:4]
        rest = rest[4:]
        new_p, wide_x, wide_y, new_z, out_a, out_b, out_c, out_d, buoy, modu = rest[:10]
        rest = rest[10:]
        padded, rho, vel = rest
        unpack_model(info, corners, window, buoy, modu, rho, vel)
        wide_x[4 * CY : 36 * CY, :] = in_x[...]

        def spread_y(x, carry):
            for j in range(4):
                put_every(wide_y, x * WIDE + 4 + j, 4, every(in_y, x * CY + j, 4))
            return carry

        lax.fori_loop(0, CX, spread_y, 0)
        odd_x, odd_y, end_x, end_y = info[8], info[9], info[10], info[11]
        for which, ref in enumerate((gx_a, gx_b)):
            high = (odd_x == 0) if which == 0 else (odd_x == 1)
            value = ref[HALO * 32 : (HALO + 4) * 32, :]
            if which == 1:
                value = jnp.where(end_x == 1, 0.0, value)
            wide_x[pl.ds(pl.multiple_of(jnp.where(high, 36 * CY, 0), 32), 4 * CY), :] = value
        for which, ref in enumerate((gy_a, gy_b)):
            high = (odd_y == 0) if which == 0 else (odd_y == 1)
            start = jnp.where(high, 36, 0)
            for c in range(4):
                for part in range(4):
                    at = (HALO + c) * 32 + part * 8
                    value = ref[at : at + 8, :]
                    if which == 1:
                        value = jnp.where(end_y == 1, 0.0, value)
                    put_every(wide_y, part * 8 * WIDE + start + c, WIDE, value)
        old_x, old_y, old_z = wide_x, wide_y, in_z
    else:
        old_x, old_y, old_z, buoy, modu = rest[:5]
        rest = rest[5:]
        if last:
            new_p, out_x, out_y, new_z = rest[:4]
            padded, wide_x, wide_y = rest[4:]
        else:
            new_p, wide_x, wide_y, new_z, out_a, out_b, out_c, out_d = rest[:8]
            padded = rest[8]

    def spread_p(x, carry):
        padded[pl.ds(pl.multiple_of((x + 8) * PAD + 8, 8), 32), :] = pres[
            pl.ds(pl.multiple_of(x * CY, 32), 32), :
        ]
        return carry

    lax.fori_loop(0, CX, spread_p, 0)
    receive_faces(info, (gx_a, gx_b), (gy_a, gy_b), padded)

    def update_x(chunk, carry):
        x0 = chunk * 4 - 4
        for j in range(4):
            taps = [every(padded, (x0 + d + 8) * PAD + 8 + j, 4) for d in range(-3, 8)]
            for i in range(4):
                at = (x0 + i + 4) * CY + j
                value = every(old_x, at, 4) - every(buoy, (x0 + i + 4) * WIDE + 4 + j, 4) * forward(taps, i)
                put_every(wide_x, at, 4, value)
        return carry

    lax.fori_loop(0, 10, update_x, 0)

    def update_y(x, carry):
        taps = [every(padded, (x + 8) * PAD + 4 + d, 5) for d in range(-3, 9)]
        for j in range(5):
            at = x * WIDE + j
            value = every(old_y, at, 5) - every(buoy, (x + 4) * WIDE + j, 5) * forward(taps, j)
            put_every(wide_y, at, 5, value)
        return carry

    lax.fori_loop(0, CX, update_y, 0)

    def update_p(chunk, carry):
        x0 = chunk * 4
        old = [every(pres, (x0 + i) * CY + j, 4) for i in range(4) for j in range(4)]
        grad = depth_difference(jnp.concatenate(old, axis=0), mat_f)
        flow = []
        for i in range(4):
            for j in range(4):
                n = i * 4 + j
                at = (x0 + i) * CY + j
                value = every(old_z, at, 4) - every(
                    buoy, (x0 + i + 4) * WIDE + 4 + j, 4
                ) * grad[n * 8 : n * 8 + 8, :]
                put_every(new_z, at, 4, value)
                flow.append(value)
        part_z = depth_difference(jnp.concatenate(flow, axis=0), mat_b)
        part_x = {}
        for j in range(4):
            taps = [every(wide_x, (x0 + d + 4) * CY + j, 4) for d in range(-4, 7)]
            for i in range(4):
                part_x[i, j] = backward(taps, i)
        for i in range(4):
            taps = [every(wide_y, (x0 + i) * WIDE + 4 + d, 4) for d in range(-4, 7)]
            for j in range(4):
                n = i * 4 + j
                total = part_x[i, j] + backward(taps, j) + part_z[n * 8 : n * 8 + 8, :]
                at = (x0 + i) * CY + j
                put_every(new_p, at, 4, old[n] - every(modu, at, 4) * total)
        return carry

    lax.fori_loop(0, 8, update_p, 0)

    shot = info[0]
    src_x = info[4] - info[1] * CX
    src_y = info[5] - info[2] * CY

    @pl.when((src_x >= 0) & (src_x < CX) & (src_y >= 0) & (src_y < CY))
    def _():
        at = src_x * CY + src_y
        lane = lax.broadcasted_iota(jnp.int32, (1, 128), 1)
        kick = time_step * amps[shot * STEPS + step]
        new_p[pl.ds(at, 1), :] = new_p[pl.ds(at, 1), :] + jnp.where(lane == info[6], kick, 0.0)

    if last:
        out_x[...] = wide_x[4 * CY : 36 * CY, :]

        def trim_y(x, carry):
            for j in range(4):
                put_every(out_y, x * CY + j, 4, every(wide_y, x * WIDE + 4 + j, 4))
            return carry

        lax.fori_loop(0, CX, trim_y, 0)
    else:
        send_faces(info, new_p, (out_a, out_b), (out_c, out_d), 0, (HALO, HALO))


def shape(rows, dtype=f32):
    return jax.ShapeDtypeStruct((rows, 128), dtype)


def call(kernel, outs, args, scratch, smem, name):
    specs = [pl.BlockSpec(memory_space=pltpu.SMEM)] * smem + [
        pl.BlockSpec(memory_space=pltpu.VMEM)
    ] * (len(args) - smem)
    return pl.pallas_call(
        kernel,
        out_shape=outs,
        in_specs=specs,
        out_specs=[pl.BlockSpec(memory_space=pltpu.VMEM)] * len(outs),
        scratch_shapes=scratch,
        compiler_params=pltpu.CompilerParams(vmem_limit_bytes=40 * 1024 * 1024),
        name=name,
    )(*args)


x_swaps = ([(0, 1), (1, 0), (2, 3), (3, 2)], [(1, 2), (2, 1), (0, 3), (3, 0)])
y_swaps = (
    [(i, i ^ 1) for i in range(8)],
    [(1, 2), (2, 1), (3, 4), (4, 3), (5, 6), (6, 5), (7, 0), (0, 7)],
)


def exchange(faces):
    return [
        lax.ppermute(faces[0], "gx", x_swaps[0]),
        lax.ppermute(faces[1], "gx", x_swaps[1]),
        lax.ppermute(faces[2], "gy", y_swaps[0]),
        lax.ppermute(faces[3], "gy", y_swaps[1]),
    ]


def shards(velocity, density, offsets, pressure, vel_x, vel_y, vel_z, source_cells, wavelet):
    s, g, h = (lax.axis_index(axis) for axis in DEVICES)
    cell = lax.dynamic_index_in_dim(source_cells, s, 0, keepdims=False)
    zero = jnp.int32(0)
    info = jnp.stack(
        [
            s, g, h, s * 4 + g,
            cell[0], cell[1], cell[2], zero,
            g % 2, h % 2,
            ((g == 0) | (g == 3)).astype(jnp.int32),
            ((h == 0) | (h == 7)).astype(jnp.int32),
        ]
    ).astype(jnp.int32)
    corners = offsets.reshape(-1)
    amps = wavelet.reshape(-1)
    mat_f, mat_b = (jnp.asarray(m) for m in depth_matrices())

    vel = velocity.reshape(16 * 64, 128)
    den = density.reshape(16 * 64, 128)
    pres = pressure.reshape(CX * CY, 128)
    flow_x = vel_x.reshape(CX * CY, 128)
    flow_y = vel_y.reshape(CX * CY, 128)
    flow_z = vel_z.reshape(CX * CY, 128)

    face = shape((HALO + 4) * 32)
    deal, *faces = call(
        pack_kernel, [shape(128 * 16)] + [face] * 4, [info, vel, den, pres, flow_x, flow_y], [], 1, "pack"
    )
    faces = exchange(faces)
    dealt = lax.all_to_all(deal.reshape(128, 16, 128), DEVICES, 0, 0, tiled=True)
    (cut,) = call(
        cut_kernel,
        [shape(128 * 24)],
        [info, corners, dealt.reshape(128 * 16, 128)],
        [pltpu.VMEM((16 * LINE, 128), f32), pltpu.VMEM((16 * LINE, 128), f32)],
        2,
        "cut",
    )
    window = lax.all_to_all(cut.reshape(128, 24, 128), DEVICES, 0, 0, tiled=True)
    window = window.reshape(128 * 24, 128)

    block = shape(CX * CY)
    wide = shape(WIDE * CY)
    face = shape(HALO * 32)
    padded = pltpu.VMEM((PAD * PAD, 128), f32)
    for step in range(STEPS):
        head = [info, corners, amps, mat_f, mat_b, pres] + list(faces)
        kernel = functools.partial(step_kernel, step)
        name = f"step{step}"
        if step == 0:
            pres, flow_x, flow_y, flow_z, *faces, buoy, modu = call(
                kernel,
                [block, wide, wide, block] + [face] * 4 + [shape(WIDE * WIDE), block],
                head + [window, flow_x, flow_y, flow_z],
                [padded, pltpu.VMEM((WIDE * WIDE, 128), f32), pltpu.VMEM((CX * CY, 128), f32)],
                3,
                name,
            )
        elif step < STEPS - 1:
            pres, flow_x, flow_y, flow_z, *faces = call(
                kernel,
                [block, wide, wide, block] + [face] * 4,
                head + [flow_x, flow_y, flow_z, buoy, modu],
                [padded],
                3,
                name,
            )
        else:
            pres, flow_x, flow_y, flow_z = call(
                kernel,
                [block] * 4,
                head + [flow_x, flow_y, flow_z, buoy, modu],
                [padded] + [pltpu.VMEM((WIDE * CY, 128), f32)] * 2,
                3,
                name,
            )
        if step < STEPS - 1:
            faces = exchange(faces)
    return tuple(a.reshape(1, CX, CY, 128) for a in (pres, flow_x, flow_y, flow_z))


def solution(mesh):
    return jax.shard_map(
        shards,
        mesh=mesh,
        in_specs=(
            P(("shot", "gx"), "gy", None),
            P(("shot", "gx"), "gy", None),
            P(),
            P("shot", "gx", "gy", None),
            P("shot", "gx", "gy", None),
            P("shot", "gx", "gy", None),
            P("shot", "gx", "gy", None),
            P(),
            P(),
        ),
        out_specs=(
            P("shot", "gx", "gy", None),
            P("shot", "gx", "gy", None),
            P("shot", "gx", "gy", None),
            P("shot", "gx", "gy", None),
        ),
        check_vma=False,
    )
```

```python
import functools

import jax
import jax.numpy as jnp
import numpy as np
from jax import lax
from jax.experimental import pallas as pl
from jax.experimental.pallas import tpu as pltpu
from jax.sharding import PartitionSpec as P

CX = 32
CY = 32
STEPS = 4
HALO = 7
WIDE = 40
PAD = 48
LINE = 80
STRIP = 24
DEVICES = ("shot", "gx", "gy")

coefs = (1225.0 / 1024.0, -245.0 / 3072.0, 49.0 / 5120.0, -5.0 / 7168.0)
time_step = 0.09

f32 = jnp.float32
bf16 = jnp.bfloat16


def depth_matrices():
    out = []
    for lead in (0, 1):
        full = np.zeros((128, 128), np.float32)
        for reach in range(1, 5):
            for k in range(128):
                up, down = k + reach - lead, k - reach + 1 - lead
                if up < 128:
                    full[up, k] += np.float32(coefs[reach - 1])
                if down >= 0:
                    full[down, k] -= np.float32(coefs[reach - 1])
        high = full.astype(jnp.bfloat16)
        low = (full - high.astype(np.float32)).astype(jnp.bfloat16)
        out.append(np.concatenate([high, high, low], axis=0))
    return out


def depth_difference(values, mat_ref):
    high = values.astype(bf16)
    low = (values - high.astype(f32)).astype(bf16)
    main = jnp.dot(
        jnp.concatenate([high, low], axis=1), mat_ref[0:256, :], preferred_element_type=f32
    )
    return main + jnp.dot(high, mat_ref[256:384, :], preferred_element_type=f32)


def forward(taps, at):
    total = None
    for reach in range(1, 5):
        term = coefs[reach - 1] * (taps[at + 3 + reach] - taps[at + 4 - reach])
        total = term if total is None else total + term
    return total


def backward(taps, at):
    total = None
    for reach in range(1, 5):
        term = coefs[reach - 1] * (taps[at + 3 + reach] - taps[at + 4 - reach])
        total = term if total is None else total + term
    return total


def every(ref, start, step):
    return ref[pl.ds(start, 8, stride=step), :]


def put_every(ref, start, step, value):
    ref[pl.ds(start, 8, stride=step), :] = value


def place():
    return tuple(lax.axis_index(axis) for axis in DEVICES)


def odd(index):
    return lax.rem(index, 2) == 1


def send_faces(field, x_pair, y_pair, base, rows):
    s, g, h = place()
    for which, ref in enumerate(x_pair):
        low = odd(g) if which == 0 else jnp.logical_not(odd(g))
        start = pl.multiple_of(jnp.where(low, 0, (CX - rows) * CY), 32)
        ref[base * 32 : (base + rows) * 32, :] = field[pl.ds(start, rows * 32), :]
    for which, ref in enumerate(y_pair):
        low = odd(h) if which == 0 else jnp.logical_not(odd(h))
        start = jnp.where(low, 0, CY - rows)
        for c in range(rows):
            for part in range(4):
                at = (base + c) * 32 + part * 8
                ref[at : at + 8, :] = every(field, part * 8 * CY + start + c, CY)


def received(pair, which, end, at):
    value = pair[which][at : at + 8, :]
    return jnp.where(end, 0.0, value) if which == 1 else value


def pack_kernel(vel, den, deal, vel_in, den_in, out, in_sem, out_sem):
    pulls = []
    for part in range(4):
        rows = pl.ds(part * 256, 256)
        pulls.append(
            [
                pltpu.make_async_copy(src.at[rows], dst.at[rows], in_sem.at[part * 2 + i])
                for i, (src, dst) in enumerate(((vel, vel_in), (den, den_in)))
            ]
        )
        for pull in pulls[-1]:
            pull.start()
    pushes = []
    for part in range(4):
        for pull in pulls[part]:
            pull.wait()
        for row in range(part * 4, part * 4 + 4):
            for cls in range(8):
                at = (row * 8 + cls) * 16
                out[at : at + 8, :] = every(vel_in, row * 64 + cls, 8)
                out[at + 8 : at + 16, :] = every(den_in, row * 64 + cls, 8)
        rows = pl.ds(part * 512, 512)
        pushes.append(pltpu.make_async_copy(out.at[rows], deal.at[rows], out_sem.at[part]))
        pushes[-1].start()
    for push in pushes:
        push.wait()


def face_kernel(pres, flow_x, flow_y, gx_a, gx_b, gy_a, gy_b, pres_in, x_in, y_in, sem):
    pulls = [
        pltpu.make_async_copy(src, dst, sem.at[i])
        for i, (src, dst) in enumerate(((pres, pres_in), (flow_x, x_in), (flow_y, y_in)))
    ]
    for pull in pulls:
        pull.start()
    for pull in pulls:
        pull.wait()
    send_faces(pres_in, (gx_a, gx_b), (gy_a, gy_b), 0, HALO)
    send_faces(x_in, (gx_a, gx_b), (), HALO, 4)
    send_faces(y_in, (), (gy_a, gy_b), HALO, 4)


def cut_kernel(corners, dealt, out, rho_lines, vel_lines, cuts, sem):
    s, g, col_class = place()
    row_class = s * 4 + g
    for t in range(16):
        for part in range(8):
            src = (t * 8 + part) * 16
            dst = t * LINE + 8 + part * 8
            vel_lines[dst : dst + 8, :] = dealt[src : src + 8, :]
            rho_lines[dst : dst + 8, :] = dealt[src + 8 : src + 16, :]

    pushes = []
    for shot in range(4):
        corner_y = corners[shot, 1]

        def block(part, carry):
            corner_x = corners[shot, 0] + part * CX
            wide_row = lax.shift_right_arithmetic(corner_x - 4 - row_class + 15, 4)
            row = lax.shift_right_arithmetic(corner_x - row_class + 15, 4)
            for h in range(8):
                base = (shot * 32 + part * 8 + h) * 24
                wide_col = lax.shift_right_arithmetic(corner_y + h * CY - 4 - col_class + 7, 3)
                col = lax.shift_right_arithmetic(corner_y + h * CY - col_class + 7, 3)
                for k in range(3):
                    line = jnp.clip(wide_row + k, 0, 15)
                    cuts[pl.ds(base + 5 * k, 5), :] = rho_lines[
                        pl.ds(line * LINE + 8 + wide_col, 5), :
                    ]
                for k in range(2):
                    cuts[pl.ds(base + 16 + 4 * k, 4), :] = vel_lines[
                        pl.ds((row + k) * LINE + 8 + col, 4), :
                    ]
            return carry

        lax.fori_loop(0, 4, block, 0)
        rows = pl.ds(shot * 768, 768)
        pushes.append(pltpu.make_async_copy(cuts.at[rows], out.at[rows], sem.at[shot]))
        pushes[-1].start()
    for push in pushes:
        push.wait()


def unpack_model(corners, window, buoy, modu, rho, vel):
    s, g, h = place()
    corner_x = corners[s, 0] + g * CX
    corner_y = corners[s, 1] + h * CY
    wide_turn = lax.rem(8 - lax.rem(corner_y + 4, 8), 8)
    turn = lax.rem(8 - lax.rem(corner_y, 8), 8)
    sub = lax.broadcasted_iota(jnp.int32, (8, 128), 0)
    for w in range(WIDE):
        cls = lax.rem(corner_x + 12 + w, 16)
        row_in = (g * CX + w - 4 >= 0) & (g * CX + w - 4 < 4 * CX)
        for n in range(5):
            got = every(window, cls * 192 + 5 * (w // 16) + n, 24)
            got = pltpu.roll(got, wide_turn, 0)
            at = w * WIDE + n * 8
            rho[at : at + 8, :] = got
            col = sub + (h * CY + n * 8 - 4)
            inside = (col >= 0) & (col < 8 * CY) & row_in
            buoy[at : at + 8, :] = jnp.where(inside, time_step * (1.0 / got), 0.0)
    for w in range(CX):
        cls = lax.rem(corner_x + w, 16)
        for n in range(4):
            got = every(window, cls * 192 + 16 + 4 * (w // 16) + n, 24)
            speed = pltpu.roll(got, turn, 0)
            at = w * CY + n * 8
            dens = rho[(w + 4) * WIDE + 4 + n * 8 : (w + 4) * WIDE + 12 + n * 8, :]
            modu[at : at + 8, :] = time_step * (dens * speed * speed)


def buoy_at(buoy, x, y, rows=8):
    return buoy[pl.ds((x + 4) * WIDE + 4 + y, rows), :]


def grad0_kernel(
    mat_f, pres, gx_a, gx_b, gy_a, gy_b, in_x, in_y, grad_x, grad_y, grad_z, wide_x, wide_y, padded
):
    s, g, h = place()
    end_x = (g == 0) | (g == 3)
    end_y = (h == 0) | (h == 7)
    for x in range(CX):
        at = (x + 8) * PAD + 8
        padded[at : at + 32, :] = pres[x * CY : (x + 1) * CY, :]
        wide_y[x * WIDE + 4 : x * WIDE + 36, :] = in_y[x * CY : (x + 1) * CY, :]
    wide_x[4 * CY : 36 * CY, :] = in_x[...]
    x_pair, y_pair = (gx_a, gx_b), (gy_a, gy_b)
    for which in range(2):
        low = odd(g) if which == 0 else jnp.logical_not(odd(g))
        start = jnp.where(low, -HALO, CX)
        for i in range(HALO):
            for part in range(4):
                at = pl.multiple_of((start + i + 8) * PAD + 8 + part * 8, 8)
                padded[pl.ds(at, 8), :] = received(x_pair, which, end_x, i * 32 + part * 8)
        start = jnp.where(low, 0, 36)
        for i in range(4):
            for part in range(4):
                at = pl.multiple_of((start + i) * CY + part * 8, 8)
                wide_x[pl.ds(at, 8), :] = received(x_pair, which, end_x, (HALO + i) * 32 + part * 8)
        low = odd(h) if which == 0 else jnp.logical_not(odd(h))
        start = jnp.where(low, -HALO, CY)
        for c in range(HALO):
            for part in range(4):
                at = (part * 8 + 8) * PAD + start + c + 8
                put_every(padded, at, PAD, received(y_pair, which, end_y, c * 32 + part * 8))
        start = jnp.where(low, 0, 36)
        for c in range(4):
            for part in range(4):
                value = received(y_pair, which, end_y, (HALO + c) * 32 + part * 8)
                put_every(wide_y, part * 8 * WIDE + start + c, WIDE, value)

    def along_x(chunk, carry):
        x0 = chunk * 4 - 4
        for n in range(4):
            taps = [
                padded[pl.ds(pl.multiple_of((x0 + d + 8) * PAD + 8 + n * 8, 8), 8), :]
                for d in range(-3, 8)
            ]
            for i in range(4):
                at = pl.multiple_of((x0 + i + 4) * CY + n * 8, 8)
                grad_x[pl.ds(at, 8), :] = forward(taps, i)
        return carry

    lax.fori_loop(0, 10, along_x, 0)

    def along_y(x, carry):
        taps = [every(padded, (x + 8) * PAD + 4 + d, 5) for d in range(-3, 9)]
        for j in range(5):
            put_every(grad_y, x * WIDE + j, 5, forward(taps, j))
        return carry

    lax.fori_loop(0, CX, along_y, 0)
    for chunk in range(8):
        rows = slice(chunk * 128, (chunk + 1) * 128)
        grad_z[rows, :] = depth_difference(pres[rows, :], mat_f)


def kick_source(step, cells, amps, field):
    s, g, h = place()
    x = cells[s, 0] - g * CX
    y = cells[s, 1] - h * CY

    @pl.when((x >= 0) & (x < CX) & (y >= 0) & (y < CY))
    def _():
        at = x * CY + y
        lane = lax.broadcasted_iota(jnp.int32, (1, 128), 1)
        kick = time_step * amps[s, step]
        field[pl.ds(at, 1), :] = field[pl.ds(at, 1), :] + jnp.where(lane == cells[s, 2], kick, 0.0)


def step0_kernel(
    corners, cells, amps, mat_b, window, pres, in_x, in_y, in_z, grad_x, grad_y, grad_z,
    new_p, wide_x, wide_y, new_z, buoy, modu, gx_a, gx_b, gy_a, gy_b, rho, vel, spread,
):
    unpack_model(corners, window, buoy, modu, rho, vel)

    def flow(x, carry):
        for n in range(4):
            at = pl.multiple_of(x * CY + n * 8, 8)
            value = in_z[pl.ds(at, 8), :] - buoy_at(buoy, x, n * 8) * grad_z[pl.ds(at, 8), :]
            new_z[pl.ds(at, 8), :] = value
        for n in range(5):
            at = pl.multiple_of(x * WIDE + n * 8, 8)
            wide_y[pl.ds(at, 8), :] = (
                in_y[pl.ds(at, 8), :] - buoy_at(buoy, x, n * 8 - 4) * grad_y[pl.ds(at, 8), :]
            )
        return carry

    lax.fori_loop(0, CX, flow, 0, unroll=4)

    def flow_x(x, carry):
        for n in range(4):
            at = pl.multiple_of(x * CY + n * 8, 8)
            wide_x[pl.ds(at, 8), :] = (
                in_x[pl.ds(at, 8), :] - buoy_at(buoy, x - 4, n * 8) * grad_x[pl.ds(at, 8), :]
            )
        return carry

    lax.fori_loop(0, WIDE, flow_x, 0, unroll=4)
    for chunk in range(8):
        rows = slice(chunk * 128, (chunk + 1) * 128)
        spread[rows, :] = depth_difference(new_z[rows, :], mat_b)

    def update(chunk, carry):
        x0 = chunk * 4
        part_x = {}
        for j in range(4):
            taps = [every(wide_x, (x0 + d + 4) * CY + j, 4) for d in range(-4, 7)]
            for i in range(4):
                part_x[i, j] = backward(taps, i)
        for i in range(4):
            taps = [every(wide_y, (x0 + i) * WIDE + 4 + d, 4) for d in range(-4, 7)]
            for j in range(4):
                at = (x0 + i) * CY + j
                total = part_x[i, j] + backward(taps, j) + every(spread, at, 4)
                put_every(new_p, at, 4, every(pres, at, 4) - every(modu, at, 4) * total)
        return carry

    lax.fori_loop(0, 8, update, 0)
    kick_source(0, cells, amps, new_p)
    send_faces(new_p, (gx_a, gx_b), (gy_a, gy_b), 0, HALO)


def inner_kernel(mat_f, mat_b, pres, in_x, in_y, in_z, buoy, wide_x, wide_y, new_z, spread):
    for chunk in range(8):
        rows = slice(chunk * 128, (chunk + 1) * 128)
        grad = depth_difference(pres[rows, :], mat_f)
        light = jnp.concatenate(
            [buoy_at(buoy, x, 0, 32) for x in range(chunk * 4, chunk * 4 + 4)], axis=0
        )
        new_z[rows, :] = in_z[rows, :] - light * grad

    def along_x(chunk, carry):
        x0 = chunk * 4 + 4
        for n in range(4):
            taps = [
                pres[pl.ds(pl.multiple_of((x0 + d) * CY + n * 8, 8), 8), :] for d in range(-3, 8)
            ]
            for i in range(4):
                at = pl.multiple_of((x0 + i + 4) * CY + n * 8, 8)
                wide_x[pl.ds(at, 8), :] = in_x[pl.ds(at, 8), :] - buoy_at(
                    buoy, x0 + i, n * 8
                ) * forward(taps, i)
        return carry

    lax.fori_loop(0, 6, along_x, 0)

    def along_y(x, carry):
        taps = [every(pres, x * CY + 4 + d, 3) for d in range(-3, 7)]
        for j in range(3):
            at = x * WIDE + 8 + j
            light = every(buoy, (x + 4) * WIDE + 8 + j, 3)
            put_every(wide_y, at, 3, every(in_y, at, 3) - light * forward(taps, j))
        return carry

    lax.fori_loop(0, CX, along_y, 0, unroll=4)
    wide_x[0 : 8 * CY, :] = in_x[0 : 8 * CY, :]
    wide_x[32 * CY : 40 * CY, :] = in_x[32 * CY : 40 * CY, :]
    for x in range(CX):
        wide_y[x * WIDE : x * WIDE + 8, :] = in_y[x * WIDE : x * WIDE + 8, :]
        wide_y[x * WIDE + 32 : x * WIDE + 40, :] = in_y[x * WIDE + 32 : x * WIDE + 40, :]
    for chunk in range(8):
        rows = slice(chunk * 128, (chunk + 1) * 128)
        spread[rows, :] = depth_difference(new_z[rows, :], mat_b)

    def across(chunk, carry):
        x0 = chunk * 4 + 8
        for n in range(4):
            taps = [
                wide_x[pl.ds(pl.multiple_of((x0 + d + 4) * CY + n * 8, 8), 8), :]
                for d in range(-4, 7)
            ]
            for i in range(4):
                at = pl.multiple_of((x0 + i) * CY + n * 8, 8)
                spread[pl.ds(at, 8), :] = spread[pl.ds(at, 8), :] + backward(taps, i)
        return carry

    lax.fori_loop(0, 4, across, 0)

    def along(x, carry):
        taps = [every(wide_y, x * WIDE + 12 + d, 2) for d in range(-4, 5)]
        for j in range(2):
            at = x * CY + 8 + j
            put_every(spread, at, 2, every(spread, at, 2) + backward(taps, j))
        return carry

    lax.fori_loop(0, CX, along, 0, unroll=4)


def edge_kernel(step, *refs):
    cells, amps, pres, gx_a, gx_b, gy_a, gy_b, in_x, in_y, buoy, modu, spread = refs[:12]
    last = step == STEPS - 1
    if last:
        new_p, out_x, out_y, low_x, high_x, low_y, high_y, wide_x, wide_y = refs[12:]
    else:
        new_p, wide_x, wide_y, to_a, to_b, to_c, to_d, low_x, high_x, low_y, high_y = refs[12:]
    wide_x[8 * CY : 32 * CY, :] = in_x[8 * CY : 32 * CY, :]
    for x in range(CX):
        wide_y[x * WIDE + 8 : x * WIDE + 32, :] = in_y[x * WIDE + 8 : x * WIDE + 32, :]
    s, g, h = place()
    end_x = (g == 0) | (g == 3)
    end_y = (h == 0) | (h == 7)
    x_pair, y_pair = (gx_a, gx_b), (gy_a, gy_b)
    low_x[8 * CY : 16 * CY, :] = pres[0 : 8 * CY, :]
    high_x[0 : 8 * CY, :] = pres[24 * CY : 32 * CY, :]
    for x in range(CX):
        low_y[x * STRIP + 8 : x * STRIP + 16, :] = pres[x * CY : x * CY + 8, :]
        high_y[x * STRIP : x * STRIP + 8, :] = pres[x * CY + 24 : x * CY + 32, :]

    def place_x(which, ref, start):
        for i in range(HALO):
            for part in range(4):
                at = (start + i) * CY + part * 8
                ref[at : at + 8, :] = received(x_pair, which, end_x, i * 32 + part * 8)

    def place_y(which, ref, start):
        for c in range(HALO):
            for part in range(4):
                value = received(y_pair, which, end_y, c * 32 + part * 8)
                put_every(ref, part * 8 * STRIP + start + c, STRIP, value)

    for where, put, low, high in ((g, place_x, low_x, high_x), (h, place_y, low_y, high_y)):

        @pl.when(odd(where))
        def _():
            put(0, low, 1)
            put(1, high, 8)

        @pl.when(jnp.logical_not(odd(where)))
        def _():
            put(1, low, 1)
            put(0, high, 8)

    for strip, first in ((low_x, -4), (high_x, 28)):
        for half in range(2):
            for n in range(4):
                taps = [
                    strip[(half * 4 + 4 + d) * CY + n * 8 : (half * 4 + 4 + d) * CY + n * 8 + 8, :]
                    for d in range(-3, 8)
                ]
                for i in range(4):
                    x = first + half * 4 + i
                    at = (x + 4) * CY + n * 8
                    wide_x[at : at + 8, :] = in_x[at : at + 8, :] - buoy_at(
                        buoy, x, n * 8
                    ) * forward(taps, i)

    def rows(x0, with_x):
        part_x = {}
        if with_x:
            for n in range(4):
                taps = [
                    wide_x[pl.ds(pl.multiple_of((x0 + d + 4) * CY + n * 8, 8), 8), :]
                    for d in range(-4, 7)
                ]
                for i in range(4):
                    part_x[i, n] = backward(taps, i)
        for i in range(4):
            x = x0 + i
            for strip, col in ((low_y, 0), (high_y, 32)):
                taps = [strip[pl.ds(x * STRIP + 4 + d, 8), :] for d in range(-3, 5)]
                at = pl.multiple_of(x * WIDE + col, 8)
                wide_y[pl.ds(at, 8), :] = in_y[pl.ds(at, 8), :] - buoy_at(
                    buoy, x, col - 4
                ) * forward(taps, 0)
            for n in range(4):
                at = pl.multiple_of(x * CY + n * 8, 8)
                total = spread[pl.ds(at, 8), :]
                if n in (0, 3):
                    taps = [wide_y[pl.ds(x * WIDE + 4 + n * 8 + d, 8), :] for d in range(-4, 4)]
                    total = total + backward(taps, 0)
                if with_x:
                    total = total + part_x[i, n]
                new_p[pl.ds(at, 8), :] = pres[pl.ds(at, 8), :] - modu[pl.ds(at, 8), :] * total

    for first, count, with_x in ((0, 2, True), (8, 4, False), (24, 2, True)):

        def some(chunk, carry):
            rows(first + chunk * 4, with_x)
            return carry

        lax.fori_loop(0, count, some, 0)

    kick_source(step, cells, amps, new_p)
    if last:
        out_x[...] = wide_x[4 * CY : 36 * CY, :]
        for x in range(CX):
            out_y[x * CY : (x + 1) * CY, :] = wide_y[x * WIDE + 4 : x * WIDE + 36, :]
    else:
        send_faces(new_p, (to_a, to_b), (to_c, to_d), 0, HALO)


def shape(rows, dtype=f32):
    return jax.ShapeDtypeStruct((rows, 128), dtype)


def vmem(rows):
    return pltpu.VMEM((rows, 128), f32)


def call(kernel, outs, args, scratch, name, smem=0, inputs=pltpu.VMEM, outputs=pltpu.VMEM, cost=None):
    specs = [pl.BlockSpec(memory_space=pltpu.SMEM)] * smem + [
        pl.BlockSpec(memory_space=inputs)
    ] * (len(args) - smem)
    return pl.pallas_call(
        kernel,
        out_shape=outs,
        in_specs=specs,
        out_specs=[pl.BlockSpec(memory_space=outputs)] * len(outs),
        scratch_shapes=scratch,
        cost_estimate=cost,
        compiler_params=pltpu.CompilerParams(vmem_limit_bytes=24 * 1024 * 1024),
        name=name,
    )(*args)


x_swaps = ([(0, 1), (1, 0), (2, 3), (3, 2)], [(1, 2), (2, 1), (0, 3), (3, 0)])
y_swaps = (
    [(i, i ^ 1) for i in range(8)],
    [(1, 2), (2, 1), (3, 4), (4, 3), (5, 6), (6, 5), (7, 0), (0, 7)],
)


def exchange(faces):
    return [
        lax.ppermute(faces[0], "gx", x_swaps[0]),
        lax.ppermute(faces[1], "gx", x_swaps[1]),
        lax.ppermute(faces[2], "gy", y_swaps[0]),
        lax.ppermute(faces[3], "gy", y_swaps[1]),
    ]


def shards(velocity, density, offsets, pressure, vel_x, vel_y, vel_z, source_cells, wavelet):
    mat_f, mat_b = (jnp.asarray(m) for m in depth_matrices())
    vel = velocity.reshape(16 * 64, 128)
    den = density.reshape(16 * 64, 128)
    pres = pressure.reshape(CX * CY, 128)
    flow_x = vel_x.reshape(CX * CY, 128)
    flow_y = vel_y.reshape(CX * CY, 128)
    flow_z = vel_z.reshape(CX * CY, 128)
    block = shape(CX * CY)
    wide = shape(WIDE * CY)
    face = shape(HALO * 32)
    cost = pl.CostEstimate(flops=20_000_000, bytes_accessed=8_000_000, transcendentals=0)

    (deal,) = call(
        pack_kernel,
        [shape(128 * 16)],
        [vel, den],
        [vmem(1024), vmem(1024), vmem(2048), pltpu.SemaphoreType.DMA((8,)), pltpu.SemaphoreType.DMA((4,))],
        "pack",
        inputs=pl.ANY,
        outputs=pl.ANY,
    )
    dealt = lax.all_to_all(deal.reshape(128, 16, 128), DEVICES, 0, 0, tiled=True)
    faces = call(
        face_kernel,
        [shape((HALO + 4) * 32)] * 4,
        [pres, flow_x, flow_y],
        [vmem(1024)] * 3 + [pltpu.SemaphoreType.DMA((3,))],
        "first_faces",
        inputs=pl.ANY,
        cost=cost,
    )
    faces = exchange(faces)
    (cut,) = call(
        cut_kernel,
        [shape(128 * 24)],
        [offsets, dealt.reshape(128 * 16, 128)],
        [vmem(16 * LINE), vmem(16 * LINE), vmem(128 * 24), pltpu.SemaphoreType.DMA((4,))],
        "cut",
        smem=1,
        outputs=pl.ANY,
    )
    window = lax.all_to_all(cut.reshape(128, 24, 128), DEVICES, 0, 0, tiled=True)
    window = window.reshape(128 * 24, 128)
    grad_x, grad_y, grad_z, flow_x, flow_y = call(
        grad0_kernel,
        [wide, wide, block, wide, wide],
        [mat_f, pres] + list(faces) + [flow_x, flow_y],
        [vmem(PAD * PAD)],
        "step0_gradients",
        cost=cost,
    )
    pres, flow_x, flow_y, flow_z, buoy, modu, *faces = call(
        step0_kernel,
        [block, wide, wide, block, shape(WIDE * WIDE), block] + [face] * 4,
        [offsets, source_cells, wavelet, mat_b, window, pres, flow_x, flow_y, flow_z]
        + [grad_x, grad_y, grad_z],
        [vmem(WIDE * WIDE), vmem(CX * CY), vmem(CX * CY)],
        "step0",
        smem=3,
    )
    for step in range(1, STEPS):
        last = step == STEPS - 1
        faces = exchange(faces)
        flow_x, flow_y, flow_z, spread = call(
            inner_kernel,
            [wide, wide, block, block],
            [mat_f, mat_b, pres, flow_x, flow_y, flow_z, buoy],
            [],
            f"inner{step}",
            cost=cost,
        )
        pres, flow_x, flow_y, *faces = call(
            functools.partial(edge_kernel, step),
            [block, block, block] if last else [block, wide, wide] + [face] * 4,
            [source_cells, wavelet, pres, *faces, flow_x, flow_y, buoy, modu, spread],
            [vmem(16 * CY), vmem(16 * CY), vmem(CX * STRIP), vmem(CX * STRIP)]
            + ([vmem(WIDE * CY)] * 2 if last else []),
            f"edge{step}",
            smem=2,
        )
    return tuple(a.reshape(1, CX, CY, 128) for a in (pres, flow_x, flow_y, flow_z))


def solution(mesh):
    return jax.shard_map(
        shards,
        mesh=mesh,
        in_specs=(
            P(("shot", "gx"), "gy", None),
            P(("shot", "gx"), "gy", None),
            P(),
            P("shot", "gx", "gy", None),
            P("shot", "gx", "gy", None),
            P("shot", "gx", "gy", None),
            P("shot", "gx", "gy", None),
            P(),
            P(),
        ),
        out_specs=(
            P("shot", "gx", "gy", None),
            P("shot", "gx", "gy", None),
            P("shot", "gx", "gy", None),
            P("shot", "gx", "gy", None),
        ),
        check_vma=False,
    )
```

```python
import functools

import jax
import jax.numpy as jnp
import numpy as np
from jax import lax
from jax.experimental import pallas as pl
from jax.experimental.pallas import tpu as pltpu
from jax.sharding import PartitionSpec as P

CX = 32
CY = 32
STEPS = 4
HALO = 7
WIDE = 40
PAD = 48
LINE = 80
STRIP = 24
DEVICES = ("shot", "gx", "gy")

coefs = (1225.0 / 1024.0, -245.0 / 3072.0, 49.0 / 5120.0, -5.0 / 7168.0)
time_step = 0.09

f32 = jnp.float32
bf16 = jnp.bfloat16


def depth_matrices():
    out = []
    for lead in (0, 1):
        full = np.zeros((128, 128), np.float32)
        for reach in range(1, 5):
            for k in range(128):
                up, down = k + reach - lead, k - reach + 1 - lead
                if up < 128:
                    full[up, k] += np.float32(coefs[reach - 1])
                if down >= 0:
                    full[down, k] -= np.float32(coefs[reach - 1])
        high = full.astype(jnp.bfloat16)
        low = (full - high.astype(np.float32)).astype(jnp.bfloat16)
        out.append(np.concatenate([high, high, low], axis=0))
    return out


def depth_difference(values, mat_ref):
    high = values.astype(bf16)
    low = (values - high.astype(f32)).astype(bf16)
    main = jnp.dot(
        jnp.concatenate([high, low], axis=1), mat_ref[0:256, :], preferred_element_type=f32
    )
    return main + jnp.dot(high, mat_ref[256:384, :], preferred_element_type=f32)


def forward(taps, at):
    total = None
    for reach in range(1, 5):
        term = coefs[reach - 1] * (taps[at + 3 + reach] - taps[at + 4 - reach])
        total = term if total is None else total + term
    return total


def backward(taps, at):
    total = None
    for reach in range(1, 5):
        term = coefs[reach - 1] * (taps[at + 3 + reach] - taps[at + 4 - reach])
        total = term if total is None else total + term
    return total


def every(ref, start, step):
    return ref[pl.ds(start, 8, stride=step), :]


def put_every(ref, start, step, value):
    ref[pl.ds(start, 8, stride=step), :] = value


def place():
    return tuple(lax.axis_index(axis) for axis in DEVICES)


def odd(index):
    return lax.rem(index, 2) == 1


def send_faces(field, x_pair, y_pair, base, rows):
    s, g, h = place()
    for which, ref in enumerate(x_pair):
        low = odd(g) if which == 0 else jnp.logical_not(odd(g))
        start = pl.multiple_of(jnp.where(low, 0, (CX - rows) * CY), 32)
        ref[base * 32 : (base + rows) * 32, :] = field[pl.ds(start, rows * 32), :]
    for which, ref in enumerate(y_pair):
        low = odd(h) if which == 0 else jnp.logical_not(odd(h))
        start = jnp.where(low, 0, CY - rows)
        for c in range(rows):
            for part in range(4):
                at = (base + c) * 32 + part * 8
                ref[at : at + 8, :] = every(field, part * 8 * CY + start + c, CY)


def received(pair, which, end, at):
    value = pair[which][at : at + 8, :]
    return jnp.where(end, 0.0, value) if which == 1 else value


def pack_kernel(vel, den, deal, vel_in, den_in, out, in_sem, out_sem):
    pulls = []
    for part in range(4):
        rows = pl.ds(part * 256, 256)
        pulls.append(
            [
                pltpu.make_async_copy(src.at[rows], dst.at[rows], in_sem.at[part * 2 + i])
                for i, (src, dst) in enumerate(((vel, vel_in), (den, den_in)))
            ]
        )
        for pull in pulls[-1]:
            pull.start()
    pushes = []
    for part in range(4):
        for pull in pulls[part]:
            pull.wait()
        for row in range(part * 4, part * 4 + 4):
            for cls in range(8):
                at = (row * 8 + cls) * 16
                out[at : at + 8, :] = every(vel_in, row * 64 + cls, 8)
                out[at + 8 : at + 16, :] = every(den_in, row * 64 + cls, 8)
        rows = pl.ds(part * 512, 512)
        pushes.append(pltpu.make_async_copy(out.at[rows], deal.at[rows], out_sem.at[part]))
        pushes[-1].start()
    for push in pushes:
        push.wait()


def face_kernel(pres, flow_x, flow_y, gx_a, gx_b, gy_a, gy_b, pres_in, x_in, y_in, sem):
    pulls = [
        pltpu.make_async_copy(src, dst, sem.at[i])
        for i, (src, dst) in enumerate(((pres, pres_in), (flow_x, x_in), (flow_y, y_in)))
    ]
    for pull in pulls:
        pull.start()
    for pull in pulls:
        pull.wait()
    send_faces(pres_in, (gx_a, gx_b), (gy_a, gy_b), 0, HALO)
    send_faces(x_in, (gx_a, gx_b), (), HALO, 4)
    send_faces(y_in, (), (gy_a, gy_b), HALO, 4)


def cut_kernel(corners, dealt, *refs):
    out, rho_lines, vel_lines, cuts, sem = refs[-5:]
    s, g, col_class = place()
    row_class = s * 4 + g
    for t in range(16):
        for part in range(8):
            src = (t * 8 + part) * 16
            dst = t * LINE + 8 + part * 8
            vel_lines[dst : dst + 8, :] = dealt[src : src + 8, :]
            rho_lines[dst : dst + 8, :] = dealt[src + 8 : src + 16, :]

    pushes = []
    for shot in range(4):
        corner_y = corners[shot, 1]

        def block(part, carry):
            corner_x = corners[shot, 0] + part * CX
            wide_row = lax.shift_right_arithmetic(corner_x - 4 - row_class + 15, 4)
            row = lax.shift_right_arithmetic(corner_x - row_class + 15, 4)
            for h in range(8):
                base = (shot * 32 + part * 8 + h) * 24
                wide_col = lax.shift_right_arithmetic(corner_y + h * CY - 4 - col_class + 7, 3)
                col = lax.shift_right_arithmetic(corner_y + h * CY - col_class + 7, 3)
                for k in range(3):
                    line = jnp.clip(wide_row + k, 0, 15)
                    cuts[pl.ds(base + 5 * k, 5), :] = rho_lines[
                        pl.ds(line * LINE + 8 + wide_col, 5), :
                    ]
                for k in range(2):
                    cuts[pl.ds(base + 16 + 4 * k, 4), :] = vel_lines[
                        pl.ds((row + k) * LINE + 8 + col, 4), :
                    ]
            return carry

        lax.fori_loop(0, 4, block, 0)
        rows = pl.ds(shot * 768, 768)
        pushes.append(pltpu.make_async_copy(cuts.at[rows], out.at[rows], sem.at[shot]))
        pushes[-1].start()
    for push in pushes:
        push.wait()


def unpack_model(corners, window, buoy, modu, rho):
    s, g, h = place()
    corner_x = corners[s, 0] + g * CX
    corner_y = corners[s, 1] + h * CY
    wide_turn = lax.rem(8 - lax.rem(corner_y + 4, 8), 8)
    turn = lax.rem(8 - lax.rem(corner_y, 8), 8)
    sub = lax.broadcasted_iota(jnp.int32, (8, 128), 0)
    for w in range(WIDE):
        cls = lax.rem(corner_x + 12 + w, 16)
        row_in = (g * CX + w - 4 >= 0) & (g * CX + w - 4 < 4 * CX)
        for n in range(5):
            got = every(window, cls * 192 + 5 * (w // 16) + n, 24)
            got = pltpu.roll(got, wide_turn, 0)
            at = w * WIDE + n * 8
            rho[at : at + 8, :] = got
            col = sub + (h * CY + n * 8 - 4)
            inside = (col >= 0) & (col < 8 * CY) & row_in
            buoy[at : at + 8, :] = jnp.where(inside, time_step * (1.0 / got), 0.0)
    for w in range(CX):
        cls = lax.rem(corner_x + w, 16)
        for n in range(4):
            got = every(window, cls * 192 + 16 + 4 * (w // 16) + n, 24)
            speed = pltpu.roll(got, turn, 0)
            at = w * CY + n * 8
            dens = rho[(w + 4) * WIDE + 4 + n * 8 : (w + 4) * WIDE + 12 + n * 8, :]
            modu[at : at + 8, :] = time_step * (dens * speed * speed)


def buoy_at(buoy, x, y, rows=8):
    return buoy[pl.ds((x + 4) * WIDE + 4 + y, rows), :]


def pull_all(pairs, sem):
    pulls = [pltpu.make_async_copy(src, dst, sem.at[i]) for i, (src, dst) in enumerate(pairs)]
    for pull in pulls:
        pull.start()
    return pulls


def grad0_kernel(mat_f, pres_from, gx_a, gx_b, gy_a, gy_b, x_from, y_from, *refs):
    outs, scratch = refs[:5], refs[5:]
    grad_x, grad_y, grad_z, wide_x, wide_y, padded, pres, in_x, in_y, in_sem, out_sem = scratch
    for pull in pull_all(((pres_from, pres), (x_from, in_x), (y_from, in_y)), in_sem):
        pull.wait()
    s, g, h = place()
    end_x = (g == 0) | (g == 3)
    end_y = (h == 0) | (h == 7)
    for x in range(CX):
        at = (x + 8) * PAD + 8
        padded[at : at + 32, :] = pres[x * CY : (x + 1) * CY, :]
        wide_y[x * WIDE + 4 : x * WIDE + 36, :] = in_y[x * CY : (x + 1) * CY, :]
    wide_x[4 * CY : 36 * CY, :] = in_x[...]
    x_pair, y_pair = (gx_a, gx_b), (gy_a, gy_b)
    for which in range(2):
        low = odd(g) if which == 0 else jnp.logical_not(odd(g))
        start = jnp.where(low, -HALO, CX)
        for i in range(HALO):
            for part in range(4):
                at = pl.multiple_of((start + i + 8) * PAD + 8 + part * 8, 8)
                padded[pl.ds(at, 8), :] = received(x_pair, which, end_x, i * 32 + part * 8)
        start = jnp.where(low, 0, 36)
        for i in range(4):
            for part in range(4):
                at = pl.multiple_of((start + i) * CY + part * 8, 8)
                wide_x[pl.ds(at, 8), :] = received(x_pair, which, end_x, (HALO + i) * 32 + part * 8)
        low = odd(h) if which == 0 else jnp.logical_not(odd(h))
        start = jnp.where(low, -HALO, CY)
        for c in range(HALO):
            for part in range(4):
                at = (part * 8 + 8) * PAD + start + c + 8
                put_every(padded, at, PAD, received(y_pair, which, end_y, c * 32 + part * 8))
        start = jnp.where(low, 0, 36)
        for c in range(4):
            for part in range(4):
                value = received(y_pair, which, end_y, (HALO + c) * 32 + part * 8)
                put_every(wide_y, part * 8 * WIDE + start + c, WIDE, value)

    def along_x(chunk, carry):
        x0 = chunk * 4 - 4
        for n in range(4):
            taps = [
                padded[pl.ds(pl.multiple_of((x0 + d + 8) * PAD + 8 + n * 8, 8), 8), :]
                for d in range(-3, 8)
            ]
            for i in range(4):
                at = pl.multiple_of((x0 + i + 4) * CY + n * 8, 8)
                grad_x[pl.ds(at, 8), :] = forward(taps, i)
        return carry

    lax.fori_loop(0, 10, along_x, 0)

    def along_y(x, carry):
        taps = [every(padded, (x + 8) * PAD + 4 + d, 5) for d in range(-3, 9)]
        for j in range(5):
            put_every(grad_y, x * WIDE + j, 5, forward(taps, j))
        return carry

    lax.fori_loop(0, CX, along_y, 0)
    for chunk in range(8):
        rows = slice(chunk * 128, (chunk + 1) * 128)
        grad_z[rows, :] = depth_difference(pres[rows, :], mat_f)
    for push in pull_all(zip(scratch[:5], outs), out_sem):
        push.wait()


def kick_source(step, cells, amps, field, first=0, end=CX):
    s, g, h = place()
    x = cells[s, 0] - g * CX
    y = cells[s, 1] - h * CY

    @pl.when((x >= first) & (x < end) & (y >= 0) & (y < CY))
    def _():
        at = x * CY + y
        lane = lax.broadcasted_iota(jnp.int32, (1, 128), 1)
        kick = time_step * amps[s, step]
        field[pl.ds(at, 1), :] = field[pl.ds(at, 1), :] + jnp.where(lane == cells[s, 2], kick, 0.0)


def step0_kernel(corners, cells, amps, mat_b, window, *refs):
    sources, outs, scratch = refs[:7], refs[7:17], refs[17:]
    new_p, wide_x, wide_y, new_z, buoy, modu, gx_a, gx_b, gy_a, gy_b = outs
    pres, in_x, in_y, in_z, grad_x, grad_y, grad_z, rho, spread, sem = scratch
    pulls = pull_all(zip(sources, scratch[:7]), sem)
    unpack_model(corners, window, buoy, modu, rho)
    for pull in pulls:
        pull.wait()

    def flow(x, carry):
        for n in range(4):
            at = pl.multiple_of(x * CY + n * 8, 8)
            value = in_z[pl.ds(at, 8), :] - buoy_at(buoy, x, n * 8) * grad_z[pl.ds(at, 8), :]
            new_z[pl.ds(at, 8), :] = value
        for n in range(5):
            at = pl.multiple_of(x * WIDE + n * 8, 8)
            wide_y[pl.ds(at, 8), :] = (
                in_y[pl.ds(at, 8), :] - buoy_at(buoy, x, n * 8 - 4) * grad_y[pl.ds(at, 8), :]
            )
        return carry

    lax.fori_loop(0, CX, flow, 0, unroll=4)

    def flow_x(x, carry):
        for n in range(4):
            at = pl.multiple_of(x * CY + n * 8, 8)
            wide_x[pl.ds(at, 8), :] = (
                in_x[pl.ds(at, 8), :] - buoy_at(buoy, x - 4, n * 8) * grad_x[pl.ds(at, 8), :]
            )
        return carry

    lax.fori_loop(0, WIDE, flow_x, 0, unroll=4)
    for chunk in range(8):
        rows = slice(chunk * 128, (chunk + 1) * 128)
        spread[rows, :] = depth_difference(new_z[rows, :], mat_b)

    def update(chunk, carry):
        x0 = chunk * 4
        part_x = {}
        for j in range(4):
            taps = [every(wide_x, (x0 + d + 4) * CY + j, 4) for d in range(-4, 7)]
            for i in range(4):
                part_x[i, j] = backward(taps, i)
        for i in range(4):
            taps = [every(wide_y, (x0 + i) * WIDE + 4 + d, 4) for d in range(-4, 7)]
            for j in range(4):
                at = (x0 + i) * CY + j
                total = part_x[i, j] + backward(taps, j) + every(spread, at, 4)
                put_every(new_p, at, 4, every(pres, at, 4) - every(modu, at, 4) * total)
        return carry

    lax.fori_loop(0, 8, update, 0)
    kick_source(0, cells, amps, new_p)
    send_faces(new_p, (gx_a, gx_b), (gy_a, gy_b), 0, HALO)


def inner_kernel(mat_f, mat_b, pres, in_x, in_y, in_z, buoy, wide_x, wide_y, new_z, spread):
    for chunk in range(8):
        rows = slice(chunk * 128, (chunk + 1) * 128)
        grad = depth_difference(pres[rows, :], mat_f)
        light = jnp.concatenate(
            [buoy_at(buoy, x, 0, 32) for x in range(chunk * 4, chunk * 4 + 4)], axis=0
        )
        new_z[rows, :] = in_z[rows, :] - light * grad

    def along_x(chunk, carry):
        x0 = chunk * 4 + 4
        for n in range(4):
            taps = [
                pres[pl.ds(pl.multiple_of((x0 + d) * CY + n * 8, 8), 8), :] for d in range(-3, 8)
            ]
            for i in range(4):
                at = pl.multiple_of((x0 + i + 4) * CY + n * 8, 8)
                wide_x[pl.ds(at, 8), :] = in_x[pl.ds(at, 8), :] - buoy_at(
                    buoy, x0 + i, n * 8
                ) * forward(taps, i)
        return carry

    lax.fori_loop(0, 6, along_x, 0)

    def along_y(x, carry):
        taps = [every(pres, x * CY + 4 + d, 3) for d in range(-3, 7)]
        for j in range(3):
            at = x * WIDE + 8 + j
            light = every(buoy, (x + 4) * WIDE + 8 + j, 3)
            put_every(wide_y, at, 3, every(in_y, at, 3) - light * forward(taps, j))
        return carry

    lax.fori_loop(0, CX, along_y, 0, unroll=4)
    wide_x[0 : 8 * CY, :] = in_x[0 : 8 * CY, :]
    wide_x[32 * CY : 40 * CY, :] = in_x[32 * CY : 40 * CY, :]
    for x in range(CX):
        wide_y[x * WIDE : x * WIDE + 8, :] = in_y[x * WIDE : x * WIDE + 8, :]
        wide_y[x * WIDE + 32 : x * WIDE + 40, :] = in_y[x * WIDE + 32 : x * WIDE + 40, :]
    for chunk in range(8):
        rows = slice(chunk * 128, (chunk + 1) * 128)
        spread[rows, :] = depth_difference(new_z[rows, :], mat_b)

    def across(chunk, carry):
        x0 = chunk * 4 + 8
        for n in range(4):
            taps = [
                wide_x[pl.ds(pl.multiple_of((x0 + d + 4) * CY + n * 8, 8), 8), :]
                for d in range(-4, 7)
            ]
            for i in range(4):
                at = pl.multiple_of((x0 + i) * CY + n * 8, 8)
                spread[pl.ds(at, 8), :] = spread[pl.ds(at, 8), :] + backward(taps, i)
        return carry

    lax.fori_loop(0, 4, across, 0)

    def along(x, carry):
        taps = [every(wide_y, x * WIDE + 12 + d, 2) for d in range(-4, 5)]
        for j in range(2):
            at = x * CY + 8 + j
            put_every(spread, at, 2, every(spread, at, 2) + backward(taps, j))
        return carry

    lax.fori_loop(0, CX, along, 0, unroll=4)


def edge_kernel(step, *refs):
    cells, amps, pres, gx_a, gx_b, gy_a, gy_b, in_x, in_y, buoy, modu, spread = refs[:12]
    last = step == STEPS - 1
    if last:
        p_to, x_to, y_to, low_x, high_x, low_y, high_y, wide_x, wide_y, new_p, out_y, sem = refs[12:]
        pushes = []

        def push(src, dst, rows):
            pushes.append(pltpu.make_async_copy(src, dst.at[rows], sem.at[len(pushes)]))
            pushes[-1].start()

    else:
        new_p, wide_x, wide_y, to_a, to_b, to_c, to_d, low_x, high_x, low_y, high_y = refs[12:]
    wide_x[8 * CY : 32 * CY, :] = in_x[8 * CY : 32 * CY, :]
    for x in range(CX):
        wide_y[x * WIDE + 8 : x * WIDE + 32, :] = in_y[x * WIDE + 8 : x * WIDE + 32, :]
    s, g, h = place()
    end_x = (g == 0) | (g == 3)
    end_y = (h == 0) | (h == 7)
    x_pair, y_pair = (gx_a, gx_b), (gy_a, gy_b)
    low_x[8 * CY : 16 * CY, :] = pres[0 : 8 * CY, :]
    high_x[0 : 8 * CY, :] = pres[24 * CY : 32 * CY, :]
    for x in range(CX):
        low_y[x * STRIP + 8 : x * STRIP + 16, :] = pres[x * CY : x * CY + 8, :]
        high_y[x * STRIP : x * STRIP + 8, :] = pres[x * CY + 24 : x * CY + 32, :]

    def place_x(which, ref, start):
        for i in range(HALO):
            for part in range(4):
                at = (start + i) * CY + part * 8
                ref[at : at + 8, :] = received(x_pair, which, end_x, i * 32 + part * 8)

    def place_y(which, ref, start):
        for c in range(HALO):
            for part in range(4):
                value = received(y_pair, which, end_y, c * 32 + part * 8)
                put_every(ref, part * 8 * STRIP + start + c, STRIP, value)

    for where, put, low, high in ((g, place_x, low_x, high_x), (h, place_y, low_y, high_y)):

        @pl.when(odd(where))
        def _():
            put(0, low, 1)
            put(1, high, 8)

        @pl.when(jnp.logical_not(odd(where)))
        def _():
            put(1, low, 1)
            put(0, high, 8)

    for strip, first in ((low_x, -4), (high_x, 28)):
        for half in range(2):
            for n in range(4):
                taps = [
                    strip[(half * 4 + 4 + d) * CY + n * 8 : (half * 4 + 4 + d) * CY + n * 8 + 8, :]
                    for d in range(-3, 8)
                ]
                for i in range(4):
                    x = first + half * 4 + i
                    at = (x + 4) * CY + n * 8
                    wide_x[at : at + 8, :] = in_x[at : at + 8, :] - buoy_at(
                        buoy, x, n * 8
                    ) * forward(taps, i)

    if last:
        push(wide_x.at[pl.ds(4 * CY, CX * CY)], x_to, pl.ds(0, CX * CY))

    def rows(x0, with_x):
        part_x = {}
        if with_x:
            for n in range(4):
                taps = [
                    wide_x[pl.ds(pl.multiple_of((x0 + d + 4) * CY + n * 8, 8), 8), :]
                    for d in range(-4, 7)
                ]
                for i in range(4):
                    part_x[i, n] = backward(taps, i)
        for i in range(4):
            x = x0 + i
            for strip, col in ((low_y, 0), (high_y, 32)):
                taps = [strip[pl.ds(x * STRIP + 4 + d, 8), :] for d in range(-3, 5)]
                at = pl.multiple_of(x * WIDE + col, 8)
                wide_y[pl.ds(at, 8), :] = in_y[pl.ds(at, 8), :] - buoy_at(
                    buoy, x, col - 4
                ) * forward(taps, 0)
            for n in range(4):
                at = pl.multiple_of(x * CY + n * 8, 8)
                total = spread[pl.ds(at, 8), :]
                if n in (0, 3):
                    taps = [wide_y[pl.ds(x * WIDE + 4 + n * 8 + d, 8), :] for d in range(-4, 4)]
                    total = total + backward(taps, 0)
                if with_x:
                    total = total + part_x[i, n]
                new_p[pl.ds(at, 8), :] = pres[pl.ds(at, 8), :] - modu[pl.ds(at, 8), :] * total

    for first, count, with_x in ((0, 2, True), (8, 4, False), (24, 2, True)):

        def some(chunk, carry):
            rows(first + chunk * 4, with_x)
            return carry

        lax.fori_loop(0, count, some, 0)
        if last:
            kick_source(step, cells, amps, new_p, first, first + count * 4)
            for x in range(first, first + count * 4):
                out_y[x * CY : (x + 1) * CY, :] = wide_y[x * WIDE + 4 : x * WIDE + 36, :]
            part = pl.ds(first * CY, count * 4 * CY)
            push(new_p.at[part], p_to, part)
            push(out_y.at[part], y_to, part)
    if last:
        for copy in pushes:
            copy.wait()
    else:
        kick_source(step, cells, amps, new_p)
        send_faces(new_p, (to_a, to_b), (to_c, to_d), 0, HALO)


def shape(rows, dtype=f32):
    return jax.ShapeDtypeStruct((rows, 128), dtype)


def vmem(rows):
    return pltpu.VMEM((rows, 128), f32)


def call(kernel, outs, args, scratch, name, smem=0, hbm=(), loose=(), to_hbm=False, cost=None):
    spaces = [
        pltpu.SMEM if i < smem else pltpu.HBM if i in hbm else pl.ANY if i in loose else pltpu.VMEM
        for i in range(len(args))
    ]
    if to_hbm:
        outs = [pltpu.HBM(out.shape, out.dtype) for out in outs]
    outputs = pltpu.HBM if to_hbm else pltpu.VMEM
    specs = [pl.BlockSpec(memory_space=space) for space in spaces]
    args = [
        pltpu.with_memory_space_constraint(arg, pltpu.HBM) if i in hbm else arg
        for i, arg in enumerate(args)
    ]
    return pl.pallas_call(
        kernel,
        out_shape=outs,
        in_specs=specs,
        out_specs=[pl.BlockSpec(memory_space=outputs)] * len(outs),
        scratch_shapes=scratch,
        cost_estimate=cost,
        compiler_params=pltpu.CompilerParams(vmem_limit_bytes=24 * 1024 * 1024),
        name=name,
    )(*args)


x_swaps = ([(0, 1), (1, 0), (2, 3), (3, 2)], [(1, 2), (2, 1), (0, 3), (3, 0)])
y_swaps = (
    [(i, i ^ 1) for i in range(8)],
    [(1, 2), (2, 1), (3, 4), (4, 3), (5, 6), (6, 5), (7, 0), (0, 7)],
)


def exchange(faces):
    gy_b = lax.ppermute(faces[3], "gy", y_swaps[1])
    gy_a = lax.ppermute(faces[2], "gy", y_swaps[0])
    gx_b = lax.ppermute(faces[1], "gx", x_swaps[1])
    gx_a = lax.ppermute(faces[0], "gx", x_swaps[0])
    return [gx_a, gx_b, gy_a, gy_b]


def shards(velocity, density, offsets, pressure, vel_x, vel_y, vel_z, source_cells, wavelet):
    mat_f, mat_b = (jnp.asarray(m) for m in depth_matrices())
    vel = velocity.reshape(16 * 64, 128)
    den = density.reshape(16 * 64, 128)
    pres = pressure.reshape(CX * CY, 128)
    flow_x = vel_x.reshape(CX * CY, 128)
    flow_y = vel_y.reshape(CX * CY, 128)
    flow_z = vel_z.reshape(CX * CY, 128)
    block = shape(CX * CY)
    wide = shape(WIDE * CY)
    face = shape(HALO * 32)
    cost = pl.CostEstimate(flops=20_000_000, bytes_accessed=8_000_000, transcendentals=0)

    dma = pltpu.SemaphoreType.DMA
    (deal,) = call(
        pack_kernel,
        [shape(128 * 16)],
        [vel, den],
        [vmem(1024), vmem(1024), vmem(2048), dma((8,)), dma((4,))],
        "pack",
        hbm=(0, 1),
        to_hbm=True,
    )
    dealt = lax.all_to_all(deal.reshape(128, 16, 128), DEVICES, 0, 0, tiled=True)
    faces = call(
        face_kernel,
        [shape((HALO + 4) * 32)] * 4,
        [pres, flow_x, flow_y],
        [vmem(1024)] * 3 + [dma((3,))],
        "first_faces",
        hbm=(0, 1, 2),
        cost=cost,
    )
    faces = exchange(faces)
    (cut,) = call(
        cut_kernel,
        [shape(128 * 24)],
        [offsets, dealt.reshape(128 * 16, 128), *faces],
        [vmem(16 * LINE), vmem(16 * LINE), vmem(128 * 24), dma((4,))],
        "cut",
        smem=1,
        loose=(2, 3, 4, 5),
        to_hbm=True,
    )
    window = lax.all_to_all(cut.reshape(128, 24, 128), DEVICES, 0, 0, tiled=True)
    window = window.reshape(128 * 24, 128)
    grad_x, grad_y, grad_z, flow_x, flow_y = call(
        grad0_kernel,
        [wide, wide, block, wide, wide],
        [mat_f, pres, *faces, flow_x, flow_y],
        [vmem(WIDE * CY)] * 2 + [vmem(CX * CY)] + [vmem(WIDE * CY)] * 2
        + [vmem(PAD * PAD)] + [vmem(CX * CY)] * 3 + [dma((3,)), dma((5,))],
        "step0_gradients",
        hbm=(1, 6, 7),
        to_hbm=True,
        cost=cost,
    )
    pres, flow_x, flow_y, flow_z, buoy, modu, *faces = call(
        step0_kernel,
        [block, wide, wide, block, shape(WIDE * WIDE), block] + [face] * 4,
        [offsets, source_cells, wavelet, mat_b, window]
        + [pres, flow_x, flow_y, flow_z, grad_x, grad_y, grad_z],
        [vmem(CX * CY), vmem(WIDE * CY), vmem(WIDE * CY), vmem(CX * CY)]
        + [vmem(WIDE * CY), vmem(WIDE * CY), vmem(CX * CY)]
        + [vmem(WIDE * WIDE), vmem(CX * CY), dma((7,))],
        "step0",
        smem=3,
        hbm=range(5, 12),
    )
    for step in range(1, STEPS):
        last = step == STEPS - 1
        faces = exchange(faces)
        flow_x, flow_y, flow_z, spread = call(
            inner_kernel,
            [wide, wide, block, block],
            [mat_f, mat_b, pres, flow_x, flow_y, flow_z, buoy],
            [],
            f"inner{step}",
            cost=cost,
        )
        pres, flow_x, flow_y, *faces = call(
            functools.partial(edge_kernel, step),
            [block, block, block] if last else [block, wide, wide] + [face] * 4,
            [source_cells, wavelet, pres, *faces, flow_x, flow_y, buoy, modu, spread],
            [vmem(16 * CY), vmem(16 * CY), vmem(CX * STRIP), vmem(CX * STRIP)]
            + ([vmem(WIDE * CY)] * 2 + [vmem(CX * CY)] * 2 + [dma((7,))] if last else []),
            f"edge{step}",
            smem=2,
            to_hbm=last,
        )
    return tuple(a.reshape(1, CX, CY, 128) for a in (pres, flow_x, flow_y, flow_z))


def solution(mesh):
    return jax.shard_map(
        shards,
        mesh=mesh,
        in_specs=(
            P(("shot", "gx"), "gy", None),
            P(("shot", "gx"), "gy", None),
            P(),
            P("shot", "gx", "gy", None),
            P("shot", "gx", "gy", None),
            P("shot", "gx", "gy", None),
            P("shot", "gx", "gy", None),
            P(),
            P(),
        ),
        out_specs=(
            P("shot", "gx", "gy", None),
            P("shot", "gx", "gy", None),
            P("shot", "gx", "gy", None),
            P("shot", "gx", "gy", None),
        ),
        check_vma=False,
    )
```

```python
import functools

import jax
import jax.numpy as jnp
import numpy as np
from jax import lax
from jax.experimental import pallas as pl
from jax.experimental.pallas import tpu as pltpu
from jax.sharding import PartitionSpec as P

CX = 32
CY = 32
STEPS = 4
HALO = 7
WIDE = 40
PAD = 48
LINE = 80
STRIP = 24
DEVICES = ("shot", "gx", "gy")

coefs = (1225.0 / 1024.0, -245.0 / 3072.0, 49.0 / 5120.0, -5.0 / 7168.0)
time_step = 0.09

f32 = jnp.float32
bf16 = jnp.bfloat16


def depth_matrices():
    out = []
    for lead in (0, 1):
        full = np.zeros((128, 128), np.float32)
        for reach in range(1, 5):
            for k in range(128):
                up, down = k + reach - lead, k - reach + 1 - lead
                if up < 128:
                    full[up, k] += np.float32(coefs[reach - 1])
                if down >= 0:
                    full[down, k] -= np.float32(coefs[reach - 1])
        high = full.astype(jnp.bfloat16)
        low = (full - high.astype(np.float32)).astype(jnp.bfloat16)
        out.append(np.concatenate([high, high, low], axis=0))
    return out


def depth_difference(values, mat_ref):
    high = values.astype(bf16)
    low = (values - high.astype(f32)).astype(bf16)
    main = jnp.dot(
        jnp.concatenate([high, low], axis=1), mat_ref[0:256, :], preferred_element_type=f32
    )
    return main + jnp.dot(high, mat_ref[256:384, :], preferred_element_type=f32)


def forward(taps, at):
    total = None
    for reach in range(1, 5):
        term = coefs[reach - 1] * (taps[at + 3 + reach] - taps[at + 4 - reach])
        total = term if total is None else total + term
    return total


def backward(taps, at):
    total = None
    for reach in range(1, 5):
        term = coefs[reach - 1] * (taps[at + 3 + reach] - taps[at + 4 - reach])
        total = term if total is None else total + term
    return total


def every(ref, start, step):
    return ref[pl.ds(start, 8, stride=step), :]


def put_every(ref, start, step, value):
    ref[pl.ds(start, 8, stride=step), :] = value


def place():
    return tuple(lax.axis_index(axis) for axis in DEVICES)


def odd(index):
    return lax.rem(index, 2) == 1


def send_faces(field, x_pair, y_pair, base, rows):
    s, g, h = place()
    for which, ref in enumerate(x_pair):
        low = odd(g) if which == 0 else jnp.logical_not(odd(g))
        start = pl.multiple_of(jnp.where(low, 0, (CX - rows) * CY), 32)
        ref[base * 32 : (base + rows) * 32, :] = field[pl.ds(start, rows * 32), :]
    for which, ref in enumerate(y_pair):
        low = odd(h) if which == 0 else jnp.logical_not(odd(h))
        start = jnp.where(low, 0, CY - rows)
        for c in range(rows):
            for part in range(4):
                at = (base + c) * 32 + part * 8
                ref[at : at + 8, :] = every(field, part * 8 * CY + start + c, CY)


def received(pair, which, end, at):
    value = pair[which][at : at + 8, :]
    return jnp.where(end, 0.0, value) if which == 1 else value


def pull_all(pairs, sem):
    pulls = [pltpu.make_async_copy(src, dst, sem.at[i]) for i, (src, dst) in enumerate(pairs)]
    for pull in pulls:
        pull.start()
    return pulls


def pack_kernel(vel, den, pres, flow_x, flow_y, deal, gy_b, gy_a, gx_b, gx_a, *scratch):
    vel_in, den_in, pres_in, x_in, y_in, out, in_sem, field_sem, out_sem = scratch
    pulls = []
    for part in range(4):
        rows = pl.ds(part * 256, 256)
        pulls.append(
            [
                pltpu.make_async_copy(src.at[rows], dst.at[rows], in_sem.at[part * 2 + i])
                for i, (src, dst) in enumerate(((vel, vel_in), (den, den_in)))
            ]
        )
        for pull in pulls[-1]:
            pull.start()
    fields = pull_all(((pres, pres_in), (flow_x, x_in), (flow_y, y_in)), field_sem)
    pushes = []
    for part in range(4):
        for pull in pulls[part]:
            pull.wait()
        for row in range(part * 4, part * 4 + 4):
            for cls in range(8):
                at = (row * 8 + cls) * 16
                out[at : at + 8, :] = every(vel_in, row * 64 + cls, 8)
                out[at + 8 : at + 16, :] = every(den_in, row * 64 + cls, 8)
        rows = pl.ds(part * 512, 512)
        pushes.append(pltpu.make_async_copy(out.at[rows], deal.at[rows], out_sem.at[part]))
        pushes[-1].start()
    for pull in fields:
        pull.wait()
    send_faces(pres_in, (gx_a, gx_b), (gy_a, gy_b), 0, HALO)
    send_faces(x_in, (gx_a, gx_b), (), HALO, 4)
    send_faces(y_in, (), (gy_a, gy_b), HALO, 4)
    for push in pushes:
        push.wait()


def cut_kernel(corners, dealt, *refs):
    out, rho_lines, vel_lines, cuts, sem = refs[-5:]
    s, g, col_class = place()
    row_class = s * 4 + g
    for t in range(16):
        for part in range(8):
            src = (t * 8 + part) * 16
            dst = t * LINE + 8 + part * 8
            vel_lines[dst : dst + 8, :] = dealt[src : src + 8, :]
            rho_lines[dst : dst + 8, :] = dealt[src + 8 : src + 16, :]

    pushes = []
    for shot in range(4):
        corner_y = corners[shot, 1]

        def block(part, carry):
            corner_x = corners[shot, 0] + part * CX
            wide_row = lax.shift_right_arithmetic(corner_x - 4 - row_class + 15, 4)
            row = lax.shift_right_arithmetic(corner_x - row_class + 15, 4)
            for h in range(8):
                base = (shot * 32 + part * 8 + h) * 24
                wide_col = lax.shift_right_arithmetic(corner_y + h * CY - 4 - col_class + 7, 3)
                col = lax.shift_right_arithmetic(corner_y + h * CY - col_class + 7, 3)
                for k in range(3):
                    line = jnp.clip(wide_row + k, 0, 15)
                    cuts[pl.ds(base + 5 * k, 5), :] = rho_lines[
                        pl.ds(line * LINE + 8 + wide_col, 5), :
                    ]
                for k in range(2):
                    cuts[pl.ds(base + 16 + 4 * k, 4), :] = vel_lines[
                        pl.ds((row + k) * LINE + 8 + col, 4), :
                    ]
            return carry

        lax.fori_loop(0, 4, block, 0)
        rows = pl.ds(shot * 768, 768)
        pushes.append(pltpu.make_async_copy(cuts.at[rows], out.at[rows], sem.at[shot]))
        pushes[-1].start()
    for push in pushes:
        push.wait()


def unpack_model(corners, window, buoy, modu, rho):
    s, g, h = place()
    corner_x = corners[s, 0] + g * CX
    corner_y = corners[s, 1] + h * CY
    wide_turn = lax.rem(8 - lax.rem(corner_y + 4, 8), 8)
    turn = lax.rem(8 - lax.rem(corner_y, 8), 8)
    sub = lax.broadcasted_iota(jnp.int32, (8, 128), 0)
    for w in range(WIDE):
        cls = lax.rem(corner_x + 12 + w, 16)
        row_in = (g * CX + w - 4 >= 0) & (g * CX + w - 4 < 4 * CX)
        for n in range(5):
            got = every(window, cls * 192 + 5 * (w // 16) + n, 24)
            got = pltpu.roll(got, wide_turn, 0)
            at = w * WIDE + n * 8
            rho[at : at + 8, :] = got
            col = sub + (h * CY + n * 8 - 4)
            inside = (col >= 0) & (col < 8 * CY) & row_in
            buoy[at : at + 8, :] = jnp.where(inside, time_step * (1.0 / got), 0.0)
    for w in range(CX):
        cls = lax.rem(corner_x + w, 16)
        for n in range(4):
            got = every(window, cls * 192 + 16 + 4 * (w // 16) + n, 24)
            speed = pltpu.roll(got, turn, 0)
            at = w * CY + n * 8
            dens = rho[(w + 4) * WIDE + 4 + n * 8 : (w + 4) * WIDE + 12 + n * 8, :]
            modu[at : at + 8, :] = time_step * (dens * speed * speed)


def buoy_at(buoy, x, y, rows=8):
    return buoy[pl.ds((x + 4) * WIDE + 4 + y, rows), :]


def depth_kernel(mat_f, pres_from, grad_to, pres, grad_z, sem):
    pull = pltpu.make_async_copy(pres_from, pres, sem.at[0])
    pull.start()
    pull.wait()
    for chunk in range(8):
        rows = slice(chunk * 128, (chunk + 1) * 128)
        grad_z[rows, :] = depth_difference(pres[rows, :], mat_f)
    push = pltpu.make_async_copy(grad_z, grad_to, sem.at[1])
    push.start()
    push.wait()


def grad0_kernel(pres_from, gy_b, gy_a, gx_b, gx_a, x_from, y_from, *refs):
    outs, scratch = refs[:4], refs[4:]
    grad_x, grad_y, wide_x, wide_y, padded, pres, in_x, in_y, in_sem, out_sem = scratch
    for pull in pull_all(((pres_from, pres), (x_from, in_x), (y_from, in_y)), in_sem):
        pull.wait()
    s, g, h = place()
    end_x = (g == 0) | (g == 3)
    end_y = (h == 0) | (h == 7)
    for x in range(CX):
        at = (x + 8) * PAD + 8
        padded[at : at + 32, :] = pres[x * CY : (x + 1) * CY, :]
        wide_y[x * WIDE + 4 : x * WIDE + 36, :] = in_y[x * CY : (x + 1) * CY, :]
    wide_x[4 * CY : 36 * CY, :] = in_x[...]
    x_pair, y_pair = (gx_a, gx_b), (gy_a, gy_b)
    for which in range(2):
        low = odd(g) if which == 0 else jnp.logical_not(odd(g))
        start = jnp.where(low, -HALO, CX)
        for i in range(HALO):
            for part in range(4):
                at = pl.multiple_of((start + i + 8) * PAD + 8 + part * 8, 8)
                padded[pl.ds(at, 8), :] = received(x_pair, which, end_x, i * 32 + part * 8)
        start = jnp.where(low, 0, 36)
        for i in range(4):
            for part in range(4):
                at = pl.multiple_of((start + i) * CY + part * 8, 8)
                wide_x[pl.ds(at, 8), :] = received(x_pair, which, end_x, (HALO + i) * 32 + part * 8)
        low = odd(h) if which == 0 else jnp.logical_not(odd(h))
        start = jnp.where(low, -HALO, CY)
        for c in range(HALO):
            for part in range(4):
                at = (part * 8 + 8) * PAD + start + c + 8
                put_every(padded, at, PAD, received(y_pair, which, end_y, c * 32 + part * 8))
        start = jnp.where(low, 0, 36)
        for c in range(4):
            for part in range(4):
                value = received(y_pair, which, end_y, (HALO + c) * 32 + part * 8)
                put_every(wide_y, part * 8 * WIDE + start + c, WIDE, value)

    def along_x(chunk, carry):
        x0 = chunk * 4 - 4
        for n in range(4):
            taps = [
                padded[pl.ds(pl.multiple_of((x0 + d + 8) * PAD + 8 + n * 8, 8), 8), :]
                for d in range(-3, 8)
            ]
            for i in range(4):
                at = pl.multiple_of((x0 + i + 4) * CY + n * 8, 8)
                grad_x[pl.ds(at, 8), :] = forward(taps, i)
        return carry

    lax.fori_loop(0, 10, along_x, 0)

    def along_y(x, carry):
        taps = [every(padded, (x + 8) * PAD + 4 + d, 5) for d in range(-3, 9)]
        for j in range(5):
            put_every(grad_y, x * WIDE + j, 5, forward(taps, j))
        return carry

    lax.fori_loop(0, CX, along_y, 0)
    for push in pull_all(zip(scratch[:4], outs), out_sem):
        push.wait()


def kick_source(step, cells, amps, field, first=0, end=CX):
    s, g, h = place()
    x = cells[s, 0] - g * CX
    y = cells[s, 1] - h * CY

    @pl.when((x >= first) & (x < end) & (y >= 0) & (y < CY))
    def _():
        at = x * CY + y
        lane = lax.broadcasted_iota(jnp.int32, (1, 128), 1)
        kick = time_step * amps[s, step]
        field[pl.ds(at, 1), :] = field[pl.ds(at, 1), :] + jnp.where(lane == cells[s, 2], kick, 0.0)


def step0_kernel(corners, cells, amps, mat_b, window, *refs):
    sources, outs, scratch = refs[:7], refs[7:17], refs[17:]
    new_p, wide_x, wide_y, new_z, buoy, modu, gy_b, gy_a, gx_b, gx_a = outs
    pres, in_x, in_y, in_z, grad_x, grad_y, grad_z, rho, spread, sem = scratch
    order = (4, 1, 5, 2, 6, 3, 0)
    pulls = pull_all([(sources[i], scratch[i]) for i in order], sem)
    unpack_model(corners, window, buoy, modu, rho)

    def flow_x(x, carry):
        for n in range(4):
            at = pl.multiple_of(x * CY + n * 8, 8)
            wide_x[pl.ds(at, 8), :] = (
                in_x[pl.ds(at, 8), :] - buoy_at(buoy, x - 4, n * 8) * grad_x[pl.ds(at, 8), :]
            )
        return carry

    def flow_y(x, carry):
        for n in range(5):
            at = pl.multiple_of(x * WIDE + n * 8, 8)
            wide_y[pl.ds(at, 8), :] = (
                in_y[pl.ds(at, 8), :] - buoy_at(buoy, x, n * 8 - 4) * grad_y[pl.ds(at, 8), :]
            )
        return carry

    def flow_z(x, carry):
        for n in range(4):
            at = pl.multiple_of(x * CY + n * 8, 8)
            new_z[pl.ds(at, 8), :] = (
                in_z[pl.ds(at, 8), :] - buoy_at(buoy, x, n * 8) * grad_z[pl.ds(at, 8), :]
            )
        return carry

    for i, (some, count) in enumerate(((flow_x, WIDE), (flow_y, CX), (flow_z, CX))):
        pulls[2 * i].wait()
        pulls[2 * i + 1].wait()
        lax.fori_loop(0, count, some, 0, unroll=4)
    for chunk in range(8):
        rows = slice(chunk * 128, (chunk + 1) * 128)
        spread[rows, :] = depth_difference(new_z[rows, :], mat_b)
    pulls[6].wait()

    def update(chunk, carry):
        x0 = chunk * 4
        part_x = {}
        for j in range(4):
            taps = [every(wide_x, (x0 + d + 4) * CY + j, 4) for d in range(-4, 7)]
            for i in range(4):
                part_x[i, j] = backward(taps, i)
        for i in range(4):
            taps = [every(wide_y, (x0 + i) * WIDE + 4 + d, 4) for d in range(-4, 7)]
            for j in range(4):
                at = (x0 + i) * CY + j
                total = part_x[i, j] + backward(taps, j) + every(spread, at, 4)
                put_every(new_p, at, 4, every(pres, at, 4) - every(modu, at, 4) * total)
        return carry

    lax.fori_loop(0, 8, update, 0)
    kick_source(0, cells, amps, new_p)
    send_faces(new_p, (gx_a, gx_b), (gy_a, gy_b), 0, HALO)


def inner_kernel(mat_f, mat_b, pres, in_x, in_y, in_z, buoy, wide_x, wide_y, new_z, spread):
    for chunk in range(8):
        rows = slice(chunk * 128, (chunk + 1) * 128)
        grad = depth_difference(pres[rows, :], mat_f)
        light = jnp.concatenate(
            [buoy_at(buoy, x, 0, 32) for x in range(chunk * 4, chunk * 4 + 4)], axis=0
        )
        new_z[rows, :] = in_z[rows, :] - light * grad

    def along_x(chunk, carry):
        x0 = chunk * 4 + 4
        for n in range(4):
            taps = [
                pres[pl.ds(pl.multiple_of((x0 + d) * CY + n * 8, 8), 8), :] for d in range(-3, 8)
            ]
            for i in range(4):
                at = pl.multiple_of((x0 + i + 4) * CY + n * 8, 8)
                wide_x[pl.ds(at, 8), :] = in_x[pl.ds(at, 8), :] - buoy_at(
                    buoy, x0 + i, n * 8
                ) * forward(taps, i)
        return carry

    lax.fori_loop(0, 6, along_x, 0)

    def along_y(x, carry):
        taps = [every(pres, x * CY + 4 + d, 3) for d in range(-3, 7)]
        for j in range(3):
            at = x * WIDE + 8 + j
            light = every(buoy, (x + 4) * WIDE + 8 + j, 3)
            put_every(wide_y, at, 3, every(in_y, at, 3) - light * forward(taps, j))
        return carry

    lax.fori_loop(0, CX, along_y, 0, unroll=4)
    wide_x[0 : 8 * CY, :] = in_x[0 : 8 * CY, :]
    wide_x[32 * CY : 40 * CY, :] = in_x[32 * CY : 40 * CY, :]
    for x in range(CX):
        wide_y[x * WIDE : x * WIDE + 8, :] = in_y[x * WIDE : x * WIDE + 8, :]
        wide_y[x * WIDE + 32 : x * WIDE + 40, :] = in_y[x * WIDE + 32 : x * WIDE + 40, :]
    for chunk in range(8):
        rows = slice(chunk * 128, (chunk + 1) * 128)
        spread[rows, :] = depth_difference(new_z[rows, :], mat_b)

    def across(chunk, carry):
        x0 = chunk * 4 + 8
        for n in range(4):
            taps = [
                wide_x[pl.ds(pl.multiple_of((x0 + d + 4) * CY + n * 8, 8), 8), :]
                for d in range(-4, 7)
            ]
            for i in range(4):
                at = pl.multiple_of((x0 + i) * CY + n * 8, 8)
                spread[pl.ds(at, 8), :] = spread[pl.ds(at, 8), :] + backward(taps, i)
        return carry

    lax.fori_loop(0, 4, across, 0)

    def along(x, carry):
        taps = [every(wide_y, x * WIDE + 12 + d, 2) for d in range(-4, 5)]
        for j in range(2):
            at = x * CY + 8 + j
            put_every(spread, at, 2, every(spread, at, 2) + backward(taps, j))
        return carry

    lax.fori_loop(0, CX, along, 0, unroll=4)


def edge_kernel(step, *refs):
    cells, amps, pres, gy_b, gy_a, gx_b, gx_a, in_x, in_y, buoy, modu, spread = refs[:12]
    last = step == STEPS - 1
    if last:
        p_to, x_to, y_to, low_x, high_x, low_y, high_y, wide_x, wide_y, new_p, out_y, sem = refs[12:]
        pushes = []

        def push(src, dst, rows):
            pushes.append(pltpu.make_async_copy(src, dst.at[rows], sem.at[len(pushes)]))
            pushes[-1].start()

    else:
        new_p, wide_x, wide_y, to_d, to_c, to_b, to_a, low_x, high_x, low_y, high_y = refs[12:]
    wide_x[8 * CY : 32 * CY, :] = in_x[8 * CY : 32 * CY, :]
    for x in range(CX):
        wide_y[x * WIDE + 8 : x * WIDE + 32, :] = in_y[x * WIDE + 8 : x * WIDE + 32, :]
    s, g, h = place()
    end_x = (g == 0) | (g == 3)
    end_y = (h == 0) | (h == 7)
    x_pair, y_pair = (gx_a, gx_b), (gy_a, gy_b)
    low_x[8 * CY : 16 * CY, :] = pres[0 : 8 * CY, :]
    high_x[0 : 8 * CY, :] = pres[24 * CY : 32 * CY, :]
    for x in range(CX):
        low_y[x * STRIP + 8 : x * STRIP + 16, :] = pres[x * CY : x * CY + 8, :]
        high_y[x * STRIP : x * STRIP + 8, :] = pres[x * CY + 24 : x * CY + 32, :]

    def place_x(which, ref, start):
        for i in range(HALO):
            for part in range(4):
                at = (start + i) * CY + part * 8
                ref[at : at + 8, :] = received(x_pair, which, end_x, i * 32 + part * 8)

    def place_y(which, ref, start):
        for c in range(HALO):
            for part in range(4):
                value = received(y_pair, which, end_y, c * 32 + part * 8)
                put_every(ref, part * 8 * STRIP + start + c, STRIP, value)

    for where, put, low, high in ((g, place_x, low_x, high_x), (h, place_y, low_y, high_y)):

        @pl.when(odd(where))
        def _():
            put(0, low, 1)
            put(1, high, 8)

        @pl.when(jnp.logical_not(odd(where)))
        def _():
            put(1, low, 1)
            put(0, high, 8)

    for strip, first in ((low_x, -4), (high_x, 28)):
        for half in range(2):
            for n in range(4):
                taps = [
                    strip[(half * 4 + 4 + d) * CY + n * 8 : (half * 4 + 4 + d) * CY + n * 8 + 8, :]
                    for d in range(-3, 8)
                ]
                for i in range(4):
                    x = first + half * 4 + i
                    at = (x + 4) * CY + n * 8
                    wide_x[at : at + 8, :] = in_x[at : at + 8, :] - buoy_at(
                        buoy, x, n * 8
                    ) * forward(taps, i)

    if last:
        push(wide_x.at[pl.ds(4 * CY, CX * CY)], x_to, pl.ds(0, CX * CY))

    def rows(x0, with_x):
        part_x = {}
        if with_x:
            for n in range(4):
                taps = [
                    wide_x[pl.ds(pl.multiple_of((x0 + d + 4) * CY + n * 8, 8), 8), :]
                    for d in range(-4, 7)
                ]
                for i in range(4):
                    part_x[i, n] = backward(taps, i)
        for i in range(4):
            x = x0 + i
            for strip, col in ((low_y, 0), (high_y, 32)):
                taps = [strip[pl.ds(x * STRIP + 4 + d, 8), :] for d in range(-3, 5)]
                at = pl.multiple_of(x * WIDE + col, 8)
                wide_y[pl.ds(at, 8), :] = in_y[pl.ds(at, 8), :] - buoy_at(
                    buoy, x, col - 4
                ) * forward(taps, 0)
            for n in range(4):
                at = pl.multiple_of(x * CY + n * 8, 8)
                total = spread[pl.ds(at, 8), :]
                if n in (0, 3):
                    taps = [wide_y[pl.ds(x * WIDE + 4 + n * 8 + d, 8), :] for d in range(-4, 4)]
                    total = total + backward(taps, 0)
                if with_x:
                    total = total + part_x[i, n]
                new_p[pl.ds(at, 8), :] = pres[pl.ds(at, 8), :] - modu[pl.ds(at, 8), :] * total

    for first, count, with_x in ((0, 2, True), (8, 4, False), (24, 2, True)):

        def some(chunk, carry):
            rows(first + chunk * 4, with_x)
            return carry

        lax.fori_loop(0, count, some, 0)
        if last:
            kick_source(step, cells, amps, new_p, first, first + count * 4)
            for x in range(first, first + count * 4):
                out_y[x * CY : (x + 1) * CY, :] = wide_y[x * WIDE + 4 : x * WIDE + 36, :]
            part = pl.ds(first * CY, count * 4 * CY)
            push(new_p.at[part], p_to, part)
            push(out_y.at[part], y_to, part)
    if last:
        for copy in pushes:
            copy.wait()
    else:
        kick_source(step, cells, amps, new_p)
        send_faces(new_p, (to_a, to_b), (to_c, to_d), 0, HALO)


def shape(rows, dtype=f32):
    return jax.ShapeDtypeStruct((rows, 128), dtype)


def vmem(rows):
    return pltpu.VMEM((rows, 128), f32)


def call(kernel, outs, args, scratch, name, smem=0, hbm=(), loose=(), to_hbm=(), cost=None):
    spaces = [
        pltpu.SMEM if i < smem else pltpu.HBM if i in hbm else pl.ANY if i in loose else pltpu.VMEM
        for i in range(len(args))
    ]
    to_hbm = range(len(outs)) if to_hbm is True else to_hbm
    outs = [pltpu.HBM(o.shape, o.dtype) if i in to_hbm else o for i, o in enumerate(outs)]
    places = [pltpu.HBM if i in to_hbm else pltpu.VMEM for i in range(len(outs))]
    specs = [pl.BlockSpec(memory_space=space) for space in spaces]
    args = [
        pltpu.with_memory_space_constraint(arg, pltpu.HBM) if i in hbm else arg
        for i, arg in enumerate(args)
    ]
    return pl.pallas_call(
        kernel,
        out_shape=outs,
        in_specs=specs,
        out_specs=[pl.BlockSpec(memory_space=place) for place in places],
        scratch_shapes=scratch,
        cost_estimate=cost,
        compiler_params=pltpu.CompilerParams(vmem_limit_bytes=24 * 1024 * 1024),
        name=name,
    )(*args)


x_swaps = ([(0, 1), (1, 0), (2, 3), (3, 2)], [(1, 2), (2, 1), (0, 3), (3, 0)])
y_swaps = (
    [(i, i ^ 1) for i in range(8)],
    [(1, 2), (2, 1), (3, 4), (4, 3), (5, 6), (6, 5), (7, 0), (0, 7)],
)


def exchange(faces):
    return [
        lax.ppermute(faces[0], "gy", y_swaps[1]),
        lax.ppermute(faces[1], "gy", y_swaps[0]),
        lax.ppermute(faces[2], "gx", x_swaps[1]),
        lax.ppermute(faces[3], "gx", x_swaps[0]),
    ]


def shards(velocity, density, offsets, pressure, vel_x, vel_y, vel_z, source_cells, wavelet):
    mat_f, mat_b = (jnp.asarray(m) for m in depth_matrices())
    vel = velocity.reshape(16 * 64, 128)
    den = density.reshape(16 * 64, 128)
    pres = pressure.reshape(CX * CY, 128)
    flow_x = vel_x.reshape(CX * CY, 128)
    flow_y = vel_y.reshape(CX * CY, 128)
    flow_z = vel_z.reshape(CX * CY, 128)
    block = shape(CX * CY)
    wide = shape(WIDE * CY)
    face = shape(HALO * 32)
    cost = pl.CostEstimate(flops=20_000_000, bytes_accessed=8_000_000, transcendentals=0)
    long = pl.CostEstimate(flops=10**12, bytes_accessed=8_000_000, transcendentals=0)

    dma = pltpu.SemaphoreType.DMA
    deal, *faces = call(
        pack_kernel,
        [shape(128 * 16)] + [shape((HALO + 4) * 32)] * 4,
        [vel, den, pres, flow_x, flow_y],
        [vmem(1024)] * 5 + [vmem(2048), dma((8,)), dma((3,)), dma((4,))],
        "pack",
        hbm=range(5),
        to_hbm=(0,),
    )
    faces = exchange(faces)
    dealt = lax.all_to_all(deal.reshape(128, 16, 128), DEVICES, 0, 0, tiled=True)
    (grad_z,) = call(
        depth_kernel,
        [block],
        [mat_f, pres],
        [vmem(CX * CY), vmem(CX * CY), dma((2,))],
        "step0_depth",
        hbm=(1,),
        to_hbm=True,
        cost=long,
    )
    (cut,) = call(
        cut_kernel,
        [shape(128 * 24)],
        [offsets, dealt.reshape(128 * 16, 128), grad_z],
        [vmem(16 * LINE), vmem(16 * LINE), vmem(128 * 24), dma((4,))],
        "cut",
        smem=1,
        loose=(2,),
        to_hbm=True,
    )
    window = lax.all_to_all(cut.reshape(128, 24, 128), DEVICES, 0, 0, tiled=True)
    window = window.reshape(128 * 24, 128)
    grad_x, grad_y, flow_x, flow_y = call(
        grad0_kernel,
        [wide, wide, wide, wide],
        [pres, *faces, flow_x, flow_y],
        [vmem(WIDE * CY)] * 4
        + [vmem(PAD * PAD)] + [vmem(CX * CY)] * 3 + [dma((3,)), dma((4,))],
        "step0_gradients",
        hbm=(0, 5, 6),
        to_hbm=True,
        cost=long,
    )
    pres, flow_x, flow_y, flow_z, buoy, modu, *faces = call(
        step0_kernel,
        [block, wide, wide, block, shape(WIDE * WIDE), block] + [face] * 4,
        [offsets, source_cells, wavelet, mat_b, window]
        + [pres, flow_x, flow_y, flow_z, grad_x, grad_y, grad_z],
        [vmem(CX * CY), vmem(WIDE * CY), vmem(WIDE * CY), vmem(CX * CY)]
        + [vmem(WIDE * CY), vmem(WIDE * CY), vmem(CX * CY)]
        + [vmem(WIDE * WIDE), vmem(CX * CY), dma((7,))],
        "step0",
        smem=3,
        hbm=range(5, 12),
    )
    for step in range(1, STEPS):
        last = step == STEPS - 1
        faces = exchange(faces)
        flow_x, flow_y, flow_z, spread = call(
            inner_kernel,
            [wide, wide, block, block],
            [mat_f, mat_b, pres, flow_x, flow_y, flow_z, buoy],
            [],
            f"inner{step}",
            cost=cost,
        )
        pres, flow_x, flow_y, *faces = call(
            functools.partial(edge_kernel, step),
            [block, block, block] if last else [block, wide, wide] + [face] * 4,
            [source_cells, wavelet, pres, *faces, flow_x, flow_y, buoy, modu, spread],
            [vmem(16 * CY), vmem(16 * CY), vmem(CX * STRIP), vmem(CX * STRIP)]
            + ([vmem(WIDE * CY)] * 2 + [vmem(CX * CY)] * 2 + [dma((7,))] if last else []),
            f"edge{step}",
            smem=2,
            to_hbm=last or (),
        )
    return tuple(a.reshape(1, CX, CY, 128) for a in (pres, flow_x, flow_y, flow_z))


def solution(mesh):
    return jax.shard_map(
        shards,
        mesh=mesh,
        in_specs=(
            P(("shot", "gx"), "gy", None),
            P(("shot", "gx"), "gy", None),
            P(),
            P("shot", "gx", "gy", None),
            P("shot", "gx", "gy", None),
            P("shot", "gx", "gy", None),
            P("shot", "gx", "gy", None),
            P(),
            P(),
        ),
        out_specs=(
            P("shot", "gx", "gy", None),
            P("shot", "gx", "gy", None),
            P("shot", "gx", "gy", None),
            P("shot", "gx", "gy", None),
        ),
        check_vma=False,
    )
```

```python
import functools

import jax
import jax.numpy as jnp
import numpy as np
from jax import lax
from jax.experimental import pallas as pl
from jax.experimental.pallas import tpu as pltpu
from jax.sharding import PartitionSpec as P

CX = 32
CY = 32
STEPS = 4
HALO = 7
WIDE = 40
PAD = 48
LINE = 80
STRIP = 24
DEVICES = ("shot", "gx", "gy")

coefs = (1225.0 / 1024.0, -245.0 / 3072.0, 49.0 / 5120.0, -5.0 / 7168.0)
time_step = 0.09

f32 = jnp.float32
bf16 = jnp.bfloat16


def depth_matrices():
    out = []
    for lead in (0, 1):
        full = np.zeros((128, 128), np.float32)
        for reach in range(1, 5):
            for k in range(128):
                up, down = k + reach - lead, k - reach + 1 - lead
                if up < 128:
                    full[up, k] += np.float32(coefs[reach - 1])
                if down >= 0:
                    full[down, k] -= np.float32(coefs[reach - 1])
        high = full.astype(jnp.bfloat16)
        low = (full - high.astype(np.float32)).astype(jnp.bfloat16)
        out.append(np.concatenate([high, high, low], axis=0))
    return out


def depth_difference(values, mat_ref):
    high = values.astype(bf16)
    low = (values - high.astype(f32)).astype(bf16)
    main = jnp.dot(
        jnp.concatenate([high, low], axis=1), mat_ref[0:256, :], preferred_element_type=f32
    )
    return main + jnp.dot(high, mat_ref[256:384, :], preferred_element_type=f32)


def forward(taps, at):
    total = None
    for reach in range(1, 5):
        term = coefs[reach - 1] * (taps[at + 3 + reach] - taps[at + 4 - reach])
        total = term if total is None else total + term
    return total


def backward(taps, at):
    total = None
    for reach in range(1, 5):
        term = coefs[reach - 1] * (taps[at + 3 + reach] - taps[at + 4 - reach])
        total = term if total is None else total + term
    return total


def every(ref, start, step):
    return ref[pl.ds(start, 8, stride=step), :]


def put_every(ref, start, step, value):
    ref[pl.ds(start, 8, stride=step), :] = value


def place():
    return tuple(lax.axis_index(axis) for axis in DEVICES)


def odd(index):
    return lax.rem(index, 2) == 1


def send_faces(field, x_pair, y_pair, base, rows):
    s, g, h = place()
    for which, ref in enumerate(x_pair):
        low = odd(g) if which == 0 else jnp.logical_not(odd(g))
        start = pl.multiple_of(jnp.where(low, 0, (CX - rows) * CY), 32)
        ref[base * 32 : (base + rows) * 32, :] = field[pl.ds(start, rows * 32), :]
    for which, ref in enumerate(y_pair):
        low = odd(h) if which == 0 else jnp.logical_not(odd(h))
        start = jnp.where(low, 0, CY - rows)
        for c in range(rows):
            for part in range(4):
                at = (base + c) * 32 + part * 8
                ref[at : at + 8, :] = every(field, part * 8 * CY + start + c, CY)


def received(pair, which, end, at):
    value = pair[which][at : at + 8, :]
    return jnp.where(end, 0.0, value) if which == 1 else value


def pull_all(pairs, sem):
    pulls = [pltpu.make_async_copy(src, dst, sem.at[i]) for i, (src, dst) in enumerate(pairs)]
    for pull in pulls:
        pull.start()
    return pulls


def pack_kernel(vel, den, pres, flow_x, flow_y, deal, gy_b, gy_a, gx_b, gx_a, *scratch):
    vel_in, den_in, pres_in, x_in, y_in, out, in_sem, field_sem, out_sem = scratch
    pulls = []
    for part in range(4):
        rows = pl.ds(part * 256, 256)
        pulls.append(
            [
                pltpu.make_async_copy(src.at[rows], dst.at[rows], in_sem.at[part * 2 + i])
                for i, (src, dst) in enumerate(((vel, vel_in), (den, den_in)))
            ]
        )
        for pull in pulls[-1]:
            pull.start()
    fields = pull_all(((pres, pres_in), (flow_x, x_in), (flow_y, y_in)), field_sem)
    pushes = []
    for part in range(4):
        for pull in pulls[part]:
            pull.wait()
        for row in range(part * 4, part * 4 + 4):
            for cls in range(8):
                at = (row * 8 + cls) * 16
                out[at : at + 8, :] = every(vel_in, row * 64 + cls, 8)
                out[at + 8 : at + 16, :] = every(den_in, row * 64 + cls, 8)
        rows = pl.ds(part * 512, 512)
        pushes.append(pltpu.make_async_copy(out.at[rows], deal.at[rows], out_sem.at[part]))
        pushes[-1].start()
    for pull in fields:
        pull.wait()
    send_faces(pres_in, (gx_a, gx_b), (gy_a, gy_b), 0, HALO)
    send_faces(x_in, (gx_a, gx_b), (), HALO, 4)
    send_faces(y_in, (), (gy_a, gy_b), HALO, 4)
    for push in pushes:
        push.wait()


def cut_kernel(corners, dealt, *refs):
    out, rho_lines, vel_lines, cuts, sem = refs[-5:]
    s, g, col_class = place()
    row_class = s * 4 + g
    for t in range(16):
        for part in range(8):
            src = (t * 8 + part) * 16
            dst = t * LINE + 8 + part * 8
            vel_lines[dst : dst + 8, :] = dealt[src : src + 8, :]
            rho_lines[dst : dst + 8, :] = dealt[src + 8 : src + 16, :]

    pushes = []
    for shot in range(4):
        corner_y = corners[shot, 1]

        def block(part, carry):
            corner_x = corners[shot, 0] + part * CX
            wide_row = lax.shift_right_arithmetic(corner_x - 4 - row_class + 15, 4)
            row = lax.shift_right_arithmetic(corner_x - row_class + 15, 4)
            for h in range(8):
                base = (shot * 32 + part * 8 + h) * 24
                wide_col = lax.shift_right_arithmetic(corner_y + h * CY - 4 - col_class + 7, 3)
                col = lax.shift_right_arithmetic(corner_y + h * CY - col_class + 7, 3)
                for k in range(3):
                    line = jnp.clip(wide_row + k, 0, 15)
                    cuts[pl.ds(base + 5 * k, 5), :] = rho_lines[
                        pl.ds(line * LINE + 8 + wide_col, 5), :
                    ]
                for k in range(2):
                    cuts[pl.ds(base + 16 + 4 * k, 4), :] = vel_lines[
                        pl.ds((row + k) * LINE + 8 + col, 4), :
                    ]
            return carry

        lax.fori_loop(0, 4, block, 0)
        rows = pl.ds(shot * 768, 768)
        pushes.append(pltpu.make_async_copy(cuts.at[rows], out.at[rows], sem.at[shot]))
        pushes[-1].start()
    for push in pushes:
        push.wait()


def unpack_model(corners, window, buoy, modu, rho):
    s, g, h = place()
    corner_x = corners[s, 0] + g * CX
    corner_y = corners[s, 1] + h * CY
    wide_turn = lax.rem(8 - lax.rem(corner_y + 4, 8), 8)
    turn = lax.rem(8 - lax.rem(corner_y, 8), 8)
    sub = lax.broadcasted_iota(jnp.int32, (8, 128), 0)
    for w in range(WIDE):
        cls = lax.rem(corner_x + 12 + w, 16)
        row_in = (g * CX + w - 4 >= 0) & (g * CX + w - 4 < 4 * CX)
        for n in range(5):
            got = every(window, cls * 192 + 5 * (w // 16) + n, 24)
            got = pltpu.roll(got, wide_turn, 0)
            at = w * WIDE + n * 8
            rho[at : at + 8, :] = got
            col = sub + (h * CY + n * 8 - 4)
            inside = (col >= 0) & (col < 8 * CY) & row_in
            buoy[at : at + 8, :] = jnp.where(inside, time_step * (1.0 / got), 0.0)
    for w in range(CX):
        cls = lax.rem(corner_x + w, 16)
        for n in range(4):
            got = every(window, cls * 192 + 16 + 4 * (w // 16) + n, 24)
            speed = pltpu.roll(got, turn, 0)
            at = w * CY + n * 8
            dens = rho[(w + 4) * WIDE + 4 + n * 8 : (w + 4) * WIDE + 12 + n * 8, :]
            modu[at : at + 8, :] = time_step * (dens * speed * speed)


def buoy_at(buoy, x, y, rows=8):
    return buoy[pl.ds((x + 4) * WIDE + 4 + y, rows), :]


def depth_kernel(mat_f, pres_from, grad_to, pres, grad_z, sem):
    pull = pltpu.make_async_copy(pres_from, pres, sem.at[0])
    pull.start()
    pull.wait()
    for chunk in range(8):
        rows = slice(chunk * 128, (chunk + 1) * 128)
        grad_z[rows, :] = depth_difference(pres[rows, :], mat_f)
    push = pltpu.make_async_copy(grad_z, grad_to, sem.at[1])
    push.start()
    push.wait()


def grad0_kernel(pres_from, gy_b, gy_a, gx_b, gx_a, x_from, y_from, *refs):
    outs, scratch = refs[:4], refs[4:]
    grad_x, grad_y, wide_x, wide_y, padded, pres, in_x, in_y, in_sem, out_sem = scratch
    for pull in pull_all(((pres_from, pres), (x_from, in_x), (y_from, in_y)), in_sem):
        pull.wait()
    s, g, h = place()
    end_x = (g == 0) | (g == 3)
    end_y = (h == 0) | (h == 7)
    for x in range(CX):
        at = (x + 8) * PAD + 8
        padded[at : at + 32, :] = pres[x * CY : (x + 1) * CY, :]
        wide_y[x * WIDE + 4 : x * WIDE + 36, :] = in_y[x * CY : (x + 1) * CY, :]
    wide_x[4 * CY : 36 * CY, :] = in_x[...]
    x_pair, y_pair = (gx_a, gx_b), (gy_a, gy_b)
    for which in range(2):
        low = odd(g) if which == 0 else jnp.logical_not(odd(g))
        start = jnp.where(low, -HALO, CX)
        for i in range(HALO):
            for part in range(4):
                at = pl.multiple_of((start + i + 8) * PAD + 8 + part * 8, 8)
                padded[pl.ds(at, 8), :] = received(x_pair, which, end_x, i * 32 + part * 8)
        start = jnp.where(low, 0, 36)
        for i in range(4):
            for part in range(4):
                at = pl.multiple_of((start + i) * CY + part * 8, 8)
                wide_x[pl.ds(at, 8), :] = received(x_pair, which, end_x, (HALO + i) * 32 + part * 8)
        low = odd(h) if which == 0 else jnp.logical_not(odd(h))
        start = jnp.where(low, -HALO, CY)
        for c in range(HALO):
            for part in range(4):
                at = (part * 8 + 8) * PAD + start + c + 8
                put_every(padded, at, PAD, received(y_pair, which, end_y, c * 32 + part * 8))
        start = jnp.where(low, 0, 36)
        for c in range(4):
            for part in range(4):
                value = received(y_pair, which, end_y, (HALO + c) * 32 + part * 8)
                put_every(wide_y, part * 8 * WIDE + start + c, WIDE, value)

    def along_x(chunk, carry):
        x0 = chunk * 4 - 4
        for n in range(4):
            taps = [
                padded[pl.ds(pl.multiple_of((x0 + d + 8) * PAD + 8 + n * 8, 8), 8), :]
                for d in range(-3, 8)
            ]
            for i in range(4):
                at = pl.multiple_of((x0 + i + 4) * CY + n * 8, 8)
                grad_x[pl.ds(at, 8), :] = forward(taps, i)
        return carry

    lax.fori_loop(0, 10, along_x, 0)

    def along_y(x, carry):
        taps = [every(padded, (x + 8) * PAD + 4 + d, 5) for d in range(-3, 9)]
        for j in range(5):
            put_every(grad_y, x * WIDE + j, 5, forward(taps, j))
        return carry

    lax.fori_loop(0, CX, along_y, 0)
    for push in pull_all(zip(scratch[:4], outs), out_sem):
        push.wait()


def kick_source(step, cells, amps, field, first=0, end=CX):
    s, g, h = place()
    x = cells[s, 0] - g * CX
    y = cells[s, 1] - h * CY

    @pl.when((x >= first) & (x < end) & (y >= 0) & (y < CY))
    def _():
        at = x * CY + y
        lane = lax.broadcasted_iota(jnp.int32, (1, 128), 1)
        kick = time_step * amps[s, step]
        field[pl.ds(at, 1), :] = field[pl.ds(at, 1), :] + jnp.where(lane == cells[s, 2], kick, 0.0)


def step0_kernel(corners, cells, amps, mat_b, window, *refs):
    sources, outs, scratch = refs[:7], refs[7:17], refs[17:]
    new_p, wide_x, wide_y, new_z, buoy, modu, gy_b, gy_a, gx_b, gx_a = outs
    pres, in_x, in_y, in_z, grad_x, grad_y, grad_z, rho, spread, sem = scratch
    order = (4, 1, 5, 2, 6, 3, 0)
    pulls = pull_all([(sources[i], scratch[i]) for i in order], sem)
    unpack_model(corners, window, buoy, modu, rho)

    def flow_x(x, carry):
        for n in range(4):
            at = pl.multiple_of(x * CY + n * 8, 8)
            wide_x[pl.ds(at, 8), :] = (
                in_x[pl.ds(at, 8), :] - buoy_at(buoy, x - 4, n * 8) * grad_x[pl.ds(at, 8), :]
            )
        return carry

    def flow_y(x, carry):
        for n in range(5):
            at = pl.multiple_of(x * WIDE + n * 8, 8)
            wide_y[pl.ds(at, 8), :] = (
                in_y[pl.ds(at, 8), :] - buoy_at(buoy, x, n * 8 - 4) * grad_y[pl.ds(at, 8), :]
            )
        return carry

    def flow_z(x, carry):
        for n in range(4):
            at = pl.multiple_of(x * CY + n * 8, 8)
            new_z[pl.ds(at, 8), :] = (
                in_z[pl.ds(at, 8), :] - buoy_at(buoy, x, n * 8) * grad_z[pl.ds(at, 8), :]
            )
        return carry

    for i, (some, count) in enumerate(((flow_x, WIDE), (flow_y, CX), (flow_z, CX))):
        pulls[2 * i].wait()
        pulls[2 * i + 1].wait()
        lax.fori_loop(0, count, some, 0, unroll=4)
    for chunk in range(8):
        rows = slice(chunk * 128, (chunk + 1) * 128)
        spread[rows, :] = depth_difference(new_z[rows, :], mat_b)
    pulls[6].wait()

    def update(chunk, carry):
        x0 = chunk * 4
        part_x = {}
        for j in range(4):
            taps = [every(wide_x, (x0 + d + 4) * CY + j, 4) for d in range(-4, 7)]
            for i in range(4):
                part_x[i, j] = backward(taps, i)
        for i in range(4):
            taps = [every(wide_y, (x0 + i) * WIDE + 4 + d, 4) for d in range(-4, 7)]
            for j in range(4):
                at = (x0 + i) * CY + j
                total = part_x[i, j] + backward(taps, j) + every(spread, at, 4)
                put_every(new_p, at, 4, every(pres, at, 4) - every(modu, at, 4) * total)
        return carry

    lax.fori_loop(0, 8, update, 0)
    kick_source(0, cells, amps, new_p)
    send_faces(new_p, (gx_a, gx_b), (gy_a, gy_b), 0, HALO)


def inner_kernel(mat_f, mat_b, pres, in_x, in_y, in_z, buoy, wide_x, wide_y, new_z, spread):
    for chunk in range(8):
        rows = slice(chunk * 128, (chunk + 1) * 128)
        grad = depth_difference(pres[rows, :], mat_f)
        light = jnp.concatenate(
            [buoy_at(buoy, x, 0, 32) for x in range(chunk * 4, chunk * 4 + 4)], axis=0
        )
        new_z[rows, :] = in_z[rows, :] - light * grad

    def along_x(chunk, carry):
        x0 = chunk * 4 + 4
        for n in range(4):
            taps = [
                pres[pl.ds(pl.multiple_of((x0 + d) * CY + n * 8, 8), 8), :] for d in range(-3, 8)
            ]
            for i in range(4):
                at = pl.multiple_of((x0 + i + 4) * CY + n * 8, 8)
                wide_x[pl.ds(at, 8), :] = in_x[pl.ds(at, 8), :] - buoy_at(
                    buoy, x0 + i, n * 8
                ) * forward(taps, i)
        return carry

    lax.fori_loop(0, 6, along_x, 0)

    def along_y(x, carry):
        taps = [every(pres, x * CY + 4 + d, 3) for d in range(-3, 7)]
        for j in range(3):
            at = x * WIDE + 8 + j
            light = every(buoy, (x + 4) * WIDE + 8 + j, 3)
            put_every(wide_y, at, 3, every(in_y, at, 3) - light * forward(taps, j))
        return carry

    lax.fori_loop(0, CX, along_y, 0, unroll=4)
    wide_x[0 : 8 * CY, :] = in_x[0 : 8 * CY, :]
    wide_x[32 * CY : 40 * CY, :] = in_x[32 * CY : 40 * CY, :]
    for x in range(CX):
        wide_y[x * WIDE : x * WIDE + 8, :] = in_y[x * WIDE : x * WIDE + 8, :]
        wide_y[x * WIDE + 32 : x * WIDE + 40, :] = in_y[x * WIDE + 32 : x * WIDE + 40, :]
    for chunk in range(8):
        rows = slice(chunk * 128, (chunk + 1) * 128)
        spread[rows, :] = depth_difference(new_z[rows, :], mat_b)

    def across(chunk, carry):
        x0 = chunk * 4 + 8
        for n in range(4):
            taps = [
                wide_x[pl.ds(pl.multiple_of((x0 + d + 4) * CY + n * 8, 8), 8), :]
                for d in range(-4, 7)
            ]
            for i in range(4):
                at = pl.multiple_of((x0 + i) * CY + n * 8, 8)
                spread[pl.ds(at, 8), :] = spread[pl.ds(at, 8), :] + backward(taps, i)
        return carry

    lax.fori_loop(0, 4, across, 0)

    def along(x, carry):
        taps = [every(wide_y, x * WIDE + 12 + d, 2) for d in range(-4, 5)]
        for j in range(2):
            at = x * CY + 8 + j
            put_every(spread, at, 2, every(spread, at, 2) + backward(taps, j))
        return carry

    lax.fori_loop(0, CX, along, 0, unroll=4)


def edge_kernel(step, *refs):
    cells, amps, pres, gy_b, gy_a, gx_b, gx_a, in_x, in_y, buoy, modu, spread = refs[:12]
    last = step == STEPS - 1
    if last:
        p_to, x_to, y_to, low_x, high_x, low_y, high_y, wide_x, wide_y, new_p, out_y, sem = refs[12:]
        pushes = []

        def push(src, dst, rows):
            pushes.append(pltpu.make_async_copy(src, dst.at[rows], sem.at[len(pushes)]))
            pushes[-1].start()

    else:
        new_p, wide_x, wide_y, to_d, to_c, to_b, to_a, low_x, high_x, low_y, high_y = refs[12:]
    wide_x[8 * CY : 32 * CY, :] = in_x[8 * CY : 32 * CY, :]
    for x in range(CX):
        wide_y[x * WIDE + 8 : x * WIDE + 32, :] = in_y[x * WIDE + 8 : x * WIDE + 32, :]
    s, g, h = place()
    end_x = (g == 0) | (g == 3)
    end_y = (h == 0) | (h == 7)
    x_pair, y_pair = (gx_a, gx_b), (gy_a, gy_b)
    low_x[8 * CY : 16 * CY, :] = pres[0 : 8 * CY, :]
    high_x[0 : 8 * CY, :] = pres[24 * CY : 32 * CY, :]
    for x in range(CX):
        low_y[x * STRIP + 8 : x * STRIP + 16, :] = pres[x * CY : x * CY + 8, :]
        high_y[x * STRIP : x * STRIP + 8, :] = pres[x * CY + 24 : x * CY + 32, :]

    def place_x(which, ref, start):
        for i in range(HALO):
            for part in range(4):
                at = (start + i) * CY + part * 8
                ref[at : at + 8, :] = received(x_pair, which, end_x, i * 32 + part * 8)

    def place_y(which, ref, start):
        for c in range(HALO):
            for part in range(4):
                value = received(y_pair, which, end_y, c * 32 + part * 8)
                put_every(ref, part * 8 * STRIP + start + c, STRIP, value)

    for where, put, low, high in ((g, place_x, low_x, high_x), (h, place_y, low_y, high_y)):

        @pl.when(odd(where))
        def _():
            put(0, low, 1)
            put(1, high, 8)

        @pl.when(jnp.logical_not(odd(where)))
        def _():
            put(1, low, 1)
            put(0, high, 8)

    for strip, first in ((low_x, -4), (high_x, 28)):
        for half in range(2):
            for n in range(4):
                taps = [
                    strip[(half * 4 + 4 + d) * CY + n * 8 : (half * 4 + 4 + d) * CY + n * 8 + 8, :]
                    for d in range(-3, 8)
                ]
                for i in range(4):
                    x = first + half * 4 + i
                    at = (x + 4) * CY + n * 8
                    wide_x[at : at + 8, :] = in_x[at : at + 8, :] - buoy_at(
                        buoy, x, n * 8
                    ) * forward(taps, i)

    if last:
        push(wide_x.at[pl.ds(4 * CY, CX * CY)], x_to, pl.ds(0, CX * CY))

    def rows(x0, with_x):
        part_x = {}
        if with_x:
            for n in range(4):
                taps = [
                    wide_x[pl.ds(pl.multiple_of((x0 + d + 4) * CY + n * 8, 8), 8), :]
                    for d in range(-4, 7)
                ]
                for i in range(4):
                    part_x[i, n] = backward(taps, i)
        for i in range(4):
            x = x0 + i
            for strip, col in ((low_y, 0), (high_y, 32)):
                taps = [strip[pl.ds(x * STRIP + 4 + d, 8), :] for d in range(-3, 5)]
                at = pl.multiple_of(x * WIDE + col, 8)
                wide_y[pl.ds(at, 8), :] = in_y[pl.ds(at, 8), :] - buoy_at(
                    buoy, x, col - 4
                ) * forward(taps, 0)
            for n in range(4):
                at = pl.multiple_of(x * CY + n * 8, 8)
                total = spread[pl.ds(at, 8), :]
                if n in (0, 3):
                    taps = [wide_y[pl.ds(x * WIDE + 4 + n * 8 + d, 8), :] for d in range(-4, 4)]
                    total = total + backward(taps, 0)
                if with_x:
                    total = total + part_x[i, n]
                new_p[pl.ds(at, 8), :] = pres[pl.ds(at, 8), :] - modu[pl.ds(at, 8), :] * total

    for first, count, with_x in ((0, 2, True), (8, 4, False), (24, 2, True)):

        def some(chunk, carry):
            rows(first + chunk * 4, with_x)
            return carry

        lax.fori_loop(0, count, some, 0)
        if last:
            kick_source(step, cells, amps, new_p, first, first + count * 4)
            for x in range(first, first + count * 4):
                out_y[x * CY : (x + 1) * CY, :] = wide_y[x * WIDE + 4 : x * WIDE + 36, :]
            part = pl.ds(first * CY, count * 4 * CY)
            push(new_p.at[part], p_to, part)
            push(out_y.at[part], y_to, part)
    if last:
        for copy in pushes:
            copy.wait()
    else:
        kick_source(step, cells, amps, new_p)
        send_faces(new_p, (to_a, to_b), (to_c, to_d), 0, HALO)


def shape(rows, dtype=f32):
    return jax.ShapeDtypeStruct((rows, 128), dtype)


def vmem(rows):
    return pltpu.VMEM((rows, 128), f32)


def call(kernel, outs, args, scratch, name, smem=0, hbm=(), loose=(), to_hbm=(), cost=None):
    spaces = [
        pltpu.SMEM if i < smem else pltpu.HBM if i in hbm else pl.ANY if i in loose else pltpu.VMEM
        for i in range(len(args))
    ]
    to_hbm = range(len(outs)) if to_hbm is True else to_hbm
    outs = [pltpu.HBM(o.shape, o.dtype) if i in to_hbm else o for i, o in enumerate(outs)]
    places = [pltpu.HBM if i in to_hbm else pltpu.VMEM for i in range(len(outs))]
    specs = [pl.BlockSpec(memory_space=space) for space in spaces]
    args = [
        pltpu.with_memory_space_constraint(arg, pltpu.HBM) if i in hbm else arg
        for i, arg in enumerate(args)
    ]
    return pl.pallas_call(
        kernel,
        out_shape=outs,
        in_specs=specs,
        out_specs=[pl.BlockSpec(memory_space=place) for place in places],
        scratch_shapes=scratch,
        cost_estimate=cost,
        compiler_params=pltpu.CompilerParams(vmem_limit_bytes=24 * 1024 * 1024),
        name=name,
    )(*args)


GX, GY = 4, 8


def partners(match):
    out = []
    for g in range(GX):
        for h in range(GY):
            to_g, to_h = match(g, h)
            out.append((g * GY + h, to_g * GY + to_h))
    return out


gx_near = partners(lambda g, h: (g ^ 1, h))
gx_far = partners(lambda g, h: (g, h ^ 1) if g in (0, GX - 1) else (3 - g, h))
gy_near = partners(lambda g, h: (g, h ^ 1))
gy_far = partners(lambda g, h: (g ^ 1, h) if h in (0, GY - 1) else (g, ((h + 1) ^ 1) - 1))


def exchange(faces):
    plane = ("gx", "gy")
    return [
        lax.ppermute(face, plane, pairs)
        for face, pairs in zip(faces, (gy_far, gy_near, gx_far, gx_near))
    ]


def shards(velocity, density, offsets, pressure, vel_x, vel_y, vel_z, source_cells, wavelet):
    mat_f, mat_b = (jnp.asarray(m) for m in depth_matrices())
    vel = velocity.reshape(16 * 64, 128)
    den = density.reshape(16 * 64, 128)
    pres = pressure.reshape(CX * CY, 128)
    flow_x = vel_x.reshape(CX * CY, 128)
    flow_y = vel_y.reshape(CX * CY, 128)
    flow_z = vel_z.reshape(CX * CY, 128)
    block = shape(CX * CY)
    wide = shape(WIDE * CY)
    face = shape(HALO * 32)
    cost = pl.CostEstimate(flops=20_000_000, bytes_accessed=8_000_000, transcendentals=0)
    long = pl.CostEstimate(flops=3 * 10**10, bytes_accessed=8_000_000, transcendentals=0)

    dma = pltpu.SemaphoreType.DMA
    deal, *faces = call(
        pack_kernel,
        [shape(128 * 16)] + [shape((HALO + 4) * 32)] * 4,
        [vel, den, pres, flow_x, flow_y],
        [vmem(1024)] * 5 + [vmem(2048), dma((8,)), dma((3,)), dma((4,))],
        "pack",
        hbm=range(5),
        to_hbm=(0,),
    )
    faces = exchange(faces)
    dealt = lax.all_to_all(deal.reshape(128, 16, 128), DEVICES, 0, 0, tiled=True)
    (grad_z,) = call(
        depth_kernel,
        [block],
        [mat_f, pres],
        [vmem(CX * CY), vmem(CX * CY), dma((2,))],
        "step0_depth",
        hbm=(1,),
        to_hbm=True,
        cost=long,
    )
    (cut,) = call(
        cut_kernel,
        [shape(128 * 24)],
        [offsets, dealt.reshape(128 * 16, 128), grad_z],
        [vmem(16 * LINE), vmem(16 * LINE), vmem(128 * 24), dma((4,))],
        "cut",
        smem=1,
        hbm=(2,),
        to_hbm=True,
    )
    window = lax.all_to_all(cut.reshape(128, 24, 128), DEVICES, 0, 0, tiled=True)
    window = window.reshape(128 * 24, 128)
    grad_x, grad_y, flow_x, flow_y = call(
        grad0_kernel,
        [wide, wide, wide, wide],
        [pres, *faces, flow_x, flow_y],
        [vmem(WIDE * CY)] * 4
        + [vmem(PAD * PAD)] + [vmem(CX * CY)] * 3 + [dma((3,)), dma((4,))],
        "step0_gradients",
        hbm=(0, 5, 6),
        to_hbm=True,
        cost=long,
    )
    pres, flow_x, flow_y, flow_z, buoy, modu, *faces = call(
        step0_kernel,
        [block, wide, wide, block, shape(WIDE * WIDE), block] + [face] * 4,
        [offsets, source_cells, wavelet, mat_b, window]
        + [pres, flow_x, flow_y, flow_z, grad_x, grad_y, grad_z],
        [vmem(CX * CY), vmem(WIDE * CY), vmem(WIDE * CY), vmem(CX * CY)]
        + [vmem(WIDE * CY), vmem(WIDE * CY), vmem(CX * CY)]
        + [vmem(WIDE * WIDE), vmem(CX * CY), dma((7,))],
        "step0",
        smem=3,
        hbm=range(5, 12),
    )
    for step in range(1, STEPS):
        last = step == STEPS - 1
        faces = exchange(faces)
        flow_x, flow_y, flow_z, spread = call(
            inner_kernel,
            [wide, wide, block, block],
            [mat_f, mat_b, pres, flow_x, flow_y, flow_z, buoy],
            [],
            f"inner{step}",
            cost=cost,
        )
        pres, flow_x, flow_y, *faces = call(
            functools.partial(edge_kernel, step),
            [block, block, block] if last else [block, wide, wide] + [face] * 4,
            [source_cells, wavelet, pres, *faces, flow_x, flow_y, buoy, modu, spread],
            [vmem(16 * CY), vmem(16 * CY), vmem(CX * STRIP), vmem(CX * STRIP)]
            + ([vmem(WIDE * CY)] * 2 + [vmem(CX * CY)] * 2 + [dma((7,))] if last else []),
            f"edge{step}",
            smem=2,
            to_hbm=last or (),
        )
    return tuple(a.reshape(1, CX, CY, 128) for a in (pres, flow_x, flow_y, flow_z))


def solution(mesh):
    return jax.shard_map(
        shards,
        mesh=mesh,
        in_specs=(
            P(("shot", "gx"), "gy", None),
            P(("shot", "gx"), "gy", None),
            P(),
            P("shot", "gx", "gy", None),
            P("shot", "gx", "gy", None),
            P("shot", "gx", "gy", None),
            P("shot", "gx", "gy", None),
            P(),
            P(),
        ),
        out_specs=(
            P("shot", "gx", "gy", None),
            P("shot", "gx", "gy", None),
            P("shot", "gx", "gy", None),
            P("shot", "gx", "gy", None),
        ),
        check_vma=False,
    )
```

```python
import functools

import jax
import jax.numpy as jnp
import numpy as np
from jax import lax
from jax.experimental import pallas as pl
from jax.experimental.pallas import tpu as pltpu
from jax.sharding import PartitionSpec as P

CX = 32
CY = 32
STEPS = 4
HALO = 7
WIDE = 40
PAD = 48
LINE = 80
MESSAGE = 22
STRIP = 24
DEVICES = ("shot", "gx", "gy")

coefs = (1225.0 / 1024.0, -245.0 / 3072.0, 49.0 / 5120.0, -5.0 / 7168.0)
time_step = 0.09

f32 = jnp.float32
bf16 = jnp.bfloat16


def depth_matrices():
    out = []
    for lead in (0, 1):
        full = np.zeros((128, 128), np.float32)
        for reach in range(1, 5):
            for k in range(128):
                up, down = k + reach - lead, k - reach + 1 - lead
                if up < 128:
                    full[up, k] += np.float32(coefs[reach - 1])
                if down >= 0:
                    full[down, k] -= np.float32(coefs[reach - 1])
        high = full.astype(jnp.bfloat16)
        low = (full - high.astype(np.float32)).astype(jnp.bfloat16)
        out.append(np.concatenate([high, high, low], axis=0))
    return out


def depth_difference(values, mat_ref):
    high = values.astype(bf16)
    low = (values - high.astype(f32)).astype(bf16)
    main = jnp.dot(
        jnp.concatenate([high, low], axis=1), mat_ref[0:256, :], preferred_element_type=f32
    )
    return main + jnp.dot(high, mat_ref[256:384, :], preferred_element_type=f32)


def forward(taps, at):
    total = None
    for reach in range(1, 5):
        term = coefs[reach - 1] * (taps[at + 3 + reach] - taps[at + 4 - reach])
        total = term if total is None else total + term
    return total


def backward(taps, at):
    total = None
    for reach in range(1, 5):
        term = coefs[reach - 1] * (taps[at + 3 + reach] - taps[at + 4 - reach])
        total = term if total is None else total + term
    return total


def every(ref, start, step):
    return ref[pl.ds(start, 8, stride=step), :]


def put_every(ref, start, step, value):
    ref[pl.ds(start, 8, stride=step), :] = value


def place():
    return tuple(lax.axis_index(axis) for axis in DEVICES)


def odd(index):
    return lax.rem(index, 2) == 1


def send_faces(field, x_pair, y_pair, base, rows):
    s, g, h = place()
    for which, ref in enumerate(x_pair):
        low = odd(g) if which == 0 else jnp.logical_not(odd(g))
        start = pl.multiple_of(jnp.where(low, 0, (CX - rows) * CY), 32)
        ref[base * 32 : (base + rows) * 32, :] = field[pl.ds(start, rows * 32), :]
    for which, ref in enumerate(y_pair):
        low = odd(h) if which == 0 else jnp.logical_not(odd(h))
        start = jnp.where(low, 0, CY - rows)
        for c in range(rows):
            for part in range(4):
                at = (base + c) * 32 + part * 8
                ref[at : at + 8, :] = every(field, part * 8 * CY + start + c, CY)


def received(pair, which, end, at):
    value = pair[which][at : at + 8, :]
    return jnp.where(end, 0.0, value) if which == 1 else value


def pull_all(pairs, sem):
    pulls = [pltpu.make_async_copy(src, dst, sem.at[i]) for i, (src, dst) in enumerate(pairs)]
    for pull in pulls:
        pull.start()
    return pulls


def pack_kernel(vel, den, deal, vel_in, den_in, out, in_sem, out_sem):
    pulls = []
    for part in range(4):
        rows = pl.ds(part * 256, 256)
        pulls.append(
            [
                pltpu.make_async_copy(src.at[rows], dst.at[rows], in_sem.at[part * 2 + i])
                for i, (src, dst) in enumerate(((vel, vel_in), (den, den_in)))
            ]
        )
        for pull in pulls[-1]:
            pull.start()
    pushes = []
    for part in range(4):
        for pull in pulls[part]:
            pull.wait()
        for row in range(part * 4, part * 4 + 4):
            for cls in range(8):
                at = (row * 8 + cls) * 16
                out[at : at + 8, :] = every(vel_in, row * 64 + cls, 8)
                out[at + 8 : at + 16, :] = every(den_in, row * 64 + cls, 8)
        rows = pl.ds(part * 512, 512)
        pushes.append(pltpu.make_async_copy(out.at[rows], deal.at[rows], out_sem.at[part]))
        pushes[-1].start()
    for push in pushes:
        push.wait()


def face_kernel(pres, flow_x, flow_y, _, gy_b, gy_a, gx_b, gx_a, pres_in, x_in, y_in, sem):
    pulls = pull_all(((pres, pres_in), (flow_x, x_in), (flow_y, y_in)), sem)
    for pull in pulls:
        pull.wait()
    send_faces(pres_in, (gx_a, gx_b), (gy_a, gy_b), 0, HALO)
    send_faces(x_in, (gx_a, gx_b), (), HALO, 4)
    send_faces(y_in, (), (gy_a, gy_b), HALO, 4)


def cut_kernel(corners, dealt, _, out, rho_lines, vel_lines, cuts, sem):
    s, g, col_class = place()
    row_class = s * 4 + g
    for t in range(16):
        for part in range(8):
            src = (t * 8 + part) * 16
            dst = t * LINE + 8 + part * 8
            vel_lines[dst : dst + 8, :] = dealt[src : src + 8, :]
            rho_lines[dst : dst + 8, :] = dealt[src + 8 : src + 16, :]
    flat = out.reshape(128 * MESSAGE, 128)
    pushes = []
    for shot in range(4):
        col = lax.shift_right_arithmetic(corners[shot, 1] - col_class + 7, 3)
        wide_col = lax.shift_right_arithmetic(corners[shot, 1] - 4 - col_class + 7, 3)

        def block(part, carry):
            corner_x = corners[shot, 0] + part * CX
            row = lax.shift_right_arithmetic(corner_x - row_class + 15, 4)
            low = lax.rem(row_class - corner_x + 4 + 1024, 16) < 4
            rim = jnp.clip(jnp.where(low, row - 1, row + 2), 0, 15)
            base = (shot * 32 + part * 8) * MESSAGE
            line = row * LINE + 8
            rim_line = rim * LINE + 8 + col
            for h in range(8):
                to = base + h * MESSAGE
                for k in range(2):
                    cuts[pl.ds(to + 5 * k, 5), :] = rho_lines[
                        pl.ds(line + wide_col + (k * LINE + 4 * h), 5), :
                    ]
                    cuts[pl.ds(to + 14 + 4 * k, 4), :] = vel_lines[
                        pl.ds(line + col + (k * LINE + 4 * h), 4), :
                    ]
                cuts[pl.ds(to + 10, 4), :] = rho_lines[pl.ds(rim_line + 4 * h, 4), :]
            return carry

        lax.fori_loop(0, 4, block, 0)
        rows = pl.ds(shot * 32 * MESSAGE, 32 * MESSAGE)
        pushes.append(pltpu.make_async_copy(cuts.at[rows], flat.at[rows], sem.at[shot]))
        pushes[-1].start()
    for push in pushes:
        push.wait()


def unpack_model(corners, window, buoy, modu, rho):
    s, g, h = place()
    corner_x = corners[s, 0] + g * CX
    corner_y = corners[s, 1] + h * CY
    wide_turn = lax.rem(8 - lax.rem(corner_y + 4, 8), 8)
    turn = lax.rem(8 - lax.rem(corner_y, 8), 8)
    sub = lax.broadcasted_iota(jnp.int32, (8, 128), 0)
    flat = window.reshape(128 * MESSAGE, 128)
    low_in = (h > 0) | (sub >= 4)
    high_in = (h < 7) | (sub < 4)
    for x in range(-4, CX + 3):
        start = lax.rem(corner_x + 16 + x, 16) * (8 * MESSAGE)
        base = (x + 4) * WIDE
        if 0 <= x < CX:
            for n in range(5):
                got = pltpu.roll(every(flat, start + 5 * (x // 16) + n, MESSAGE), wide_turn, 0)
                rho[base + n * 8 : base + n * 8 + 8, :] = got
                light = time_step * (1.0 / got)
                if n == 0:
                    light = jnp.where(low_in, light, 0.0)
                elif n == 4:
                    light = jnp.where(high_in, light, 0.0)
                buoy[base + n * 8 : base + n * 8 + 8, :] = light
            for n in range(4):
                got = every(flat, start + 14 + 4 * (x // 16) + n, MESSAGE)
                speed = pltpu.roll(got, turn, 0)
                at = x * CY + n * 8
                dens = rho[base + 4 + n * 8 : base + 12 + n * 8, :]
                modu[at : at + 8, :] = time_step * (dens * speed * speed)
        else:
            row_in = (g > 0) if x < 0 else (g < 3)
            for n in range(4):
                got = pltpu.roll(every(flat, start + 10 + n, MESSAGE), turn, 0)
                buoy[base + 4 + n * 8 : base + 12 + n * 8, :] = jnp.where(
                    row_in, time_step * (1.0 / got), 0.0
                )


def buoy_at(buoy, x, y, rows=8):
    return buoy[pl.ds((x + 4) * WIDE + 4 + y, rows), :]


def depth_kernel(mat_f, pres_from, grad_to, pres, grad_z, sem):
    pull = pltpu.make_async_copy(pres_from, pres, sem.at[0])
    pull.start()
    pull.wait()
    for chunk in range(8):
        rows = slice(chunk * 128, (chunk + 1) * 128)
        grad_z[rows, :] = depth_difference(pres[rows, :], mat_f)
    push = pltpu.make_async_copy(grad_z, grad_to, sem.at[1])
    push.start()
    push.wait()


def grad0_kernel(pres_from, gy_b, gy_a, gx_b, gx_a, x_from, y_from, *refs):
    outs, scratch = refs[:4], refs[4:]
    grad_x, grad_y, wide_x, wide_y, padded, pres, in_x, in_y, in_sem, out_sem = scratch
    for pull in pull_all(((pres_from, pres), (x_from, in_x), (y_from, in_y)), in_sem):
        pull.wait()
    s, g, h = place()
    end_x = (g == 0) | (g == 3)
    end_y = (h == 0) | (h == 7)
    for x in range(CX):
        at = (x + 8) * PAD + 8
        padded[at : at + 32, :] = pres[x * CY : (x + 1) * CY, :]
        wide_y[x * WIDE + 4 : x * WIDE + 36, :] = in_y[x * CY : (x + 1) * CY, :]
    wide_x[4 * CY : 36 * CY, :] = in_x[...]
    x_pair, y_pair = (gx_a, gx_b), (gy_a, gy_b)
    for which in range(2):
        low = odd(g) if which == 0 else jnp.logical_not(odd(g))
        start = jnp.where(low, -HALO, CX)
        for i in range(HALO):
            for part in range(4):
                at = pl.multiple_of((start + i + 8) * PAD + 8 + part * 8, 8)
                padded[pl.ds(at, 8), :] = received(x_pair, which, end_x, i * 32 + part * 8)
        start = jnp.where(low, 0, 36)
        for i in range(4):
            for part in range(4):
                at = pl.multiple_of((start + i) * CY + part * 8, 8)
                wide_x[pl.ds(at, 8), :] = received(x_pair, which, end_x, (HALO + i) * 32 + part * 8)
        low = odd(h) if which == 0 else jnp.logical_not(odd(h))
        start = jnp.where(low, -HALO, CY)
        for c in range(HALO):
            for part in range(4):
                at = (part * 8 + 8) * PAD + start + c + 8
                put_every(padded, at, PAD, received(y_pair, which, end_y, c * 32 + part * 8))
        start = jnp.where(low, 0, 36)
        for c in range(4):
            for part in range(4):
                value = received(y_pair, which, end_y, (HALO + c) * 32 + part * 8)
                put_every(wide_y, part * 8 * WIDE + start + c, WIDE, value)

    def along_x(chunk, carry):
        x0 = chunk * 4 - 4
        for n in range(4):
            taps = [
                padded[pl.ds(pl.multiple_of((x0 + d + 8) * PAD + 8 + n * 8, 8), 8), :]
                for d in range(-3, 8)
            ]
            for i in range(4):
                at = pl.multiple_of((x0 + i + 4) * CY + n * 8, 8)
                grad_x[pl.ds(at, 8), :] = forward(taps, i)
        return carry

    lax.fori_loop(0, 10, along_x, 0)

    def along_y(x, carry):
        taps = [every(padded, (x + 8) * PAD + 4 + d, 5) for d in range(-3, 9)]
        for j in range(5):
            put_every(grad_y, x * WIDE + j, 5, forward(taps, j))
        return carry

    lax.fori_loop(0, CX, along_y, 0)
    for push in pull_all(zip(scratch[:4], outs), out_sem):
        push.wait()


def kick_source(step, cells, amps, field, first=0, end=CX):
    s, g, h = place()
    x = cells[s, 0] - g * CX
    y = cells[s, 1] - h * CY

    @pl.when((x >= first) & (x < end) & (y >= 0) & (y < CY))
    def _():
        at = x * CY + y
        lane = lax.broadcasted_iota(jnp.int32, (1, 128), 1)
        kick = time_step * amps[s, step]
        field[pl.ds(at, 1), :] = field[pl.ds(at, 1), :] + jnp.where(lane == cells[s, 2], kick, 0.0)


def step0_kernel(corners, cells, amps, mat_b, window, *refs):
    sources, outs, scratch = refs[:7], refs[7:17], refs[17:]
    new_p, wide_x, wide_y, new_z, buoy, modu, gy_b, gy_a, gx_b, gx_a = outs
    pres, in_x, in_y, in_z, grad_x, grad_y, grad_z, rho, spread, sem = scratch
    order = (6, 3, 4, 1, 0, 5, 2)
    pulls = pull_all([(sources[i], scratch[i]) for i in order], sem)
    unpack_model(corners, window, buoy, modu, rho)

    def flow_x(x, carry):
        for n in range(4):
            at = pl.multiple_of(x * CY + n * 8, 8)
            wide_x[pl.ds(at, 8), :] = (
                in_x[pl.ds(at, 8), :] - buoy_at(buoy, x - 4, n * 8) * grad_x[pl.ds(at, 8), :]
            )
        return carry

    def flow_y(x, carry):
        for n in range(5):
            at = pl.multiple_of(x * WIDE + n * 8, 8)
            wide_y[pl.ds(at, 8), :] = (
                in_y[pl.ds(at, 8), :] - buoy_at(buoy, x, n * 8 - 4) * grad_y[pl.ds(at, 8), :]
            )
        return carry

    def flow_z(x, carry):
        for n in range(4):
            at = pl.multiple_of(x * CY + n * 8, 8)
            new_z[pl.ds(at, 8), :] = (
                in_z[pl.ds(at, 8), :] - buoy_at(buoy, x, n * 8) * grad_z[pl.ds(at, 8), :]
            )
        return carry

    def wait(*which):
        for i in which:
            pulls[i].wait()

    wait(0, 1)
    lax.fori_loop(0, CX, flow_z, 0, unroll=4)
    for chunk in range(8):
        rows = slice(chunk * 128, (chunk + 1) * 128)
        spread[rows, :] = depth_difference(new_z[rows, :], mat_b)
    wait(2, 3)
    lax.fori_loop(0, WIDE, flow_x, 0, unroll=4)
    wait(4, 5, 6)
    lax.fori_loop(0, CX, flow_y, 0, unroll=4)

    def update(chunk, carry):
        x0 = chunk * 4
        part_x = {}
        for j in range(4):
            taps = [every(wide_x, (x0 + d + 4) * CY + j, 4) for d in range(-4, 7)]
            for i in range(4):
                part_x[i, j] = backward(taps, i)
        for i in range(4):
            taps = [every(wide_y, (x0 + i) * WIDE + 4 + d, 4) for d in range(-4, 7)]
            for j in range(4):
                at = (x0 + i) * CY + j
                total = part_x[i, j] + backward(taps, j) + every(spread, at, 4)
                put_every(new_p, at, 4, every(pres, at, 4) - every(modu, at, 4) * total)
        return carry

    lax.fori_loop(0, 8, update, 0)
    kick_source(0, cells, amps, new_p)
    send_faces(new_p, (gx_a, gx_b), (gy_a, gy_b), 0, HALO)


def inner_kernel(mat_f, mat_b, pres, in_x, in_y, in_z, buoy, wide_x, wide_y, new_z, spread):
    for chunk in range(8):
        rows = slice(chunk * 128, (chunk + 1) * 128)
        grad = depth_difference(pres[rows, :], mat_f)
        light = jnp.concatenate(
            [buoy_at(buoy, x, 0, 32) for x in range(chunk * 4, chunk * 4 + 4)], axis=0
        )
        new_z[rows, :] = in_z[rows, :] - light * grad

    def along_x(chunk, carry):
        x0 = chunk * 4 + 4
        for n in range(4):
            taps = [
                pres[pl.ds(pl.multiple_of((x0 + d) * CY + n * 8, 8), 8), :] for d in range(-3, 8)
            ]
            for i in range(4):
                at = pl.multiple_of((x0 + i + 4) * CY + n * 8, 8)
                wide_x[pl.ds(at, 8), :] = in_x[pl.ds(at, 8), :] - buoy_at(
                    buoy, x0 + i, n * 8
                ) * forward(taps, i)
        return carry

    lax.fori_loop(0, 6, along_x, 0)

    def along_y(x, carry):
        taps = [every(pres, x * CY + 4 + d, 3) for d in range(-3, 7)]
        for j in range(3):
            at = x * WIDE + 8 + j
            light = every(buoy, (x + 4) * WIDE + 8 + j, 3)
            put_every(wide_y, at, 3, every(in_y, at, 3) - light * forward(taps, j))
        return carry

    lax.fori_loop(0, CX, along_y, 0, unroll=4)
    wide_x[0 : 8 * CY, :] = in_x[0 : 8 * CY, :]
    wide_x[32 * CY : 40 * CY, :] = in_x[32 * CY : 40 * CY, :]
    for x in range(CX):
        wide_y[x * WIDE : x * WIDE + 8, :] = in_y[x * WIDE : x * WIDE + 8, :]
        wide_y[x * WIDE + 32 : x * WIDE + 40, :] = in_y[x * WIDE + 32 : x * WIDE + 40, :]
    for chunk in range(8):
        rows = slice(chunk * 128, (chunk + 1) * 128)
        spread[rows, :] = depth_difference(new_z[rows, :], mat_b)

    def across(chunk, carry):
        x0 = chunk * 4 + 8
        for n in range(4):
            taps = [
                wide_x[pl.ds(pl.multiple_of((x0 + d + 4) * CY + n * 8, 8), 8), :]
                for d in range(-4, 7)
            ]
            for i in range(4):
                at = pl.multiple_of((x0 + i) * CY + n * 8, 8)
                spread[pl.ds(at, 8), :] = spread[pl.ds(at, 8), :] + backward(taps, i)
        return carry

    lax.fori_loop(0, 4, across, 0)

    def along(x, carry):
        taps = [every(wide_y, x * WIDE + 12 + d, 2) for d in range(-4, 5)]
        for j in range(2):
            at = x * CY + 8 + j
            put_every(spread, at, 2, every(spread, at, 2) + backward(taps, j))
        return carry

    lax.fori_loop(0, CX, along, 0, unroll=4)


def edge_kernel(step, *refs):
    cells, amps, pres, gy_b, gy_a, gx_b, gx_a, in_x, in_y, buoy, modu, spread = refs[:12]
    last = step == STEPS - 1
    if last:
        p_to, x_to, y_to, low_x, high_x, low_y, high_y, wide_x, wide_y, new_p, out_y, sem = refs[12:]
        pushes = []

        def push(src, dst, rows):
            pushes.append(pltpu.make_async_copy(src, dst.at[rows], sem.at[len(pushes)]))
            pushes[-1].start()

    else:
        new_p, wide_x, wide_y, to_d, to_c, to_b, to_a, low_x, high_x, low_y, high_y = refs[12:]
    wide_x[8 * CY : 32 * CY, :] = in_x[8 * CY : 32 * CY, :]
    for x in range(CX):
        wide_y[x * WIDE + 8 : x * WIDE + 32, :] = in_y[x * WIDE + 8 : x * WIDE + 32, :]
    s, g, h = place()
    end_x = (g == 0) | (g == 3)
    end_y = (h == 0) | (h == 7)
    x_pair, y_pair = (gx_a, gx_b), (gy_a, gy_b)
    low_x[8 * CY : 16 * CY, :] = pres[0 : 8 * CY, :]
    high_x[0 : 8 * CY, :] = pres[24 * CY : 32 * CY, :]
    for x in range(CX):
        low_y[x * STRIP + 8 : x * STRIP + 16, :] = pres[x * CY : x * CY + 8, :]
        high_y[x * STRIP : x * STRIP + 8, :] = pres[x * CY + 24 : x * CY + 32, :]

    def place_x(which, ref, start):
        for i in range(HALO):
            for part in range(4):
                at = (start + i) * CY + part * 8
                ref[at : at + 8, :] = received(x_pair, which, end_x, i * 32 + part * 8)

    def place_y(which, ref, start):
        for c in range(HALO):
            for part in range(4):
                value = received(y_pair, which, end_y, c * 32 + part * 8)
                put_every(ref, part * 8 * STRIP + start + c, STRIP, value)

    for where, put, low, high in ((g, place_x, low_x, high_x), (h, place_y, low_y, high_y)):

        @pl.when(odd(where))
        def _():
            put(0, low, 1)
            put(1, high, 8)

        @pl.when(jnp.logical_not(odd(where)))
        def _():
            put(1, low, 1)
            put(0, high, 8)

    for strip, first in ((low_x, -4), (high_x, 28)):
        for half in range(2):
            for n in range(4):
                taps = [
                    strip[(half * 4 + 4 + d) * CY + n * 8 : (half * 4 + 4 + d) * CY + n * 8 + 8, :]
                    for d in range(-3, 8)
                ]
                for i in range(4):
                    x = first + half * 4 + i
                    at = (x + 4) * CY + n * 8
                    wide_x[at : at + 8, :] = in_x[at : at + 8, :] - buoy_at(
                        buoy, x, n * 8
                    ) * forward(taps, i)

    if last:
        push(wide_x.at[pl.ds(4 * CY, CX * CY)], x_to, pl.ds(0, CX * CY))

    def rows(x0, with_x):
        part_x = {}
        if with_x:
            for n in range(4):
                taps = [
                    wide_x[pl.ds(pl.multiple_of((x0 + d + 4) * CY + n * 8, 8), 8), :]
                    for d in range(-4, 7)
                ]
                for i in range(4):
                    part_x[i, n] = backward(taps, i)
        for i in range(4):
            x = x0 + i
            for strip, col in ((low_y, 0), (high_y, 32)):
                taps = [strip[pl.ds(x * STRIP + 4 + d, 8), :] for d in range(-3, 5)]
                at = pl.multiple_of(x * WIDE + col, 8)
                wide_y[pl.ds(at, 8), :] = in_y[pl.ds(at, 8), :] - buoy_at(
                    buoy, x, col - 4
                ) * forward(taps, 0)
            for n in range(4):
                at = pl.multiple_of(x * CY + n * 8, 8)
                total = spread[pl.ds(at, 8), :]
                if n in (0, 3):
                    taps = [wide_y[pl.ds(x * WIDE + 4 + n * 8 + d, 8), :] for d in range(-4, 4)]
                    total = total + backward(taps, 0)
                if with_x:
                    total = total + part_x[i, n]
                new_p[pl.ds(at, 8), :] = pres[pl.ds(at, 8), :] - modu[pl.ds(at, 8), :] * total

    for first, count, with_x in ((0, 2, True), (8, 4, False), (24, 2, True)):

        def some(chunk, carry):
            rows(first + chunk * 4, with_x)
            return carry

        lax.fori_loop(0, count, some, 0)
        if last:
            kick_source(step, cells, amps, new_p, first, first + count * 4)
            for x in range(first, first + count * 4):
                out_y[x * CY : (x + 1) * CY, :] = wide_y[x * WIDE + 4 : x * WIDE + 36, :]
            part = pl.ds(first * CY, count * 4 * CY)
            push(new_p.at[part], p_to, part)
            push(out_y.at[part], y_to, part)
    if last:
        for copy in pushes:
            copy.wait()
    else:
        kick_source(step, cells, amps, new_p)
        send_faces(new_p, (to_a, to_b), (to_c, to_d), 0, HALO)


def shape(rows, dtype=f32):
    return jax.ShapeDtypeStruct((rows, 128), dtype)


def vmem(rows):
    return pltpu.VMEM((rows, 128), f32)


def call(kernel, outs, args, scratch, name, smem=0, hbm=(), loose=(), to_hbm=(), cost=None):
    spaces = [
        pltpu.SMEM if i < smem else pltpu.HBM if i in hbm else pl.ANY if i in loose else pltpu.VMEM
        for i in range(len(args))
    ]
    to_hbm = range(len(outs)) if to_hbm is True else to_hbm
    outs = [pltpu.HBM(o.shape, o.dtype) if i in to_hbm else o for i, o in enumerate(outs)]
    places = [pltpu.HBM if i in to_hbm else pltpu.VMEM for i in range(len(outs))]
    specs = [pl.BlockSpec(memory_space=space) for space in spaces]
    args = [
        pltpu.with_memory_space_constraint(arg, pltpu.HBM) if i in hbm else arg
        for i, arg in enumerate(args)
    ]
    return pl.pallas_call(
        kernel,
        out_shape=outs,
        in_specs=specs,
        out_specs=[pl.BlockSpec(memory_space=place) for place in places],
        scratch_shapes=scratch,
        cost_estimate=cost,
        compiler_params=pltpu.CompilerParams(vmem_limit_bytes=24 * 1024 * 1024),
        name=name,
    )(*args)


GX, GY = 4, 8


def partners(match):
    out = []
    for g in range(GX):
        for h in range(GY):
            to_g, to_h = match(g, h)
            out.append((g * GY + h, to_g * GY + to_h))
    return out


gx_near = partners(lambda g, h: (g ^ 1, h))
gx_far = partners(lambda g, h: (g, h ^ 1) if g in (0, GX - 1) else (3 - g, h))
gy_near = partners(lambda g, h: (g, h ^ 1))
gy_far = partners(lambda g, h: (g ^ 1, h) if h in (0, GY - 1) else (g, ((h + 1) ^ 1) - 1))


def exchange(faces):
    plane = ("gx", "gy")
    return [
        lax.ppermute(face, plane, pairs)
        for face, pairs in zip(faces, (gy_far, gy_near, gx_far, gx_near))
    ]


def shards(velocity, density, offsets, pressure, vel_x, vel_y, vel_z, source_cells, wavelet):
    mat_f, mat_b = (jnp.asarray(m) for m in depth_matrices())
    vel = velocity.reshape(16 * 64, 128)
    den = density.reshape(16 * 64, 128)
    pres = pressure.reshape(CX * CY, 128)
    flow_x = vel_x.reshape(CX * CY, 128)
    flow_y = vel_y.reshape(CX * CY, 128)
    flow_z = vel_z.reshape(CX * CY, 128)
    block = shape(CX * CY)
    wide = shape(WIDE * CY)
    face = shape(HALO * 32)
    cost = pl.CostEstimate(flops=20_000_000, bytes_accessed=8_000_000, transcendentals=0)
    long = pl.CostEstimate(flops=3 * 10**10, bytes_accessed=8_000_000, transcendentals=0)

    dma = pltpu.SemaphoreType.DMA
    (deal,) = call(
        pack_kernel,
        [shape(128 * 16)],
        [vel, den],
        [vmem(1024)] * 2 + [vmem(2048), dma((8,)), dma((4,))],
        "pack",
        hbm=range(2),
        to_hbm=True,
    )
    dealt = lax.all_to_all(deal.reshape(128, 16, 128), DEVICES, 0, 0, tiled=True)
    faces = call(
        face_kernel,
        [shape((HALO + 4) * 32)] * 4,
        [pres, flow_x, flow_y, deal],
        [vmem(1024)] * 3 + [dma((3,))],
        "first_faces",
        hbm=range(4),
        cost=cost,
    )
    faces = exchange(faces)
    (grad_z,) = call(
        depth_kernel,
        [block],
        [mat_f, pres],
        [vmem(CX * CY), vmem(CX * CY), dma((2,))],
        "step0_depth",
        hbm=(1,),
        to_hbm=True,
        cost=long,
    )
    (cut,) = call(
        cut_kernel,
        [jax.ShapeDtypeStruct((128, MESSAGE // 2, 2, 128), f32)],
        [offsets, dealt.reshape(128 * 16, 128), grad_z],
        [vmem(16 * LINE), vmem(16 * LINE), vmem(128 * MESSAGE), dma((4,))],
        "cut",
        smem=1,
        hbm=(2,),
        to_hbm=True,
    )
    window = lax.all_to_all(cut, DEVICES, 0, 0, tiled=True)
    grad_x, grad_y, flow_x, flow_y = call(
        grad0_kernel,
        [wide, wide, wide, wide],
        [pres, *faces, flow_x, flow_y],
        [vmem(WIDE * CY)] * 4
        + [vmem(PAD * PAD)] + [vmem(CX * CY)] * 3 + [dma((3,)), dma((4,))],
        "step0_gradients",
        hbm=(0, 5, 6),
        to_hbm=True,
        cost=long,
    )
    pres, flow_x, flow_y, flow_z, buoy, modu, *faces = call(
        step0_kernel,
        [block, wide, wide, block, shape(WIDE * WIDE), block] + [face] * 4,
        [offsets, source_cells, wavelet, mat_b, window]
        + [pres, flow_x, flow_y, flow_z, grad_x, grad_y, grad_z],
        [vmem(CX * CY), vmem(WIDE * CY), vmem(WIDE * CY), vmem(CX * CY)]
        + [vmem(WIDE * CY), vmem(WIDE * CY), vmem(CX * CY)]
        + [vmem(WIDE * WIDE), vmem(CX * CY), dma((7,))],
        "step0",
        smem=3,
        hbm=range(5, 12),
    )
    for step in range(1, STEPS):
        last = step == STEPS - 1
        faces = exchange(faces)
        flow_x, flow_y, flow_z, spread = call(
            inner_kernel,
            [wide, wide, block, block],
            [mat_f, mat_b, pres, flow_x, flow_y, flow_z, buoy],
            [],
            f"inner{step}",
            cost=cost,
        )
        pres, flow_x, flow_y, *faces = call(
            functools.partial(edge_kernel, step),
            [block, block, block] if last else [block, wide, wide] + [face] * 4,
            [source_cells, wavelet, pres, *faces, flow_x, flow_y, buoy, modu, spread],
            [vmem(16 * CY), vmem(16 * CY), vmem(CX * STRIP), vmem(CX * STRIP)]
            + ([vmem(WIDE * CY)] * 2 + [vmem(CX * CY)] * 2 + [dma((7,))] if last else []),
            f"edge{step}",
            smem=2,
            to_hbm=last or (),
        )
    return tuple(a.reshape(1, CX, CY, 128) for a in (pres, flow_x, flow_y, flow_z))


def solution(mesh):
    return jax.shard_map(
        shards,
        mesh=mesh,
        in_specs=(
            P(("shot", "gx"), "gy", None),
            P(("shot", "gx"), "gy", None),
            P(),
            P("shot", "gx", "gy", None),
            P("shot", "gx", "gy", None),
            P("shot", "gx", "gy", None),
            P("shot", "gx", "gy", None),
            P(),
            P(),
        ),
        out_specs=(
            P("shot", "gx", "gy", None),
            P("shot", "gx", "gy", None),
            P("shot", "gx", "gy", None),
            P("shot", "gx", "gy", None),
        ),
        check_vma=False,
    )
```

```python
import functools

import jax
import jax.numpy as jnp
import numpy as np
from jax import lax
from jax.experimental import pallas as pl
from jax.experimental.pallas import tpu as pltpu
from jax.sharding import PartitionSpec as P

CX = 32
CY = 32
STEPS = 4
HALO = 7
WIDE = 40
PAD = 48
LINE = 80
MESSAGE = 22
STRIP = 24
DEVICES = ("shot", "gx", "gy")

coefs = (1225.0 / 1024.0, -245.0 / 3072.0, 49.0 / 5120.0, -5.0 / 7168.0)
time_step = 0.09

f32 = jnp.float32
bf16 = jnp.bfloat16


def depth_matrices():
    out = []
    for lead in (0, 1):
        full = np.zeros((128, 128), np.float32)
        for reach in range(1, 5):
            for k in range(128):
                up, down = k + reach - lead, k - reach + 1 - lead
                if up < 128:
                    full[up, k] += np.float32(coefs[reach - 1])
                if down >= 0:
                    full[down, k] -= np.float32(coefs[reach - 1])
        high = full.astype(jnp.bfloat16)
        low = (full - high.astype(np.float32)).astype(jnp.bfloat16)
        out.append(np.concatenate([high, high, low], axis=0))
    return out


def depth_difference(values, mat_ref):
    high = values.astype(bf16)
    low = (values - high.astype(f32)).astype(bf16)
    main = jnp.dot(
        jnp.concatenate([high, low], axis=1), mat_ref[0:256, :], preferred_element_type=f32
    )
    return main + jnp.dot(high, mat_ref[256:384, :], preferred_element_type=f32)


def forward(taps, at):
    total = None
    for reach in range(1, 5):
        term = coefs[reach - 1] * (taps[at + 3 + reach] - taps[at + 4 - reach])
        total = term if total is None else total + term
    return total


def backward(taps, at):
    total = None
    for reach in range(1, 5):
        term = coefs[reach - 1] * (taps[at + 3 + reach] - taps[at + 4 - reach])
        total = term if total is None else total + term
    return total


def every(ref, start, step):
    return ref[pl.ds(start, 8, stride=step), :]


def put_every(ref, start, step, value):
    ref[pl.ds(start, 8, stride=step), :] = value


def place():
    return tuple(lax.axis_index(axis) for axis in DEVICES)


def odd(index):
    return lax.rem(index, 2) == 1


def send_faces(field, x_pair, y_pair, base, rows):
    s, g, h = place()
    for which, ref in enumerate(x_pair):
        low = odd(g) if which == 0 else jnp.logical_not(odd(g))
        start = pl.multiple_of(jnp.where(low, 0, (CX - rows) * CY), 32)
        ref[base * 32 : (base + rows) * 32, :] = field[pl.ds(start, rows * 32), :]
    for which, ref in enumerate(y_pair):
        low = odd(h) if which == 0 else jnp.logical_not(odd(h))
        start = jnp.where(low, 0, CY - rows)
        for c in range(rows):
            for part in range(4):
                at = (base + c) * 32 + part * 8
                ref[at : at + 8, :] = every(field, part * 8 * CY + start + c, CY)


def received(pair, which, end, at):
    value = pair[which][at : at + 8, :]
    return jnp.where(end, 0.0, value) if which == 1 else value


def pull_all(pairs, sem):
    pulls = [pltpu.make_async_copy(src, dst, sem.at[i]) for i, (src, dst) in enumerate(pairs)]
    for pull in pulls:
        pull.start()
    return pulls


def pack_kernel(vel, den, deal, vel_in, den_in, out, in_sem, out_sem):
    pulls = []
    for part in range(4):
        rows = pl.ds(part * 256, 256)
        pulls.append(
            [
                pltpu.make_async_copy(src.at[rows], dst.at[rows], in_sem.at[part * 2 + i])
                for i, (src, dst) in enumerate(((vel, vel_in), (den, den_in)))
            ]
        )
        for pull in pulls[-1]:
            pull.start()
    pushes = []
    for part in range(4):
        for pull in pulls[part]:
            pull.wait()
        for row in range(part * 4, part * 4 + 4):
            for cls in range(8):
                at = (row * 8 + cls) * 16
                out[at : at + 8, :] = every(vel_in, row * 64 + cls, 8)
                out[at + 8 : at + 16, :] = every(den_in, row * 64 + cls, 8)
        rows = pl.ds(part * 512, 512)
        pushes.append(pltpu.make_async_copy(out.at[rows], deal.at[rows], out_sem.at[part]))
        pushes[-1].start()
    for push in pushes:
        push.wait()


def face_kernel(pres, flow_x, flow_y, _, gy_b, gy_a, gx_b, gx_a, pres_in, x_in, y_in, sem):
    pulls = pull_all(((pres, pres_in), (flow_x, x_in), (flow_y, y_in)), sem)
    for pull in pulls:
        pull.wait()
    send_faces(pres_in, (gx_a, gx_b), (gy_a, gy_b), 0, HALO)
    send_faces(x_in, (gx_a, gx_b), (), HALO, 4)
    send_faces(y_in, (), (gy_a, gy_b), HALO, 4)


def cut_kernel(corners, dealt, _, out, rho_lines, vel_lines, cuts, sem):
    s, g, col_class = place()
    row_class = s * 4 + g
    for t in range(16):
        for part in range(8):
            src = (t * 8 + part) * 16
            dst = t * LINE + 8 + part * 8
            vel_lines[dst : dst + 8, :] = dealt[src : src + 8, :]
            rho_lines[dst : dst + 8, :] = dealt[src + 8 : src + 16, :]
    flat = out.reshape(128 * MESSAGE, 128)
    pushes = []
    for shot in range(4):
        col = lax.shift_right_arithmetic(corners[shot, 1] - col_class + 7, 3)
        wide_col = lax.shift_right_arithmetic(corners[shot, 1] - 4 - col_class + 7, 3)

        def block(part, carry):
            corner_x = corners[shot, 0] + part * CX
            row = lax.shift_right_arithmetic(corner_x - row_class + 15, 4)
            low = lax.rem(row_class - corner_x + 4 + 1024, 16) < 4
            rim = jnp.clip(jnp.where(low, row - 1, row + 2), 0, 15)
            base = (shot * 32 + part * 8) * MESSAGE
            line = row * LINE + 8
            rim_line = rim * LINE + 8 + col
            for h in range(8):
                to = base + h * MESSAGE
                for k in range(2):
                    cuts[pl.ds(to + 5 * k, 5), :] = rho_lines[
                        pl.ds(line + wide_col + (k * LINE + 4 * h), 5), :
                    ]
                    cuts[pl.ds(to + 14 + 4 * k, 4), :] = vel_lines[
                        pl.ds(line + col + (k * LINE + 4 * h), 4), :
                    ]
                cuts[pl.ds(to + 10, 4), :] = rho_lines[pl.ds(rim_line + 4 * h, 4), :]
            return carry

        lax.fori_loop(0, 4, block, 0)
        rows = pl.ds(shot * 32 * MESSAGE, 32 * MESSAGE)
        pushes.append(pltpu.make_async_copy(cuts.at[rows], flat.at[rows], sem.at[shot]))
        pushes[-1].start()
    for push in pushes:
        push.wait()


def unpack_model(corners, window, buoy, modu, rho):
    s, g, h = place()
    corner_x = corners[s, 0] + g * CX
    corner_y = corners[s, 1] + h * CY
    wide_turn = lax.rem(8 - lax.rem(corner_y + 4, 8), 8)
    turn = lax.rem(8 - lax.rem(corner_y, 8), 8)
    sub = lax.broadcasted_iota(jnp.int32, (8, 128), 0)
    flat = window.reshape(128 * MESSAGE, 128)
    low_in = (h > 0) | (sub >= 4)
    high_in = (h < 7) | (sub < 4)
    for x in range(-4, CX + 3):
        start = lax.rem(corner_x + 16 + x, 16) * (8 * MESSAGE)
        base = (x + 4) * WIDE
        if 0 <= x < CX:
            for n in range(5):
                got = pltpu.roll(every(flat, start + 5 * (x // 16) + n, MESSAGE), wide_turn, 0)
                rho[base + n * 8 : base + n * 8 + 8, :] = got
                light = time_step * (1.0 / got)
                if n == 0:
                    light = jnp.where(low_in, light, 0.0)
                elif n == 4:
                    light = jnp.where(high_in, light, 0.0)
                buoy[base + n * 8 : base + n * 8 + 8, :] = light
            for n in range(4):
                got = every(flat, start + 14 + 4 * (x // 16) + n, MESSAGE)
                speed = pltpu.roll(got, turn, 0)
                at = x * CY + n * 8
                dens = rho[base + 4 + n * 8 : base + 12 + n * 8, :]
                modu[at : at + 8, :] = time_step * (dens * speed * speed)
        else:
            row_in = (g > 0) if x < 0 else (g < 3)
            for n in range(4):
                got = pltpu.roll(every(flat, start + 10 + n, MESSAGE), turn, 0)
                buoy[base + 4 + n * 8 : base + 12 + n * 8, :] = jnp.where(
                    row_in, time_step * (1.0 / got), 0.0
                )


def buoy_at(buoy, x, y, rows=8):
    return buoy[pl.ds((x + 4) * WIDE + 4 + y, rows), :]


def depth_kernel(mat_f, pres_from, grad_to, pres, grad_z, sem):
    pull = pltpu.make_async_copy(pres_from, pres, sem.at[0])
    pull.start()
    pull.wait()
    for chunk in range(8):
        rows = slice(chunk * 128, (chunk + 1) * 128)
        grad_z[rows, :] = depth_difference(pres[rows, :], mat_f)
    push = pltpu.make_async_copy(grad_z, grad_to, sem.at[1])
    push.start()
    push.wait()


def grad0_kernel(cells, amps, pres_from, gy_b, gy_a, gx_b, gx_a, x_from, y_from, *refs):
    outs, scratch = refs[:5], refs[5:]
    grad_x, grad_y, wide_x, wide_y, pres, padded, in_x, in_y, in_sem, out_sem = scratch
    for pull in pull_all(((pres_from, pres), (x_from, in_x), (y_from, in_y)), in_sem):
        pull.wait()
    s, g, h = place()
    end_x = (g == 0) | (g == 3)
    end_y = (h == 0) | (h == 7)
    for x in range(CX):
        at = (x + 8) * PAD + 8
        padded[at : at + 32, :] = pres[x * CY : (x + 1) * CY, :]
        wide_y[x * WIDE + 4 : x * WIDE + 36, :] = in_y[x * CY : (x + 1) * CY, :]
    wide_x[4 * CY : 36 * CY, :] = in_x[...]
    x_pair, y_pair = (gx_a, gx_b), (gy_a, gy_b)
    for which in range(2):
        low = odd(g) if which == 0 else jnp.logical_not(odd(g))
        start = jnp.where(low, -HALO, CX)
        for i in range(HALO):
            for part in range(4):
                at = pl.multiple_of((start + i + 8) * PAD + 8 + part * 8, 8)
                padded[pl.ds(at, 8), :] = received(x_pair, which, end_x, i * 32 + part * 8)
        start = jnp.where(low, 0, 36)
        for i in range(4):
            for part in range(4):
                at = pl.multiple_of((start + i) * CY + part * 8, 8)
                wide_x[pl.ds(at, 8), :] = received(x_pair, which, end_x, (HALO + i) * 32 + part * 8)
        low = odd(h) if which == 0 else jnp.logical_not(odd(h))
        start = jnp.where(low, -HALO, CY)
        for c in range(HALO):
            for part in range(4):
                at = (part * 8 + 8) * PAD + start + c + 8
                put_every(padded, at, PAD, received(y_pair, which, end_y, c * 32 + part * 8))
        start = jnp.where(low, 0, 36)
        for c in range(4):
            for part in range(4):
                value = received(y_pair, which, end_y, (HALO + c) * 32 + part * 8)
                put_every(wide_y, part * 8 * WIDE + start + c, WIDE, value)

    def along_x(chunk, carry):
        x0 = chunk * 4 - 4
        for n in range(4):
            taps = [
                padded[pl.ds(pl.multiple_of((x0 + d + 8) * PAD + 8 + n * 8, 8), 8), :]
                for d in range(-3, 8)
            ]
            for i in range(4):
                at = pl.multiple_of((x0 + i + 4) * CY + n * 8, 8)
                grad_x[pl.ds(at, 8), :] = forward(taps, i)
        return carry

    lax.fori_loop(0, 10, along_x, 0)

    def along_y(x, carry):
        taps = [every(padded, (x + 8) * PAD + 4 + d, 5) for d in range(-3, 9)]
        for j in range(5):
            put_every(grad_y, x * WIDE + j, 5, forward(taps, j))
        return carry

    lax.fori_loop(0, CX, along_y, 0)
    kick_source(0, cells, amps, pres)
    for push in pull_all(zip(scratch[:5], outs), out_sem):
        push.wait()


def kick_source(step, cells, amps, field):
    s, g, h = place()
    x = cells[s, 0] - g * CX
    y = cells[s, 1] - h * CY

    @pl.when((x >= 0) & (x < CX) & (y >= 0) & (y < CY))
    def _():
        at = x * CY + y
        lane = lax.broadcasted_iota(jnp.int32, (1, 128), 1)
        kick = time_step * amps[s, step]
        field[pl.ds(at, 1), :] = field[pl.ds(at, 1), :] + jnp.where(lane == cells[s, 2], kick, 0.0)


def step0_kernel(corners, mat_b, window, *refs):
    sources, outs, scratch = refs[:7], refs[7:17], refs[17:]
    new_p, wide_x, wide_y, new_z, buoy, modu, gy_b, gy_a, gx_b, gx_a = outs
    pres, in_x, in_y, in_z, grad_x, grad_y, grad_z, rho, spread, sem = scratch
    order = (6, 3, 4, 1, 0, 5, 2)
    pulls = pull_all([(sources[i], scratch[i]) for i in order], sem)
    unpack_model(corners, window, buoy, modu, rho)

    def wait(*which):
        for i in which:
            pulls[i].wait()

    def tiles(count, per):
        return [(x, n, (x * per + n) * 8) for x in range(count) for n in range(per)]

    wait(0, 1)
    for x, n, at in tiles(CX, 4):
        new_z[at : at + 8, :] = in_z[at : at + 8, :] - buoy_at(buoy, x, n * 8) * grad_z[at : at + 8, :]
    for chunk in range(8):
        rows = slice(chunk * 128, (chunk + 1) * 128)
        spread[rows, :] = depth_difference(new_z[rows, :], mat_b)
    wait(2, 3)
    for x, n, at in tiles(WIDE, 4):
        wide_x[at : at + 8, :] = (
            in_x[at : at + 8, :] - buoy_at(buoy, x - 4, n * 8) * grad_x[at : at + 8, :]
        )
    wait(4, 5, 6)
    for x, n, at in tiles(CX, 5):
        wide_y[at : at + 8, :] = (
            in_y[at : at + 8, :] - buoy_at(buoy, x, n * 8 - 4) * grad_y[at : at + 8, :]
        )
    for x0 in range(0, CX, 4):
        part_x = {}
        for j in range(4):
            taps = [every(wide_x, (x0 + d + 4) * CY + j, 4) for d in range(-4, 7)]
            for i in range(4):
                part_x[i, j] = backward(taps, i)
        for i in range(4):
            taps = [every(wide_y, (x0 + i) * WIDE + 4 + d, 4) for d in range(-4, 7)]
            for j in range(4):
                at = (x0 + i) * CY + j
                total = part_x[i, j] + backward(taps, j) + every(spread, at, 4)
                put_every(new_p, at, 4, every(pres, at, 4) - every(modu, at, 4) * total)
    send_faces(new_p, (gx_a, gx_b), (gy_a, gy_b), 0, HALO)


def inner_kernel(step, cells, amps, mat_f, mat_b, pres, in_x, in_y, in_z, buoy, *outs):
    wide_x, wide_y, new_z, spread, kicked = outs
    kicked[...] = pres[...]
    kick_source(step, cells, amps, kicked)
    for chunk in range(8):
        rows = slice(chunk * 128, (chunk + 1) * 128)
        grad = depth_difference(pres[rows, :], mat_f)
        light = jnp.concatenate(
            [buoy_at(buoy, x, 0, 32) for x in range(chunk * 4, chunk * 4 + 4)], axis=0
        )
        new_z[rows, :] = in_z[rows, :] - light * grad

    def along_x(chunk, carry):
        x0 = chunk * 4 + 4
        for n in range(4):
            taps = [
                pres[pl.ds(pl.multiple_of((x0 + d) * CY + n * 8, 8), 8), :] for d in range(-3, 8)
            ]
            for i in range(4):
                at = pl.multiple_of((x0 + i + 4) * CY + n * 8, 8)
                wide_x[pl.ds(at, 8), :] = in_x[pl.ds(at, 8), :] - buoy_at(
                    buoy, x0 + i, n * 8
                ) * forward(taps, i)
        return carry

    lax.fori_loop(0, 6, along_x, 0)

    def along_y(x, carry):
        taps = [every(pres, x * CY + 4 + d, 3) for d in range(-3, 7)]
        for j in range(3):
            at = x * WIDE + 8 + j
            light = every(buoy, (x + 4) * WIDE + 8 + j, 3)
            put_every(wide_y, at, 3, every(in_y, at, 3) - light * forward(taps, j))
        return carry

    lax.fori_loop(0, CX, along_y, 0, unroll=4)
    wide_x[0 : 8 * CY, :] = in_x[0 : 8 * CY, :]
    wide_x[32 * CY : 40 * CY, :] = in_x[32 * CY : 40 * CY, :]
    for x in range(CX):
        wide_y[x * WIDE : x * WIDE + 8, :] = in_y[x * WIDE : x * WIDE + 8, :]
        wide_y[x * WIDE + 32 : x * WIDE + 40, :] = in_y[x * WIDE + 32 : x * WIDE + 40, :]
    for chunk in range(8):
        rows = slice(chunk * 128, (chunk + 1) * 128)
        spread[rows, :] = depth_difference(new_z[rows, :], mat_b)

    def across(chunk, carry):
        x0 = chunk * 4 + 8
        for n in range(4):
            taps = [
                wide_x[pl.ds(pl.multiple_of((x0 + d + 4) * CY + n * 8, 8), 8), :]
                for d in range(-4, 7)
            ]
            for i in range(4):
                at = pl.multiple_of((x0 + i) * CY + n * 8, 8)
                spread[pl.ds(at, 8), :] = spread[pl.ds(at, 8), :] + backward(taps, i)
        return carry

    lax.fori_loop(0, 4, across, 0)

    def along(x, carry):
        taps = [every(wide_y, x * WIDE + 12 + d, 2) for d in range(-4, 5)]
        for j in range(2):
            at = x * CY + 8 + j
            put_every(spread, at, 2, every(spread, at, 2) + backward(taps, j))
        return carry

    lax.fori_loop(0, CX, along, 0, unroll=4)


def edge_kernel(step, *refs):
    pres, gy_b, gy_a, gx_b, gx_a, in_x, in_y, buoy, modu, spread, kicked = refs[:11]
    last = step == STEPS - 1
    if last:
        p_to, x_to, y_to, rim_x, rim_y, wide_x, wide_y, new_p, out_y, sem = refs[11:]
        pushes = []

        def push(src, dst, rows):
            pushes.append(pltpu.make_async_copy(src, dst.at[rows], sem.at[len(pushes)]))
            pushes[-1].start()

    else:
        new_p, wide_x, wide_y, to_d, to_c, to_b, to_a, rim_x, rim_y = refs[11:]
    s, g, h = place()
    end_x = (g == 0) | (g == 3)
    end_y = (h == 0) | (h == 7)
    for which in range(2):
        low = odd(g) if which == 0 else jnp.logical_not(odd(g))
        start = jnp.where(low, 1, 24) * CY
        for i in range(HALO):
            for part in range(4):
                at = pl.multiple_of(start + (i * CY + part * 8), 8)
                rim_x[pl.ds(at, 8), :] = received((gx_a, gx_b), which, end_x, i * 32 + part * 8)
        low = odd(h) if which == 0 else jnp.logical_not(odd(h))
        start = jnp.where(low, 1, CX * STRIP + 8)
        for c in range(HALO):
            for part in range(4):
                value = received((gy_a, gy_b), which, end_y, c * 32 + part * 8)
                put_every(rim_y, start + (part * 8 * STRIP + c), STRIP, value)
    rim_x[8 * CY : 24 * CY, :] = jnp.concatenate([pres[0 : 8 * CY, :], pres[24 * CY : 32 * CY, :]], axis=0)
    for x in range(CX):
        rim_y[x * STRIP + 8 : x * STRIP + 16, :] = pres[x * CY : x * CY + 8, :]
        at = (CX + x) * STRIP
        rim_y[at : at + 8, :] = pres[x * CY + 24 : x * CY + 32, :]
    wide_x[8 * CY : 32 * CY, :] = in_x[8 * CY : 32 * CY, :]
    for x in range(CX):
        wide_y[x * WIDE + 8 : x * WIDE + 32, :] = in_y[x * WIDE + 8 : x * WIDE + 32, :]
    for rim, first in ((0, -4), (16, 28)):
        for half in range(2):
            for n in range(4):
                mid = (rim + half * 4 + 4) * CY + n * 8
                taps = [rim_x[mid + d * CY : mid + d * CY + 8, :] for d in range(-3, 8)]
                for i in range(4):
                    x = first + half * 4 + i
                    at = (x + 4) * CY + n * 8
                    wide_x[at : at + 8, :] = in_x[at : at + 8, :] - buoy_at(
                        buoy, x, n * 8
                    ) * forward(taps, i)

    if last:
        push(wide_x.at[pl.ds(4 * CY, CX * CY)], x_to, pl.ds(0, CX * CY))
    for x in range(CX):
        for rim, col in ((0, 0), (CX, 32)):
            mid = (rim + x) * STRIP + 4
            taps = [rim_y[mid + d : mid + d + 8, :] for d in range(-3, 5)]
            at = x * WIDE + col
            wide_y[at : at + 8, :] = in_y[at : at + 8, :] - buoy_at(buoy, x, col - 4) * forward(taps, 0)

    for first, count in ((0, 2), (8, 4), (24, 2)):
        for x0 in range(first, first + count * 4, 4):
            part_x = {}
            if count == 2:
                for n in range(4):
                    taps = [
                        wide_x[(x0 + d + 4) * CY + n * 8 : (x0 + d + 4) * CY + n * 8 + 8, :]
                        for d in range(-4, 7)
                    ]
                    for i in range(4):
                        part_x[i, n] = backward(taps, i)
            for i in range(4):
                for n in range(4):
                    at = (x0 + i) * CY + n * 8
                    total = spread[at : at + 8, :]
                    if n in (0, 3):
                        mid = (x0 + i) * WIDE + 4 + n * 8
                        taps = [wide_y[mid + d : mid + d + 8, :] for d in range(-4, 4)]
                        total = total + backward(taps, 0)
                    if count == 2:
                        total = total + part_x[i, n]
                    new_p[at : at + 8, :] = kicked[at : at + 8, :] - modu[at : at + 8, :] * total
        if last:
            for x in range(first, first + count * 4):
                out_y[x * CY : (x + 1) * CY, :] = wide_y[x * WIDE + 4 : x * WIDE + 36, :]
            part = pl.ds(first * CY, count * 4 * CY)
            push(new_p.at[part], p_to, part)
            push(out_y.at[part], y_to, part)
    if last:
        for copy in pushes:
            copy.wait()
    else:
        send_faces(new_p, (to_a, to_b), (to_c, to_d), 0, HALO)


def shape(rows, dtype=f32):
    return jax.ShapeDtypeStruct((rows, 128), dtype)


def vmem(rows):
    return pltpu.VMEM((rows, 128), f32)


def call(kernel, outs, args, scratch, name, smem=0, hbm=(), loose=(), to_hbm=(), cost=None):
    spaces = [
        pltpu.SMEM if i < smem else pltpu.HBM if i in hbm else pl.ANY if i in loose else pltpu.VMEM
        for i in range(len(args))
    ]
    to_hbm = range(len(outs)) if to_hbm is True else to_hbm
    outs = [pltpu.HBM(o.shape, o.dtype) if i in to_hbm else o for i, o in enumerate(outs)]
    places = [pltpu.HBM if i in to_hbm else pltpu.VMEM for i in range(len(outs))]
    specs = [pl.BlockSpec(memory_space=space) for space in spaces]
    args = [
        pltpu.with_memory_space_constraint(arg, pltpu.HBM) if i in hbm else arg
        for i, arg in enumerate(args)
    ]
    return pl.pallas_call(
        kernel,
        out_shape=outs,
        in_specs=specs,
        out_specs=[pl.BlockSpec(memory_space=place) for place in places],
        scratch_shapes=scratch,
        cost_estimate=cost,
        compiler_params=pltpu.CompilerParams(vmem_limit_bytes=24 * 1024 * 1024),
        name=name,
    )(*args)


GX, GY = 4, 8


def partners(match):
    out = []
    for g in range(GX):
        for h in range(GY):
            to_g, to_h = match(g, h)
            out.append((g * GY + h, to_g * GY + to_h))
    return out


gx_near = partners(lambda g, h: (g ^ 1, h))
gx_far = partners(lambda g, h: (g, h ^ 1) if g in (0, GX - 1) else (3 - g, h))
gy_near = partners(lambda g, h: (g, h ^ 1))
gy_far = partners(lambda g, h: (g ^ 1, h) if h in (0, GY - 1) else (g, ((h + 1) ^ 1) - 1))


def exchange(faces):
    plane = ("gx", "gy")
    return [
        lax.ppermute(face, plane, pairs)
        for face, pairs in zip(faces, (gy_far, gy_near, gx_far, gx_near))
    ]


def shards(velocity, density, offsets, pressure, vel_x, vel_y, vel_z, source_cells, wavelet):
    mat_f, mat_b = (jnp.asarray(m) for m in depth_matrices())
    vel = velocity.reshape(16 * 64, 128)
    den = density.reshape(16 * 64, 128)
    pres = pressure.reshape(CX * CY, 128)
    flow_x = vel_x.reshape(CX * CY, 128)
    flow_y = vel_y.reshape(CX * CY, 128)
    flow_z = vel_z.reshape(CX * CY, 128)
    block = shape(CX * CY)
    wide = shape(WIDE * CY)
    face = shape(HALO * 32)
    cost = pl.CostEstimate(flops=20_000_000, bytes_accessed=8_000_000, transcendentals=0)
    long = pl.CostEstimate(flops=3 * 10**10, bytes_accessed=8_000_000, transcendentals=0)

    dma = pltpu.SemaphoreType.DMA
    (deal,) = call(
        pack_kernel,
        [shape(128 * 16)],
        [vel, den],
        [vmem(1024)] * 2 + [vmem(2048), dma((8,)), dma((4,))],
        "pack",
        hbm=range(2),
        to_hbm=True,
    )
    dealt = lax.all_to_all(deal.reshape(128, 16, 128), DEVICES, 0, 0, tiled=True)
    faces = call(
        face_kernel,
        [shape((HALO + 4) * 32)] * 4,
        [pres, flow_x, flow_y, deal],
        [vmem(1024)] * 3 + [dma((3,))],
        "first_faces",
        hbm=range(4),
        cost=cost,
    )
    faces = exchange(faces)
    (grad_z,) = call(
        depth_kernel,
        [block],
        [mat_f, pres],
        [vmem(CX * CY), vmem(CX * CY), dma((2,))],
        "step0_depth",
        hbm=(1,),
        to_hbm=True,
        cost=long,
    )
    (cut,) = call(
        cut_kernel,
        [jax.ShapeDtypeStruct((128, MESSAGE // 2, 2, 128), f32)],
        [offsets, dealt.reshape(128 * 16, 128), grad_z],
        [vmem(16 * LINE), vmem(16 * LINE), vmem(128 * MESSAGE), dma((4,))],
        "cut",
        smem=1,
        hbm=(2,),
        to_hbm=True,
    )
    window = lax.all_to_all(cut, DEVICES, 0, 0, tiled=True)
    grad_x, grad_y, flow_x, flow_y, pres = call(
        grad0_kernel,
        [wide, wide, wide, wide, block],
        [source_cells, wavelet, pres, *faces, flow_x, flow_y],
        [vmem(WIDE * CY)] * 4 + [vmem(CX * CY)]
        + [vmem(PAD * PAD)] + [vmem(CX * CY)] * 2 + [dma((3,)), dma((5,))],
        "step0_gradients",
        smem=2,
        hbm=(2, 7, 8),
        to_hbm=True,
        cost=long,
    )
    pres, flow_x, flow_y, flow_z, buoy, modu, *faces = call(
        step0_kernel,
        [block, wide, wide, block, shape(WIDE * WIDE), block] + [face] * 4,
        [offsets, mat_b, window]
        + [pres, flow_x, flow_y, flow_z, grad_x, grad_y, grad_z],
        [vmem(CX * CY), vmem(WIDE * CY), vmem(WIDE * CY), vmem(CX * CY)]
        + [vmem(WIDE * CY), vmem(WIDE * CY), vmem(CX * CY)]
        + [vmem(WIDE * WIDE), vmem(CX * CY), dma((7,))],
        "step0",
        smem=1,
        hbm=range(3, 10),
    )
    for step in range(1, STEPS):
        last = step == STEPS - 1
        faces = exchange(faces)
        flow_x, flow_y, flow_z, spread, kicked = call(
            functools.partial(inner_kernel, step),
            [wide, wide, block, block, block],
            [source_cells, wavelet, mat_f, mat_b, pres, flow_x, flow_y, flow_z, buoy],
            [],
            f"inner{step}",
            smem=2,
            cost=cost,
        )
        pres, flow_x, flow_y, *faces = call(
            functools.partial(edge_kernel, step),
            [block, block, block] if last else [block, wide, wide] + [face] * 4,
            [pres, *faces, flow_x, flow_y, buoy, modu, spread, kicked],
            [vmem(32 * CY), vmem(2 * CX * STRIP)]
            + ([vmem(WIDE * CY)] * 2 + [vmem(CX * CY)] * 2 + [dma((7,))] if last else []),
            f"edge{step}",
            to_hbm=last or (),
        )
    return tuple(a.reshape(1, CX, CY, 128) for a in (pres, flow_x, flow_y, flow_z))


def solution(mesh):
    return jax.shard_map(
        shards,
        mesh=mesh,
        in_specs=(
            P(("shot", "gx"), "gy", None),
            P(("shot", "gx"), "gy", None),
            P(),
            P("shot", "gx", "gy", None),
            P("shot", "gx", "gy", None),
            P("shot", "gx", "gy", None),
            P("shot", "gx", "gy", None),
            P(),
            P(),
        ),
        out_specs=(
            P("shot", "gx", "gy", None),
            P("shot", "gx", "gy", None),
            P("shot", "gx", "gy", None),
            P("shot", "gx", "gy", None),
        ),
        check_vma=False,
    )
```

```python
import functools

import jax
import jax.numpy as jnp
import numpy as np
from jax import lax
from jax.experimental import pallas as pl
from jax.experimental.pallas import tpu as pltpu
from jax.sharding import PartitionSpec as P

CX = 32
CY = 32
STEPS = 4
HALO = 7
WIDE = 40
PAD = 48
LINE = 80
MESSAGE = 22
STRIP = 24
DEVICES = ("shot", "gx", "gy")

coefs = (1225.0 / 1024.0, -245.0 / 3072.0, 49.0 / 5120.0, -5.0 / 7168.0)
time_step = 0.09

f32 = jnp.float32
bf16 = jnp.bfloat16


def depth_matrices():
    out = []
    for lead in (0, 1):
        full = np.zeros((128, 128), np.float32)
        for reach in range(1, 5):
            for k in range(128):
                up, down = k + reach - lead, k - reach + 1 - lead
                if up < 128:
                    full[up, k] += np.float32(coefs[reach - 1])
                if down >= 0:
                    full[down, k] -= np.float32(coefs[reach - 1])
        high = full.astype(jnp.bfloat16)
        low = (full - high.astype(np.float32)).astype(jnp.bfloat16)
        out.append(np.concatenate([high, high, low], axis=0))
    return out


def depth_difference(values, mat_ref):
    high = values.astype(bf16)
    low = (values - high.astype(f32)).astype(bf16)
    main = jnp.dot(
        jnp.concatenate([high, low], axis=1), mat_ref[0:256, :], preferred_element_type=f32
    )
    return main + jnp.dot(high, mat_ref[256:384, :], preferred_element_type=f32)


def forward(taps, at):
    total = None
    for reach in range(1, 5):
        term = coefs[reach - 1] * (taps[at + 3 + reach] - taps[at + 4 - reach])
        total = term if total is None else total + term
    return total


def backward(taps, at):
    total = None
    for reach in range(1, 5):
        term = coefs[reach - 1] * (taps[at + 3 + reach] - taps[at + 4 - reach])
        total = term if total is None else total + term
    return total


def every(ref, start, step):
    return ref[pl.ds(start, 8, stride=step), :]


def put_every(ref, start, step, value):
    ref[pl.ds(start, 8, stride=step), :] = value


def place():
    return tuple(lax.axis_index(axis) for axis in DEVICES)


def odd(index):
    return lax.rem(index, 2) == 1


def send_faces(field, x_pair, y_pair, base, rows):
    s, g, h = place()
    for which, ref in enumerate(x_pair):
        low = odd(g) if which == 0 else jnp.logical_not(odd(g))
        start = pl.multiple_of(jnp.where(low, 0, (CX - rows) * CY), 32)
        ref[base * 32 : (base + rows) * 32, :] = field[pl.ds(start, rows * 32), :]
    for which, ref in enumerate(y_pair):
        low = odd(h) if which == 0 else jnp.logical_not(odd(h))
        start = jnp.where(low, 0, CY - rows)
        for c in range(rows):
            for part in range(4):
                at = (base + c) * 32 + part * 8
                ref[at : at + 8, :] = every(field, part * 8 * CY + start + c, CY)


def received(pair, which, end, at):
    value = pair[which][at : at + 8, :]
    return jnp.where(end, 0.0, value) if which == 1 else value


def pull_all(pairs, sem):
    pulls = [pltpu.make_async_copy(src, dst, sem.at[i]) for i, (src, dst) in enumerate(pairs)]
    for pull in pulls:
        pull.start()
    return pulls


def pack_kernel(vel, den, deal, vel_in, den_in, out, in_sem, out_sem):
    pulls = []
    for part in range(4):
        rows = pl.ds(part * 256, 256)
        pulls.append(
            [
                pltpu.make_async_copy(src.at[rows], dst.at[rows], in_sem.at[part * 2 + i])
                for i, (src, dst) in enumerate(((vel, vel_in), (den, den_in)))
            ]
        )
        for pull in pulls[-1]:
            pull.start()
    pushes = []
    for part in range(4):
        for pull in pulls[part]:
            pull.wait()
        for row in range(part * 4, part * 4 + 4):
            for cls in range(8):
                at = (row * 8 + cls) * 16
                out[at : at + 8, :] = every(vel_in, row * 64 + cls, 8)
                out[at + 8 : at + 16, :] = every(den_in, row * 64 + cls, 8)
        rows = pl.ds(part * 512, 512)
        pushes.append(pltpu.make_async_copy(out.at[rows], deal.at[rows], out_sem.at[part]))
        pushes[-1].start()
    for push in pushes:
        push.wait()


def face_kernel(pres, flow_x, flow_y, _, gy_b, gy_a, gx_b, gx_a, pres_in, x_in, y_in, sem):
    pulls = pull_all(((pres, pres_in), (flow_x, x_in), (flow_y, y_in)), sem)
    for pull in pulls:
        pull.wait()
    send_faces(pres_in, (gx_a, gx_b), (gy_a, gy_b), 0, HALO)
    send_faces(x_in, (gx_a, gx_b), (), HALO, 4)
    send_faces(y_in, (), (gy_a, gy_b), HALO, 4)


def cut_kernel(dealt, corners_from, _, out, rho_lines, vel_lines, cuts, sem, corners, corner_sem):
    pull = pltpu.make_async_copy(corners_from, corners, corner_sem.at[0])
    pull.start()
    s, g, col_class = place()
    row_class = s * 4 + g
    for t in range(16):
        for part in range(8):
            src = (t * 8 + part) * 16
            dst = t * LINE + 8 + part * 8
            vel_lines[dst : dst + 8, :] = dealt[src : src + 8, :]
            rho_lines[dst : dst + 8, :] = dealt[src + 8 : src + 16, :]
    flat = out.reshape(128 * MESSAGE, 128)
    pull.wait()
    pushes = []
    for shot in range(4):
        col = lax.shift_right_arithmetic(corners[shot, 1] - col_class + 7, 3)
        wide_col = lax.shift_right_arithmetic(corners[shot, 1] - 4 - col_class + 7, 3)

        def block(part, carry):
            corner_x = corners[shot, 0] + part * CX
            row = lax.shift_right_arithmetic(corner_x - row_class + 15, 4)
            low = lax.rem(row_class - corner_x + 4 + 1024, 16) < 4
            rim = jnp.clip(jnp.where(low, row - 1, row + 2), 0, 15)
            base = (shot * 32 + part * 8) * MESSAGE
            line = row * LINE + 8
            rim_line = rim * LINE + 8 + col
            for h in range(8):
                to = base + h * MESSAGE
                for k in range(2):
                    cuts[pl.ds(to + 5 * k, 5), :] = rho_lines[
                        pl.ds(line + wide_col + (k * LINE + 4 * h), 5), :
                    ]
                    cuts[pl.ds(to + 14 + 4 * k, 4), :] = vel_lines[
                        pl.ds(line + col + (k * LINE + 4 * h), 4), :
                    ]
                cuts[pl.ds(to + 10, 4), :] = rho_lines[pl.ds(rim_line + 4 * h, 4), :]
            return carry

        lax.fori_loop(0, 4, block, 0)
        rows = pl.ds(shot * 32 * MESSAGE, 32 * MESSAGE)
        pushes.append(pltpu.make_async_copy(cuts.at[rows], flat.at[rows], sem.at[shot]))
        pushes[-1].start()
    for push in pushes:
        push.wait()


def unpack_model(corners, window, buoy, modu, rho):
    s, g, h = place()
    corner_x = corners[s, 0] + g * CX
    corner_y = corners[s, 1] + h * CY
    wide_turn = lax.rem(8 - lax.rem(corner_y + 4, 8), 8)
    turn = lax.rem(8 - lax.rem(corner_y, 8), 8)
    sub = lax.broadcasted_iota(jnp.int32, (8, 128), 0)
    flat = window.reshape(128 * MESSAGE, 128)
    low_in = (h > 0) | (sub >= 4)
    high_in = (h < 7) | (sub < 4)
    for x in range(-4, CX + 3):
        start = lax.rem(corner_x + 16 + x, 16) * (8 * MESSAGE)
        base = (x + 4) * WIDE
        if 0 <= x < CX:
            for n in range(5):
                got = pltpu.roll(every(flat, start + 5 * (x // 16) + n, MESSAGE), wide_turn, 0)
                rho[base + n * 8 : base + n * 8 + 8, :] = got
                light = time_step * (1.0 / got)
                if n == 0:
                    light = jnp.where(low_in, light, 0.0)
                elif n == 4:
                    light = jnp.where(high_in, light, 0.0)
                buoy[base + n * 8 : base + n * 8 + 8, :] = light
            for n in range(4):
                got = every(flat, start + 14 + 4 * (x // 16) + n, MESSAGE)
                speed = pltpu.roll(got, turn, 0)
                at = x * CY + n * 8
                dens = rho[base + 4 + n * 8 : base + 12 + n * 8, :]
                modu[at : at + 8, :] = time_step * (dens * speed * speed)
        else:
            row_in = (g > 0) if x < 0 else (g < 3)
            for n in range(4):
                got = pltpu.roll(every(flat, start + 10 + n, MESSAGE), turn, 0)
                buoy[base + 4 + n * 8 : base + 12 + n * 8, :] = jnp.where(
                    row_in, time_step * (1.0 / got), 0.0
                )


def buoy_at(buoy, x, y, rows=8):
    return buoy[pl.ds((x + 4) * WIDE + 4 + y, rows), :]


def depth_kernel(mat_f, pres_from, grad_to, pres, grad_z, sem):
    pull = pltpu.make_async_copy(pres_from, pres, sem.at[0])
    pull.start()
    pull.wait()
    for chunk in range(8):
        rows = slice(chunk * 128, (chunk + 1) * 128)
        grad_z[rows, :] = depth_difference(pres[rows, :], mat_f)
    push = pltpu.make_async_copy(grad_z, grad_to, sem.at[1])
    push.start()
    push.wait()


def grad0_kernel(cells, amps, pres_from, gy_b, gy_a, gx_b, gx_a, x_from, y_from, *refs):
    outs, scratch = refs[:5], refs[5:]
    grad_x, grad_y, wide_x, wide_y, pres, padded, in_x, in_y, in_sem, out_sem = scratch
    for pull in pull_all(((pres_from, pres), (x_from, in_x), (y_from, in_y)), in_sem):
        pull.wait()
    s, g, h = place()
    end_x = (g == 0) | (g == 3)
    end_y = (h == 0) | (h == 7)
    for x in range(CX):
        at = (x + 8) * PAD + 8
        padded[at : at + 32, :] = pres[x * CY : (x + 1) * CY, :]
        wide_y[x * WIDE + 4 : x * WIDE + 36, :] = in_y[x * CY : (x + 1) * CY, :]
    wide_x[4 * CY : 36 * CY, :] = in_x[...]
    x_pair, y_pair = (gx_a, gx_b), (gy_a, gy_b)
    for which in range(2):
        low = odd(g) if which == 0 else jnp.logical_not(odd(g))
        start = jnp.where(low, -HALO, CX)
        for i in range(HALO):
            for part in range(4):
                at = pl.multiple_of((start + i + 8) * PAD + 8 + part * 8, 8)
                padded[pl.ds(at, 8), :] = received(x_pair, which, end_x, i * 32 + part * 8)
        start = jnp.where(low, 0, 36)
        for i in range(4):
            for part in range(4):
                at = pl.multiple_of((start + i) * CY + part * 8, 8)
                wide_x[pl.ds(at, 8), :] = received(x_pair, which, end_x, (HALO + i) * 32 + part * 8)
        low = odd(h) if which == 0 else jnp.logical_not(odd(h))
        start = jnp.where(low, -HALO, CY)
        for c in range(HALO):
            for part in range(4):
                at = (part * 8 + 8) * PAD + start + c + 8
                put_every(padded, at, PAD, received(y_pair, which, end_y, c * 32 + part * 8))
        start = jnp.where(low, 0, 36)
        for c in range(4):
            for part in range(4):
                value = received(y_pair, which, end_y, (HALO + c) * 32 + part * 8)
                put_every(wide_y, part * 8 * WIDE + start + c, WIDE, value)

    def along_x(chunk, carry):
        x0 = chunk * 4 - 4
        for n in range(4):
            taps = [
                padded[pl.ds(pl.multiple_of((x0 + d + 8) * PAD + 8 + n * 8, 8), 8), :]
                for d in range(-3, 8)
            ]
            for i in range(4):
                at = pl.multiple_of((x0 + i + 4) * CY + n * 8, 8)
                grad_x[pl.ds(at, 8), :] = forward(taps, i)
        return carry

    lax.fori_loop(0, 10, along_x, 0)

    def along_y(x, carry):
        taps = [every(padded, (x + 8) * PAD + 4 + d, 5) for d in range(-3, 9)]
        for j in range(5):
            put_every(grad_y, x * WIDE + j, 5, forward(taps, j))
        return carry

    lax.fori_loop(0, CX, along_y, 0)
    kick_source(0, cells, amps, pres)
    for push in pull_all(zip(scratch[:5], outs), out_sem):
        push.wait()


def kick_source(step, cells, amps, field):
    s, g, h = place()
    x = cells[s, 0] - g * CX
    y = cells[s, 1] - h * CY

    @pl.when((x >= 0) & (x < CX) & (y >= 0) & (y < CY))
    def _():
        at = x * CY + y
        lane = lax.broadcasted_iota(jnp.int32, (1, 128), 1)
        kick = time_step * amps[s, step]
        field[pl.ds(at, 1), :] = field[pl.ds(at, 1), :] + jnp.where(lane == cells[s, 2], kick, 0.0)


def step0_kernel(corners_from, mat_b, window, *refs):
    sources, outs, scratch = refs[:7], refs[7:17], refs[17:]
    new_p, wide_x, wide_y, new_z, buoy, modu, gy_b, gy_a, gx_b, gx_a = outs
    pres, in_x, in_y, in_z, grad_x, grad_y, grad_z, rho, spread, sem, corners, corner_sem = scratch
    pull = pltpu.make_async_copy(corners_from, corners, corner_sem.at[0])
    pull.start()
    order = (6, 3, 4, 1, 0, 5, 2)
    pulls = pull_all([(sources[i], scratch[i]) for i in order], sem)
    pull.wait()
    unpack_model(corners, window, buoy, modu, rho)

    def wait(*which):
        for i in which:
            pulls[i].wait()

    def tiles(count, per):
        return [(x, n, (x * per + n) * 8) for x in range(count) for n in range(per)]

    wait(0, 1)
    for x, n, at in tiles(CX, 4):
        new_z[at : at + 8, :] = in_z[at : at + 8, :] - buoy_at(buoy, x, n * 8) * grad_z[at : at + 8, :]
    for chunk in range(8):
        rows = slice(chunk * 128, (chunk + 1) * 128)
        spread[rows, :] = depth_difference(new_z[rows, :], mat_b)
    wait(2, 3)
    for x, n, at in tiles(WIDE, 4):
        wide_x[at : at + 8, :] = (
            in_x[at : at + 8, :] - buoy_at(buoy, x - 4, n * 8) * grad_x[at : at + 8, :]
        )
    for x0 in range(0, CX, 4):
        for n in range(4):
            mid = (x0 + 4) * CY + n * 8
            taps = [wide_x[mid + d * CY : mid + d * CY + 8, :] for d in range(-4, 7)]
            for i in range(4):
                at = (x0 + i) * CY + n * 8
                spread[at : at + 8, :] = spread[at : at + 8, :] + backward(taps, i)
    wait(4, 5, 6)
    for x, n, at in tiles(CX, 5):
        wide_y[at : at + 8, :] = (
            in_y[at : at + 8, :] - buoy_at(buoy, x, n * 8 - 4) * grad_y[at : at + 8, :]
        )
    for x in range(CX):
        taps = [every(wide_y, x * WIDE + 4 + d, 4) for d in range(-4, 7)]
        for j in range(4):
            at = x * CY + j
            total = every(spread, at, 4) + backward(taps, j)
            put_every(new_p, at, 4, every(pres, at, 4) - every(modu, at, 4) * total)
    send_faces(new_p, (gx_a, gx_b), (gy_a, gy_b), 0, HALO)


def inner_kernel(step, cells, amps, mat_f, mat_b, pres, in_x, in_y, in_z, buoy, *outs):
    wide_x, wide_y, new_z, spread, kicked = outs
    kicked[...] = pres[...]
    kick_source(step, cells, amps, kicked)
    for chunk in range(8):
        rows = slice(chunk * 128, (chunk + 1) * 128)
        grad = depth_difference(pres[rows, :], mat_f)
        light = jnp.concatenate(
            [buoy_at(buoy, x, 0, 32) for x in range(chunk * 4, chunk * 4 + 4)], axis=0
        )
        new_z[rows, :] = in_z[rows, :] - light * grad

    def along_x(chunk, carry):
        x0 = chunk * 4 + 4
        for n in range(4):
            taps = [
                pres[pl.ds(pl.multiple_of((x0 + d) * CY + n * 8, 8), 8), :] for d in range(-3, 8)
            ]
            for i in range(4):
                at = pl.multiple_of((x0 + i + 4) * CY + n * 8, 8)
                wide_x[pl.ds(at, 8), :] = in_x[pl.ds(at, 8), :] - buoy_at(
                    buoy, x0 + i, n * 8
                ) * forward(taps, i)
        return carry

    lax.fori_loop(0, 6, along_x, 0)

    def along_y(x, carry):
        taps = [every(pres, x * CY + 4 + d, 3) for d in range(-3, 7)]
        for j in range(3):
            at = x * WIDE + 8 + j
            light = every(buoy, (x + 4) * WIDE + 8 + j, 3)
            put_every(wide_y, at, 3, every(in_y, at, 3) - light * forward(taps, j))
        return carry

    lax.fori_loop(0, CX, along_y, 0, unroll=4)
    wide_x[0 : 8 * CY, :] = in_x[0 : 8 * CY, :]
    wide_x[32 * CY : 40 * CY, :] = in_x[32 * CY : 40 * CY, :]
    for x in range(CX):
        wide_y[x * WIDE : x * WIDE + 8, :] = in_y[x * WIDE : x * WIDE + 8, :]
        wide_y[x * WIDE + 32 : x * WIDE + 40, :] = in_y[x * WIDE + 32 : x * WIDE + 40, :]
    for chunk in range(8):
        rows = slice(chunk * 128, (chunk + 1) * 128)
        spread[rows, :] = depth_difference(new_z[rows, :], mat_b)

    def across(chunk, carry):
        x0 = chunk * 4 + 8
        for n in range(4):
            taps = [
                wide_x[pl.ds(pl.multiple_of((x0 + d + 4) * CY + n * 8, 8), 8), :]
                for d in range(-4, 7)
            ]
            for i in range(4):
                at = pl.multiple_of((x0 + i) * CY + n * 8, 8)
                spread[pl.ds(at, 8), :] = spread[pl.ds(at, 8), :] + backward(taps, i)
        return carry

    lax.fori_loop(0, 4, across, 0)

    def along(x, carry):
        taps = [every(wide_y, x * WIDE + 12 + d, 2) for d in range(-4, 5)]
        for j in range(2):
            at = x * CY + 8 + j
            put_every(spread, at, 2, every(spread, at, 2) + backward(taps, j))
        return carry

    lax.fori_loop(0, CX, along, 0, unroll=4)


def edge_kernel(step, *refs):
    pres, gy_b, gy_a, gx_b, gx_a, in_x, in_y, buoy, modu, spread, kicked = refs[:11]
    last = step == STEPS - 1
    if last:
        p_to, x_to, y_to, rim_x, rim_y, wide_x, wide_y, new_p, out_y, sem = refs[11:]
        pushes = []

        def push(src, dst, rows):
            pushes.append(pltpu.make_async_copy(src, dst.at[rows], sem.at[len(pushes)]))
            pushes[-1].start()

    else:
        new_p, wide_x, wide_y, to_d, to_c, to_b, to_a, rim_x, rim_y = refs[11:]
    s, g, h = place()
    end_x = (g == 0) | (g == 3)
    end_y = (h == 0) | (h == 7)
    for which in range(2):
        low = odd(g) if which == 0 else jnp.logical_not(odd(g))
        start = jnp.where(low, 1, 24) * CY
        for i in range(HALO):
            for part in range(4):
                at = pl.multiple_of(start + (i * CY + part * 8), 8)
                rim_x[pl.ds(at, 8), :] = received((gx_a, gx_b), which, end_x, i * 32 + part * 8)
        low = odd(h) if which == 0 else jnp.logical_not(odd(h))
        start = jnp.where(low, 1, CX * STRIP + 8)
        for c in range(HALO):
            for part in range(4):
                value = received((gy_a, gy_b), which, end_y, c * 32 + part * 8)
                put_every(rim_y, start + (part * 8 * STRIP + c), STRIP, value)
    rim_x[8 * CY : 24 * CY, :] = jnp.concatenate([pres[0 : 8 * CY, :], pres[24 * CY : 32 * CY, :]], axis=0)
    for x in range(CX):
        rim_y[x * STRIP + 8 : x * STRIP + 16, :] = pres[x * CY : x * CY + 8, :]
        at = (CX + x) * STRIP
        rim_y[at : at + 8, :] = pres[x * CY + 24 : x * CY + 32, :]
    wide_x[8 * CY : 32 * CY, :] = in_x[8 * CY : 32 * CY, :]
    for x in range(CX):
        wide_y[x * WIDE + 8 : x * WIDE + 32, :] = in_y[x * WIDE + 8 : x * WIDE + 32, :]
    for rim, first in ((0, -4), (16, 28)):
        for half in range(2):
            for n in range(4):
                mid = (rim + half * 4 + 4) * CY + n * 8
                taps = [rim_x[mid + d * CY : mid + d * CY + 8, :] for d in range(-3, 8)]
                for i in range(4):
                    x = first + half * 4 + i
                    at = (x + 4) * CY + n * 8
                    wide_x[at : at + 8, :] = in_x[at : at + 8, :] - buoy_at(
                        buoy, x, n * 8
                    ) * forward(taps, i)

    if last:
        push(wide_x.at[pl.ds(4 * CY, CX * CY)], x_to, pl.ds(0, CX * CY))
    for x in range(CX):
        for rim, col in ((0, 0), (CX, 32)):
            mid = (rim + x) * STRIP + 4
            taps = [rim_y[mid + d : mid + d + 8, :] for d in range(-3, 5)]
            at = x * WIDE + col
            wide_y[at : at + 8, :] = in_y[at : at + 8, :] - buoy_at(buoy, x, col - 4) * forward(taps, 0)

    for first, count in ((0, 2), (8, 4), (24, 2)):
        for x0 in range(first, first + count * 4, 4):
            part_x = {}
            if count == 2:
                for n in range(4):
                    taps = [
                        wide_x[(x0 + d + 4) * CY + n * 8 : (x0 + d + 4) * CY + n * 8 + 8, :]
                        for d in range(-4, 7)
                    ]
                    for i in range(4):
                        part_x[i, n] = backward(taps, i)
            for i in range(4):
                for n in range(4):
                    at = (x0 + i) * CY + n * 8
                    total = spread[at : at + 8, :]
                    if n in (0, 3):
                        mid = (x0 + i) * WIDE + 4 + n * 8
                        taps = [wide_y[mid + d : mid + d + 8, :] for d in range(-4, 4)]
                        total = total + backward(taps, 0)
                    if count == 2:
                        total = total + part_x[i, n]
                    new_p[at : at + 8, :] = kicked[at : at + 8, :] - modu[at : at + 8, :] * total
        if last:
            for x in range(first, first + count * 4):
                out_y[x * CY : (x + 1) * CY, :] = wide_y[x * WIDE + 4 : x * WIDE + 36, :]
            part = pl.ds(first * CY, count * 4 * CY)
            push(new_p.at[part], p_to, part)
            push(out_y.at[part], y_to, part)
    if last:
        for copy in pushes:
            copy.wait()
    else:
        send_faces(new_p, (to_a, to_b), (to_c, to_d), 0, HALO)


def shape(rows, dtype=f32):
    return jax.ShapeDtypeStruct((rows, 128), dtype)


def vmem(rows):
    return pltpu.VMEM((rows, 128), f32)


def call(kernel, outs, args, scratch, name, smem=0, hbm=(), loose=(), to_hbm=(), cost=None):
    spaces = [
        pltpu.SMEM if i < smem else pltpu.HBM if i in hbm else pl.ANY if i in loose else pltpu.VMEM
        for i in range(len(args))
    ]
    to_hbm = range(len(outs)) if to_hbm is True else to_hbm
    outs = [pltpu.HBM(o.shape, o.dtype) if i in to_hbm else o for i, o in enumerate(outs)]
    places = [pltpu.HBM if i in to_hbm else pltpu.VMEM for i in range(len(outs))]
    specs = [pl.BlockSpec(memory_space=space) for space in spaces]
    args = [
        pltpu.with_memory_space_constraint(arg, pltpu.HBM) if i in hbm else arg
        for i, arg in enumerate(args)
    ]
    return pl.pallas_call(
        kernel,
        out_shape=outs,
        in_specs=specs,
        out_specs=[pl.BlockSpec(memory_space=place) for place in places],
        scratch_shapes=scratch,
        cost_estimate=cost,
        compiler_params=pltpu.CompilerParams(vmem_limit_bytes=24 * 1024 * 1024),
        name=name,
    )(*args)


GX, GY = 4, 8


def partners(match):
    out = []
    for g in range(GX):
        for h in range(GY):
            to_g, to_h = match(g, h)
            out.append((g * GY + h, to_g * GY + to_h))
    return out


gx_near = partners(lambda g, h: (g ^ 1, h))
gx_far = partners(lambda g, h: (g, h ^ 1) if g in (0, GX - 1) else (3 - g, h))
gy_near = partners(lambda g, h: (g, h ^ 1))
gy_far = partners(lambda g, h: (g ^ 1, h) if h in (0, GY - 1) else (g, ((h + 1) ^ 1) - 1))


def exchange(faces):
    plane = ("gx", "gy")
    return [
        lax.ppermute(face, plane, pairs)
        for face, pairs in zip(faces, (gy_far, gy_near, gx_far, gx_near))
    ]


def shards(velocity, density, offsets, pressure, vel_x, vel_y, vel_z, source_cells, wavelet):
    mat_f, mat_b = (jnp.asarray(m) for m in depth_matrices())
    vel = velocity.reshape(16 * 64, 128)
    den = density.reshape(16 * 64, 128)
    pres = pressure.reshape(CX * CY, 128)
    flow_x = vel_x.reshape(CX * CY, 128)
    flow_y = vel_y.reshape(CX * CY, 128)
    flow_z = vel_z.reshape(CX * CY, 128)
    block = shape(CX * CY)
    wide = shape(WIDE * CY)
    face = shape(HALO * 32)
    cost = pl.CostEstimate(flops=20_000_000, bytes_accessed=8_000_000, transcendentals=0)
    long = pl.CostEstimate(flops=3 * 10**10, bytes_accessed=8_000_000, transcendentals=0)

    dma = pltpu.SemaphoreType.DMA
    corner_scratch = [pltpu.SMEM((4, 2), jnp.int32), dma((1,))]
    (deal,) = call(
        pack_kernel,
        [shape(128 * 16)],
        [vel, den],
        [vmem(1024)] * 2 + [vmem(2048), dma((8,)), dma((4,))],
        "pack",
        hbm=range(2),
        to_hbm=True,
    )
    dealt = lax.all_to_all(deal.reshape(128, 16, 128), DEVICES, 0, 0, tiled=True)
    faces = call(
        face_kernel,
        [shape((HALO + 4) * 32)] * 4,
        [pres, flow_x, flow_y, deal],
        [vmem(1024)] * 3 + [dma((3,))],
        "first_faces",
        hbm=range(4),
        cost=cost,
    )
    faces = exchange(faces)
    (grad_z,) = call(
        depth_kernel,
        [block],
        [mat_f, pres],
        [vmem(CX * CY), vmem(CX * CY), dma((2,))],
        "step0_depth",
        hbm=(1,),
        to_hbm=True,
        cost=long,
    )
    (cut,) = call(
        cut_kernel,
        [jax.ShapeDtypeStruct((128, MESSAGE // 2, 2, 128), f32)],
        [dealt.reshape(128 * 16, 128), offsets, grad_z],
        [vmem(16 * LINE), vmem(16 * LINE), vmem(128 * MESSAGE), dma((4,))] + corner_scratch,
        "cut",
        hbm=(1, 2),
        to_hbm=True,
    )
    window = lax.all_to_all(cut, DEVICES, 0, 0, tiled=True)
    grad_x, grad_y, flow_x, flow_y, pres = call(
        grad0_kernel,
        [wide, wide, wide, wide, block],
        [source_cells, wavelet, pres, *faces, flow_x, flow_y],
        [vmem(WIDE * CY)] * 4 + [vmem(CX * CY)]
        + [vmem(PAD * PAD)] + [vmem(CX * CY)] * 2 + [dma((3,)), dma((5,))],
        "step0_gradients",
        smem=2,
        hbm=(2, 7, 8),
        to_hbm=True,
        cost=long,
    )
    pres, flow_x, flow_y, flow_z, buoy, modu, *faces = call(
        step0_kernel,
        [block, wide, wide, block, shape(WIDE * WIDE), block] + [face] * 4,
        [offsets, mat_b, window]
        + [pres, flow_x, flow_y, flow_z, grad_x, grad_y, grad_z],
        [vmem(CX * CY), vmem(WIDE * CY), vmem(WIDE * CY), vmem(CX * CY)]
        + [vmem(WIDE * CY), vmem(WIDE * CY), vmem(CX * CY)]
        + [vmem(WIDE * WIDE), vmem(CX * CY), dma((7,))] + corner_scratch,
        "step0",
        hbm=[0, *range(3, 10)],
    )
    for step in range(1, STEPS):
        last = step == STEPS - 1
        faces = exchange(faces)
        flow_x, flow_y, flow_z, spread, kicked = call(
            functools.partial(inner_kernel, step),
            [wide, wide, block, block, block],
            [source_cells, wavelet, mat_f, mat_b, pres, flow_x, flow_y, flow_z, buoy],
            [],
            f"inner{step}",
            smem=2,
            cost=cost,
        )
        pres, flow_x, flow_y, *faces = call(
            functools.partial(edge_kernel, step),
            [block, block, block] if last else [block, wide, wide] + [face] * 4,
            [pres, *faces, flow_x, flow_y, buoy, modu, spread, kicked],
            [vmem(32 * CY), vmem(2 * CX * STRIP)]
            + ([vmem(WIDE * CY)] * 2 + [vmem(CX * CY)] * 2 + [dma((7,))] if last else []),
            f"edge{step}",
            to_hbm=last or (),
        )
    return tuple(a.reshape(1, CX, CY, 128) for a in (pres, flow_x, flow_y, flow_z))


def solution(mesh):
    return jax.shard_map(
        shards,
        mesh=mesh,
        in_specs=(
            P(("shot", "gx"), "gy", None),
            P(("shot", "gx"), "gy", None),
            P(),
            P("shot", "gx", "gy", None),
            P("shot", "gx", "gy", None),
            P("shot", "gx", "gy", None),
            P("shot", "gx", "gy", None),
            P(),
            P(),
        ),
        out_specs=(
            P("shot", "gx", "gy", None),
            P("shot", "gx", "gy", None),
            P("shot", "gx", "gy", None),
            P("shot", "gx", "gy", None),
        ),
        check_vma=False,
    )
```

```python
import functools

import jax
import jax.numpy as jnp
import numpy as np
from jax import lax
from jax.experimental import pallas as pl
from jax.experimental.pallas import tpu as pltpu
from jax.sharding import PartitionSpec as P

CX = 32
CY = 32
STEPS = 4
HALO = 7
WIDE = 40
PAD = 48
LINE = 80
MESSAGE = 22
STRIP = 24
DEVICES = ("shot", "gx", "gy")

coefs = (1225.0 / 1024.0, -245.0 / 3072.0, 49.0 / 5120.0, -5.0 / 7168.0)
time_step = 0.09

f32 = jnp.float32
bf16 = jnp.bfloat16


def depth_matrices():
    out = []
    for lead in (0, 1):
        full = np.zeros((128, 128), np.float32)
        for reach in range(1, 5):
            for k in range(128):
                up, down = k + reach - lead, k - reach + 1 - lead
                if up < 128:
                    full[up, k] += np.float32(coefs[reach - 1])
                if down >= 0:
                    full[down, k] -= np.float32(coefs[reach - 1])
        high = full.astype(jnp.bfloat16)
        low = (full - high.astype(np.float32)).astype(jnp.bfloat16)
        out.append(np.concatenate([high, high, low], axis=0))
    return out


def depth_difference(values, mat_ref):
    high = values.astype(bf16)
    low = (values - high.astype(f32)).astype(bf16)
    main = jnp.dot(
        jnp.concatenate([high, low], axis=1), mat_ref[0:256, :], preferred_element_type=f32
    )
    return main + jnp.dot(high, mat_ref[256:384, :], preferred_element_type=f32)


def forward(taps, at):
    total = None
    for reach in range(1, 5):
        term = coefs[reach - 1] * (taps[at + 3 + reach] - taps[at + 4 - reach])
        total = term if total is None else total + term
    return total


def backward(taps, at):
    total = None
    for reach in range(1, 5):
        term = coefs[reach - 1] * (taps[at + 3 + reach] - taps[at + 4 - reach])
        total = term if total is None else total + term
    return total


def every(ref, start, step):
    return ref[pl.ds(start, 8, stride=step), :]


def put_every(ref, start, step, value):
    ref[pl.ds(start, 8, stride=step), :] = value


def place():
    return tuple(lax.axis_index(axis) for axis in DEVICES)


def odd(index):
    return lax.rem(index, 2) == 1


def send_faces(field, x_pair, y_pair, base, rows):
    s, g, h = place()
    for which, ref in enumerate(x_pair):
        low = odd(g) if which == 0 else jnp.logical_not(odd(g))
        start = pl.multiple_of(jnp.where(low, 0, (CX - rows) * CY), 32)
        ref[base * 32 : (base + rows) * 32, :] = field[pl.ds(start, rows * 32), :]
    for which, ref in enumerate(y_pair):
        low = odd(h) if which == 0 else jnp.logical_not(odd(h))
        start = jnp.where(low, 0, CY - rows)
        for c in range(rows):
            for part in range(4):
                at = (base + c) * 32 + part * 8
                ref[at : at + 8, :] = every(field, part * 8 * CY + start + c, CY)


def received(pair, which, end, at):
    value = pair[which][at : at + 8, :]
    return jnp.where(end, 0.0, value) if which == 1 else value


def pull_all(pairs, sem):
    pulls = [pltpu.make_async_copy(src, dst, sem.at[i]) for i, (src, dst) in enumerate(pairs)]
    for pull in pulls:
        pull.start()
    return pulls


def pack_kernel(vel, den, deal, vel_in, den_in, out, in_sem, out_sem):
    pulls = []
    for part in range(4):
        rows = pl.ds(part * 256, 256)
        pulls.append(
            [
                pltpu.make_async_copy(src.at[rows], dst.at[rows], in_sem.at[part * 2 + i])
                for i, (src, dst) in enumerate(((vel, vel_in), (den, den_in)))
            ]
        )
        for pull in pulls[-1]:
            pull.start()
    pushes = []
    for part in range(4):
        for pull in pulls[part]:
            pull.wait()
        for row in range(part * 4, part * 4 + 4):
            for cls in range(8):
                at = (row * 8 + cls) * 16
                out[at : at + 8, :] = every(vel_in, row * 64 + cls, 8)
                out[at + 8 : at + 16, :] = every(den_in, row * 64 + cls, 8)
        rows = pl.ds(part * 512, 512)
        pushes.append(pltpu.make_async_copy(out.at[rows], deal.at[rows], out_sem.at[part]))
        pushes[-1].start()
    for push in pushes:
        push.wait()


def face_kernel(pres, flow_x, flow_y, _, gy_b, gy_a, gx_b, gx_a, pres_in, x_in, y_in, sem):
    pulls = pull_all(((pres, pres_in), (flow_x, x_in), (flow_y, y_in)), sem)
    for pull in pulls:
        pull.wait()
    send_faces(pres_in, (gx_a, gx_b), (gy_a, gy_b), 0, HALO)
    send_faces(x_in, (gx_a, gx_b), (), HALO, 4)
    send_faces(y_in, (), (gy_a, gy_b), HALO, 4)


def corner(corners, shot, which):
    return jnp.max(corners[pl.ds(shot, 1), which : which + 1])


def cut_kernel(dealt, corners, _, out, rho_lines, vel_lines, cuts, sem):
    s, g, col_class = place()
    row_class = s * 4 + g
    for t in range(16):
        for part in range(8):
            src = (t * 8 + part) * 16
            dst = t * LINE + 8 + part * 8
            vel_lines[dst : dst + 8, :] = dealt[src : src + 8, :]
            rho_lines[dst : dst + 8, :] = dealt[src + 8 : src + 16, :]
    flat = out.reshape(128 * MESSAGE, 128)
    pushes = []
    for shot in range(4):
        shot_x, shot_y = corner(corners, shot, 0), corner(corners, shot, 1)
        col = lax.shift_right_arithmetic(shot_y - col_class + 7, 3)
        wide_col = lax.shift_right_arithmetic(shot_y - 4 - col_class + 7, 3)

        def block(part, carry):
            corner_x = shot_x + part * CX
            row = lax.shift_right_arithmetic(corner_x - row_class + 15, 4)
            low = lax.rem(row_class - corner_x + 4 + 1024, 16) < 4
            rim = jnp.clip(jnp.where(low, row - 1, row + 2), 0, 15)
            base = (shot * 32 + part * 8) * MESSAGE
            line = row * LINE + 8
            rim_line = rim * LINE + 8 + col
            for h in range(8):
                to = base + h * MESSAGE
                for k in range(2):
                    cuts[pl.ds(to + 5 * k, 5), :] = rho_lines[
                        pl.ds(line + wide_col + (k * LINE + 4 * h), 5), :
                    ]
                    cuts[pl.ds(to + 14 + 4 * k, 4), :] = vel_lines[
                        pl.ds(line + col + (k * LINE + 4 * h), 4), :
                    ]
                cuts[pl.ds(to + 10, 4), :] = rho_lines[pl.ds(rim_line + 4 * h, 4), :]
            return carry

        lax.fori_loop(0, 4, block, 0)
        rows = pl.ds(shot * 32 * MESSAGE, 32 * MESSAGE)
        pushes.append(pltpu.make_async_copy(cuts.at[rows], flat.at[rows], sem.at[shot]))
        pushes[-1].start()
    for push in pushes:
        push.wait()


def unpack_model(corners, window, buoy, modu, rho):
    s, g, h = place()
    corner_x = corner(corners, s, 0) + g * CX
    corner_y = corner(corners, s, 1) + h * CY
    wide_turn = lax.rem(8 - lax.rem(corner_y + 4, 8), 8)
    turn = lax.rem(8 - lax.rem(corner_y, 8), 8)
    sub = lax.broadcasted_iota(jnp.int32, (8, 128), 0)
    flat = window.reshape(128 * MESSAGE, 128)
    low_in = (h > 0) | (sub >= 4)
    high_in = (h < 7) | (sub < 4)
    for x in range(-4, CX + 3):
        start = lax.rem(corner_x + 16 + x, 16) * (8 * MESSAGE)
        base = (x + 4) * WIDE
        if 0 <= x < CX:
            for n in range(5):
                got = pltpu.roll(every(flat, start + 5 * (x // 16) + n, MESSAGE), wide_turn, 0)
                rho[base + n * 8 : base + n * 8 + 8, :] = got
                light = time_step * (1.0 / got)
                if n == 0:
                    light = jnp.where(low_in, light, 0.0)
                elif n == 4:
                    light = jnp.where(high_in, light, 0.0)
                buoy[base + n * 8 : base + n * 8 + 8, :] = light
            for n in range(4):
                got = every(flat, start + 14 + 4 * (x // 16) + n, MESSAGE)
                speed = pltpu.roll(got, turn, 0)
                at = x * CY + n * 8
                dens = rho[base + 4 + n * 8 : base + 12 + n * 8, :]
                modu[at : at + 8, :] = time_step * (dens * speed * speed)
        else:
            row_in = (g > 0) if x < 0 else (g < 3)
            for n in range(4):
                got = pltpu.roll(every(flat, start + 10 + n, MESSAGE), turn, 0)
                buoy[base + 4 + n * 8 : base + 12 + n * 8, :] = jnp.where(
                    row_in, time_step * (1.0 / got), 0.0
                )


def buoy_at(buoy, x, y, rows=8):
    return buoy[pl.ds((x + 4) * WIDE + 4 + y, rows), :]


def depth_kernel(mat_f, pres_from, grad_to, pres, grad_z, sem):
    pull = pltpu.make_async_copy(pres_from, pres, sem.at[0])
    pull.start()
    pull.wait()
    for chunk in range(8):
        rows = slice(chunk * 128, (chunk + 1) * 128)
        grad_z[rows, :] = depth_difference(pres[rows, :], mat_f)
    push = pltpu.make_async_copy(grad_z, grad_to, sem.at[1])
    push.start()
    push.wait()


def grad0_kernel(cells, amps, pres_from, gy_b, gy_a, gx_b, gx_a, x_from, y_from, *refs):
    outs, scratch = refs[:5], refs[5:]
    grad_x, grad_y, wide_x, wide_y, pres, padded, in_x, in_y, in_sem, out_sem = scratch
    for pull in pull_all(((pres_from, pres), (x_from, in_x), (y_from, in_y)), in_sem):
        pull.wait()
    s, g, h = place()
    end_x = (g == 0) | (g == 3)
    end_y = (h == 0) | (h == 7)
    for x in range(CX):
        at = (x + 8) * PAD + 8
        padded[at : at + 32, :] = pres[x * CY : (x + 1) * CY, :]
        wide_y[x * WIDE + 4 : x * WIDE + 36, :] = in_y[x * CY : (x + 1) * CY, :]
    wide_x[4 * CY : 36 * CY, :] = in_x[...]
    x_pair, y_pair = (gx_a, gx_b), (gy_a, gy_b)
    for which in range(2):
        low = odd(g) if which == 0 else jnp.logical_not(odd(g))
        start = jnp.where(low, -HALO, CX)
        for i in range(HALO):
            for part in range(4):
                at = pl.multiple_of((start + i + 8) * PAD + 8 + part * 8, 8)
                padded[pl.ds(at, 8), :] = received(x_pair, which, end_x, i * 32 + part * 8)
        start = jnp.where(low, 0, 36)
        for i in range(4):
            for part in range(4):
                at = pl.multiple_of((start + i) * CY + part * 8, 8)
                wide_x[pl.ds(at, 8), :] = received(x_pair, which, end_x, (HALO + i) * 32 + part * 8)
        low = odd(h) if which == 0 else jnp.logical_not(odd(h))
        start = jnp.where(low, -HALO, CY)
        for c in range(HALO):
            for part in range(4):
                at = (part * 8 + 8) * PAD + start + c + 8
                put_every(padded, at, PAD, received(y_pair, which, end_y, c * 32 + part * 8))
        start = jnp.where(low, 0, 36)
        for c in range(4):
            for part in range(4):
                value = received(y_pair, which, end_y, (HALO + c) * 32 + part * 8)
                put_every(wide_y, part * 8 * WIDE + start + c, WIDE, value)

    def along_x(chunk, carry):
        x0 = chunk * 4 - 4
        for n in range(4):
            taps = [
                padded[pl.ds(pl.multiple_of((x0 + d + 8) * PAD + 8 + n * 8, 8), 8), :]
                for d in range(-3, 8)
            ]
            for i in range(4):
                at = pl.multiple_of((x0 + i + 4) * CY + n * 8, 8)
                grad_x[pl.ds(at, 8), :] = forward(taps, i)
        return carry

    lax.fori_loop(0, 10, along_x, 0)

    def along_y(x, carry):
        taps = [every(padded, (x + 8) * PAD + 4 + d, 5) for d in range(-3, 9)]
        for j in range(5):
            put_every(grad_y, x * WIDE + j, 5, forward(taps, j))
        return carry

    lax.fori_loop(0, CX, along_y, 0)
    kick_source(0, cells, amps, pres)
    for push in pull_all(zip(scratch[:5], outs), out_sem):
        push.wait()


def kick_source(step, cells, amps, field):
    s, g, h = place()
    x = cells[s, 0] - g * CX
    y = cells[s, 1] - h * CY

    @pl.when((x >= 0) & (x < CX) & (y >= 0) & (y < CY))
    def _():
        at = x * CY + y
        lane = lax.broadcasted_iota(jnp.int32, (1, 128), 1)
        kick = time_step * amps[s, step]
        field[pl.ds(at, 1), :] = field[pl.ds(at, 1), :] + jnp.where(lane == cells[s, 2], kick, 0.0)


def step0_kernel(corners, mat_b, window, *refs):
    sources, outs, scratch = refs[:7], refs[7:17], refs[17:]
    new_p, wide_x, wide_y, new_z, buoy, modu, gy_b, gy_a, gx_b, gx_a = outs
    pres, in_x, in_y, in_z, grad_x, grad_y, grad_z, rho, spread, sem = scratch
    order = (6, 3, 4, 1, 0, 5, 2)
    pulls = pull_all([(sources[i], scratch[i]) for i in order], sem)
    unpack_model(corners, window, buoy, modu, rho)

    def wait(*which):
        for i in which:
            pulls[i].wait()

    def tiles(count, per):
        return [(x, n, (x * per + n) * 8) for x in range(count) for n in range(per)]

    wait(0, 1)
    for x, n, at in tiles(CX, 4):
        new_z[at : at + 8, :] = in_z[at : at + 8, :] - buoy_at(buoy, x, n * 8) * grad_z[at : at + 8, :]
    for chunk in range(8):
        rows = slice(chunk * 128, (chunk + 1) * 128)
        spread[rows, :] = depth_difference(new_z[rows, :], mat_b)
    wait(2, 3)
    for x, n, at in tiles(WIDE, 4):
        wide_x[at : at + 8, :] = (
            in_x[at : at + 8, :] - buoy_at(buoy, x - 4, n * 8) * grad_x[at : at + 8, :]
        )
    for x0 in range(0, CX, 4):
        for n in range(4):
            mid = (x0 + 4) * CY + n * 8
            taps = [wide_x[mid + d * CY : mid + d * CY + 8, :] for d in range(-4, 7)]
            for i in range(4):
                at = (x0 + i) * CY + n * 8
                spread[at : at + 8, :] = spread[at : at + 8, :] + backward(taps, i)
    wait(4, 5, 6)
    for x, n, at in tiles(CX, 5):
        wide_y[at : at + 8, :] = (
            in_y[at : at + 8, :] - buoy_at(buoy, x, n * 8 - 4) * grad_y[at : at + 8, :]
        )
    for x in range(CX):
        taps = [every(wide_y, x * WIDE + 4 + d, 4) for d in range(-4, 7)]
        for j in range(4):
            at = x * CY + j
            total = every(spread, at, 4) + backward(taps, j)
            put_every(new_p, at, 4, every(pres, at, 4) - every(modu, at, 4) * total)
    send_faces(new_p, (gx_a, gx_b), (gy_a, gy_b), 0, HALO)


def inner_kernel(step, cells, amps, mat_f, mat_b, pres, in_x, in_y, in_z, buoy, *outs):
    wide_x, wide_y, new_z, spread, kicked = outs
    kicked[...] = pres[...]
    kick_source(step, cells, amps, kicked)
    for chunk in range(8):
        rows = slice(chunk * 128, (chunk + 1) * 128)
        grad = depth_difference(pres[rows, :], mat_f)
        light = jnp.concatenate(
            [buoy_at(buoy, x, 0, 32) for x in range(chunk * 4, chunk * 4 + 4)], axis=0
        )
        new_z[rows, :] = in_z[rows, :] - light * grad

    def along_x(chunk, carry):
        x0 = chunk * 4 + 4
        for n in range(4):
            taps = [
                pres[pl.ds(pl.multiple_of((x0 + d) * CY + n * 8, 8), 8), :] for d in range(-3, 8)
            ]
            for i in range(4):
                at = pl.multiple_of((x0 + i + 4) * CY + n * 8, 8)
                wide_x[pl.ds(at, 8), :] = in_x[pl.ds(at, 8), :] - buoy_at(
                    buoy, x0 + i, n * 8
                ) * forward(taps, i)
        return carry

    lax.fori_loop(0, 6, along_x, 0)

    def along_y(x, carry):
        taps = [every(pres, x * CY + 4 + d, 3) for d in range(-3, 7)]
        for j in range(3):
            at = x * WIDE + 8 + j
            light = every(buoy, (x + 4) * WIDE + 8 + j, 3)
            put_every(wide_y, at, 3, every(in_y, at, 3) - light * forward(taps, j))
        return carry

    lax.fori_loop(0, CX, along_y, 0, unroll=4)
    wide_x[0 : 8 * CY, :] = in_x[0 : 8 * CY, :]
    wide_x[32 * CY : 40 * CY, :] = in_x[32 * CY : 40 * CY, :]
    for x in range(CX):
        wide_y[x * WIDE : x * WIDE + 8, :] = in_y[x * WIDE : x * WIDE + 8, :]
        wide_y[x * WIDE + 32 : x * WIDE + 40, :] = in_y[x * WIDE + 32 : x * WIDE + 40, :]
    for chunk in range(8):
        rows = slice(chunk * 128, (chunk + 1) * 128)
        spread[rows, :] = depth_difference(new_z[rows, :], mat_b)

    def across(chunk, carry):
        x0 = chunk * 4 + 8
        for n in range(4):
            taps = [
                wide_x[pl.ds(pl.multiple_of((x0 + d + 4) * CY + n * 8, 8), 8), :]
                for d in range(-4, 7)
            ]
            for i in range(4):
                at = pl.multiple_of((x0 + i) * CY + n * 8, 8)
                spread[pl.ds(at, 8), :] = spread[pl.ds(at, 8), :] + backward(taps, i)
        return carry

    lax.fori_loop(0, 4, across, 0)

    def along(x, carry):
        taps = [every(wide_y, x * WIDE + 12 + d, 2) for d in range(-4, 5)]
        for j in range(2):
            at = x * CY + 8 + j
            put_every(spread, at, 2, every(spread, at, 2) + backward(taps, j))
        return carry

    lax.fori_loop(0, CX, along, 0, unroll=4)


def edge_kernel(step, *refs):
    pres, gy_b, gy_a, gx_b, gx_a, in_x, in_y, buoy, modu, spread, kicked = refs[:11]
    last = step == STEPS - 1
    if last:
        p_to, x_to, y_to, rim_x, rim_y, wide_x, wide_y, new_p, out_y, sem = refs[11:]
        pushes = []

        def push(src, dst, rows):
            pushes.append(pltpu.make_async_copy(src, dst.at[rows], sem.at[len(pushes)]))
            pushes[-1].start()

    else:
        new_p, wide_x, wide_y, to_d, to_c, to_b, to_a, rim_x, rim_y = refs[11:]
    s, g, h = place()
    end_x = (g == 0) | (g == 3)
    end_y = (h == 0) | (h == 7)
    for which in range(2):
        low = odd(g) if which == 0 else jnp.logical_not(odd(g))
        start = jnp.where(low, 1, 24) * CY
        for i in range(HALO):
            for part in range(4):
                at = pl.multiple_of(start + (i * CY + part * 8), 8)
                rim_x[pl.ds(at, 8), :] = received((gx_a, gx_b), which, end_x, i * 32 + part * 8)
        low = odd(h) if which == 0 else jnp.logical_not(odd(h))
        start = jnp.where(low, 1, CX * STRIP + 8)
        for c in range(HALO):
            for part in range(4):
                value = received((gy_a, gy_b), which, end_y, c * 32 + part * 8)
                put_every(rim_y, start + (part * 8 * STRIP + c), STRIP, value)
    rim_x[8 * CY : 24 * CY, :] = jnp.concatenate([pres[0 : 8 * CY, :], pres[24 * CY : 32 * CY, :]], axis=0)
    for x in range(CX):
        rim_y[x * STRIP + 8 : x * STRIP + 16, :] = pres[x * CY : x * CY + 8, :]
        at = (CX + x) * STRIP
        rim_y[at : at + 8, :] = pres[x * CY + 24 : x * CY + 32, :]
    wide_x[8 * CY : 32 * CY, :] = in_x[8 * CY : 32 * CY, :]
    for x in range(CX):
        wide_y[x * WIDE + 8 : x * WIDE + 32, :] = in_y[x * WIDE + 8 : x * WIDE + 32, :]
    for rim, first in ((0, -4), (16, 28)):
        for half in range(2):
            for n in range(4):
                mid = (rim + half * 4 + 4) * CY + n * 8
                taps = [rim_x[mid + d * CY : mid + d * CY + 8, :] for d in range(-3, 8)]
                for i in range(4):
                    x = first + half * 4 + i
                    at = (x + 4) * CY + n * 8
                    wide_x[at : at + 8, :] = in_x[at : at + 8, :] - buoy_at(
                        buoy, x, n * 8
                    ) * forward(taps, i)

    if last:
        push(wide_x.at[pl.ds(4 * CY, CX * CY)], x_to, pl.ds(0, CX * CY))
    for x in range(CX):
        for rim, col in ((0, 0), (CX, 32)):
            mid = (rim + x) * STRIP + 4
            taps = [rim_y[mid + d : mid + d + 8, :] for d in range(-3, 5)]
            at = x * WIDE + col
            wide_y[at : at + 8, :] = in_y[at : at + 8, :] - buoy_at(buoy, x, col - 4) * forward(taps, 0)

    for first, count in ((0, 2), (8, 4), (24, 2)):
        for x0 in range(first, first + count * 4, 4):
            part_x = {}
            if count == 2:
                for n in range(4):
                    taps = [
                        wide_x[(x0 + d + 4) * CY + n * 8 : (x0 + d + 4) * CY + n * 8 + 8, :]
                        for d in range(-4, 7)
                    ]
                    for i in range(4):
                        part_x[i, n] = backward(taps, i)
            for i in range(4):
                for n in range(4):
                    at = (x0 + i) * CY + n * 8
                    total = spread[at : at + 8, :]
                    if n in (0, 3):
                        mid = (x0 + i) * WIDE + 4 + n * 8
                        taps = [wide_y[mid + d : mid + d + 8, :] for d in range(-4, 4)]
                        total = total + backward(taps, 0)
                    if count == 2:
                        total = total + part_x[i, n]
                    new_p[at : at + 8, :] = kicked[at : at + 8, :] - modu[at : at + 8, :] * total
        if last:
            for x in range(first, first + count * 4):
                out_y[x * CY : (x + 1) * CY, :] = wide_y[x * WIDE + 4 : x * WIDE + 36, :]
            part = pl.ds(first * CY, count * 4 * CY)
            push(new_p.at[part], p_to, part)
            push(out_y.at[part], y_to, part)
    if last:
        for copy in pushes:
            copy.wait()
    else:
        send_faces(new_p, (to_a, to_b), (to_c, to_d), 0, HALO)


def shape(rows, dtype=f32):
    return jax.ShapeDtypeStruct((rows, 128), dtype)


def vmem(rows):
    return pltpu.VMEM((rows, 128), f32)


def call(kernel, outs, args, scratch, name, smem=0, hbm=(), loose=(), to_hbm=(), cost=None):
    spaces = [
        pltpu.SMEM if i < smem else pltpu.HBM if i in hbm else pl.ANY if i in loose else pltpu.VMEM
        for i in range(len(args))
    ]
    to_hbm = range(len(outs)) if to_hbm is True else to_hbm
    outs = [pltpu.HBM(o.shape, o.dtype) if i in to_hbm else o for i, o in enumerate(outs)]
    places = [pltpu.HBM if i in to_hbm else pltpu.VMEM for i in range(len(outs))]
    specs = [pl.BlockSpec(memory_space=space) for space in spaces]
    args = [
        pltpu.with_memory_space_constraint(arg, pltpu.HBM) if i in hbm else arg
        for i, arg in enumerate(args)
    ]
    return pl.pallas_call(
        kernel,
        out_shape=outs,
        in_specs=specs,
        out_specs=[pl.BlockSpec(memory_space=place) for place in places],
        scratch_shapes=scratch,
        cost_estimate=cost,
        compiler_params=pltpu.CompilerParams(vmem_limit_bytes=24 * 1024 * 1024),
        name=name,
    )(*args)


GX, GY = 4, 8


def partners(match):
    out = []
    for s in range(4):
        for g in range(GX):
            for h in range(GY):
                to_s, to_g, to_h = match(s, g, h)
                out.append(((s * GX + g) * GY + h, (to_s * GX + to_g) * GY + to_h))
    return out


gx_near = partners(lambda s, g, h: (s, g ^ 1, h))
gx_far = partners(lambda s, g, h: (s ^ 1, g, h) if g in (0, GX - 1) else (s, 3 - g, h))
gy_near = partners(lambda s, g, h: (s, g, h ^ 1))
gy_far = partners(
    lambda s, g, h: (s ^ 1, g, h) if h in (0, GY - 1) else (s, g, ((h + 1) ^ 1) - 1)
)


def exchange(faces):
    gy_b = lax.ppermute(faces[0], DEVICES, gy_far)
    gx_b = lax.ppermute(faces[2], DEVICES, gx_far)
    gy_a = lax.ppermute(faces[1], DEVICES, gy_near)
    gx_a = lax.ppermute(faces[3], DEVICES, gx_near)
    return [gy_b, gy_a, gx_b, gx_a]


def shards(velocity, density, offsets, pressure, vel_x, vel_y, vel_z, source_cells, wavelet):
    mat_f, mat_b = (jnp.asarray(m) for m in depth_matrices())
    vel = velocity.reshape(16 * 64, 128)
    den = density.reshape(16 * 64, 128)
    pres = pressure.reshape(CX * CY, 128)
    flow_x = vel_x.reshape(CX * CY, 128)
    flow_y = vel_y.reshape(CX * CY, 128)
    flow_z = vel_z.reshape(CX * CY, 128)
    block = shape(CX * CY)
    wide = shape(WIDE * CY)
    face = shape(HALO * 32)
    cost = pl.CostEstimate(flops=20_000_000, bytes_accessed=8_000_000, transcendentals=0)
    long = pl.CostEstimate(flops=3 * 10**10, bytes_accessed=8_000_000, transcendentals=0)

    dma = pltpu.SemaphoreType.DMA
    (deal,) = call(
        pack_kernel,
        [shape(128 * 16)],
        [vel, den],
        [vmem(1024)] * 2 + [vmem(2048), dma((8,)), dma((4,))],
        "pack",
        hbm=range(2),
        to_hbm=True,
    )
    dealt = lax.all_to_all(deal.reshape(128, 16, 128), DEVICES, 0, 0, tiled=True)
    faces = call(
        face_kernel,
        [shape((HALO + 4) * 32)] * 4,
        [pres, flow_x, flow_y, deal],
        [vmem(1024)] * 3 + [dma((3,))],
        "first_faces",
        hbm=range(4),
        cost=cost,
    )
    faces = exchange(faces)
    (grad_z,) = call(
        depth_kernel,
        [block],
        [mat_f, pres],
        [vmem(CX * CY), vmem(CX * CY), dma((2,))],
        "step0_depth",
        hbm=(1,),
        to_hbm=True,
        cost=long,
    )
    (cut,) = call(
        cut_kernel,
        [jax.ShapeDtypeStruct((128, MESSAGE // 2, 2, 128), f32)],
        [dealt.reshape(128 * 16, 128), offsets, grad_z],
        [vmem(16 * LINE), vmem(16 * LINE), vmem(128 * MESSAGE), dma((4,))],
        "cut",
        hbm=(2,),
        to_hbm=True,
    )
    window = lax.all_to_all(cut, DEVICES, 0, 0, tiled=True)
    grad_x, grad_y, flow_x, flow_y, pres = call(
        grad0_kernel,
        [wide, wide, wide, wide, block],
        [source_cells, wavelet, pres, *faces, flow_x, flow_y],
        [vmem(WIDE * CY)] * 4 + [vmem(CX * CY)]
        + [vmem(PAD * PAD)] + [vmem(CX * CY)] * 2 + [dma((3,)), dma((5,))],
        "step0_gradients",
        smem=2,
        hbm=(2, 7, 8),
        to_hbm=True,
        cost=long,
    )
    pres, flow_x, flow_y, flow_z, buoy, modu, *faces = call(
        step0_kernel,
        [block, wide, wide, block, shape(WIDE * WIDE), block] + [face] * 4,
        [offsets, mat_b, window]
        + [pres, flow_x, flow_y, flow_z, grad_x, grad_y, grad_z],
        [vmem(CX * CY), vmem(WIDE * CY), vmem(WIDE * CY), vmem(CX * CY)]
        + [vmem(WIDE * CY), vmem(WIDE * CY), vmem(CX * CY)]
        + [vmem(WIDE * WIDE), vmem(CX * CY), dma((7,))],
        "step0",
        hbm=range(3, 10),
    )
    for step in range(1, STEPS):
        last = step == STEPS - 1
        faces = exchange(faces)
        flow_x, flow_y, flow_z, spread, kicked = call(
            functools.partial(inner_kernel, step),
            [wide, wide, block, block, block],
            [source_cells, wavelet, mat_f, mat_b, pres, flow_x, flow_y, flow_z, buoy],
            [],
            f"inner{step}",
            smem=2,
            cost=cost,
        )
        pres, flow_x, flow_y, *faces = call(
            functools.partial(edge_kernel, step),
            [block, block, block] if last else [block, wide, wide] + [face] * 4,
            [pres, *faces, flow_x, flow_y, buoy, modu, spread, kicked],
            [vmem(32 * CY), vmem(2 * CX * STRIP)]
            + ([vmem(WIDE * CY)] * 2 + [vmem(CX * CY)] * 2 + [dma((7,))] if last else []),
            f"edge{step}",
            to_hbm=last or (),
        )
    return tuple(a.reshape(1, CX, CY, 128) for a in (pres, flow_x, flow_y, flow_z))


def solution(mesh):
    return jax.shard_map(
        shards,
        mesh=mesh,
        in_specs=(
            P(("shot", "gx"), "gy", None),
            P(("shot", "gx"), "gy", None),
            P(),
            P("shot", "gx", "gy", None),
            P("shot", "gx", "gy", None),
            P("shot", "gx", "gy", None),
            P("shot", "gx", "gy", None),
            P(),
            P(),
        ),
        out_specs=(
            P("shot", "gx", "gy", None),
            P("shot", "gx", "gy", None),
            P("shot", "gx", "gy", None),
            P("shot", "gx", "gy", None),
        ),
        check_vma=False,
    )
```

```python
import functools

import jax
import jax.numpy as jnp
import numpy as np
from jax import lax
from jax.experimental import pallas as pl
from jax.experimental.pallas import tpu as pltpu
from jax.sharding import PartitionSpec as P

CX = 32
CY = 32
STEPS = 4
HALO = 7
WIDE = 40
PAD = 48
LINE = 80
MESSAGE = 22
STRIP = 24
DEVICES = ("shot", "gx", "gy")

coefs = (1225.0 / 1024.0, -245.0 / 3072.0, 49.0 / 5120.0, -5.0 / 7168.0)
time_step = 0.09

f32 = jnp.float32
bf16 = jnp.bfloat16


def depth_matrices():
    out = []
    for lead in (0, 1):
        full = np.zeros((128, 128), np.float32)
        for reach in range(1, 5):
            for k in range(128):
                up, down = k + reach - lead, k - reach + 1 - lead
                if up < 128:
                    full[up, k] += np.float32(coefs[reach - 1])
                if down >= 0:
                    full[down, k] -= np.float32(coefs[reach - 1])
        high = full.astype(jnp.bfloat16)
        low = (full - high.astype(np.float32)).astype(jnp.bfloat16)
        out.append(np.concatenate([high, high, low], axis=0))
    return out


def depth_difference(values, mat_ref):
    high = values.astype(bf16)
    low = (values - high.astype(f32)).astype(bf16)
    main = jnp.dot(
        jnp.concatenate([high, low], axis=1), mat_ref[0:256, :], preferred_element_type=f32
    )
    return main + jnp.dot(high, mat_ref[256:384, :], preferred_element_type=f32)


def forward(taps, at):
    total = None
    for reach in range(1, 5):
        term = coefs[reach - 1] * (taps[at + 3 + reach] - taps[at + 4 - reach])
        total = term if total is None else total + term
    return total


def backward(taps, at):
    total = None
    for reach in range(1, 5):
        term = coefs[reach - 1] * (taps[at + 3 + reach] - taps[at + 4 - reach])
        total = term if total is None else total + term
    return total


def every(ref, start, step):
    return ref[pl.ds(start, 8, stride=step), :]


def put_every(ref, start, step, value):
    ref[pl.ds(start, 8, stride=step), :] = value


def place():
    return tuple(lax.axis_index(axis) for axis in DEVICES)


def odd(index):
    return lax.rem(index, 2) == 1


def send_faces(field, x_pair, y_pair, base, rows):
    s, g, h = place()
    for which, ref in enumerate(x_pair):
        low = odd(g) if which == 0 else jnp.logical_not(odd(g))
        start = pl.multiple_of(jnp.where(low, 0, (CX - rows) * CY), 32)
        ref[base * 32 : (base + rows) * 32, :] = field[pl.ds(start, rows * 32), :]
    for which, ref in enumerate(y_pair):
        low = odd(h) if which == 0 else jnp.logical_not(odd(h))
        start = jnp.where(low, 0, CY - rows)
        for c in range(rows):
            for part in range(4):
                at = (base + c) * 32 + part * 8
                ref[at : at + 8, :] = every(field, part * 8 * CY + start + c, CY)


def received(pair, which, end, at):
    value = pair[which][at : at + 8, :]
    return jnp.where(end, 0.0, value) if which == 1 else value


def pull_all(pairs, sem):
    pulls = [pltpu.make_async_copy(src, dst, sem.at[i]) for i, (src, dst) in enumerate(pairs)]
    for pull in pulls:
        pull.start()
    return pulls


def pack_kernel(vel, den, deal, vel_in, den_in, out, in_sem, out_sem):
    pulls = []
    for part in range(4):
        rows = pl.ds(part * 256, 256)
        pulls.append(
            [
                pltpu.make_async_copy(src.at[rows], dst.at[rows], in_sem.at[part * 2 + i])
                for i, (src, dst) in enumerate(((vel, vel_in), (den, den_in)))
            ]
        )
        for pull in pulls[-1]:
            pull.start()
    pushes = []
    for part in range(4):
        for pull in pulls[part]:
            pull.wait()
        for row in range(part * 4, part * 4 + 4):
            for cls in range(8):
                at = (row * 8 + cls) * 16
                out[at : at + 8, :] = every(vel_in, row * 64 + cls, 8)
                out[at + 8 : at + 16, :] = every(den_in, row * 64 + cls, 8)
        rows = pl.ds(part * 512, 512)
        pushes.append(pltpu.make_async_copy(out.at[rows], deal.at[rows], out_sem.at[part]))
        pushes[-1].start()
    for push in pushes:
        push.wait()


def face_kernel(pres, flow_x, flow_y, _, gy_b, gy_a, gx_b, gx_a, pres_in, x_in, y_in, sem):
    pulls = pull_all(((pres, pres_in), (flow_x, x_in), (flow_y, y_in)), sem)
    for pull in pulls:
        pull.wait()
    send_faces(pres_in, (gx_a, gx_b), (gy_a, gy_b), 0, HALO)
    send_faces(x_in, (gx_a, gx_b), (), HALO, 4)
    send_faces(y_in, (), (gy_a, gy_b), HALO, 4)


def corner(corners, shot, which):
    return jnp.max(corners[pl.ds(shot, 1), which : which + 1])


def cut_kernel(dealt, corners, _, out, rho_lines, vel_lines, cuts, sem):
    s, g, col_class = place()
    row_class = s * 4 + g
    for t in range(16):
        for part in range(8):
            src = (t * 8 + part) * 16
            dst = t * LINE + 8 + part * 8
            vel_lines[dst : dst + 8, :] = dealt[src : src + 8, :]
            rho_lines[dst : dst + 8, :] = dealt[src + 8 : src + 16, :]
    flat = out.reshape(128 * MESSAGE, 128)
    pushes = []
    for shot in range(4):
        shot_x, shot_y = corner(corners, shot, 0), corner(corners, shot, 1)
        col = lax.shift_right_arithmetic(shot_y - col_class + 7, 3)
        wide_col = lax.shift_right_arithmetic(shot_y - 4 - col_class + 7, 3)

        def block(part, carry):
            corner_x = shot_x + part * CX
            row = lax.shift_right_arithmetic(corner_x - row_class + 15, 4)
            low = lax.rem(row_class - corner_x + 4 + 1024, 16) < 4
            rim = jnp.clip(jnp.where(low, row - 1, row + 2), 0, 15)
            base = (shot * 32 + part * 8) * MESSAGE
            line = row * LINE + 8
            rim_line = rim * LINE + 8 + col
            for h in range(8):
                to = base + h * MESSAGE
                for k in range(2):
                    cuts[pl.ds(to + 5 * k, 5), :] = rho_lines[
                        pl.ds(line + wide_col + (k * LINE + 4 * h), 5), :
                    ]
                    cuts[pl.ds(to + 14 + 4 * k, 4), :] = vel_lines[
                        pl.ds(line + col + (k * LINE + 4 * h), 4), :
                    ]
                cuts[pl.ds(to + 10, 4), :] = rho_lines[pl.ds(rim_line + 4 * h, 4), :]
            return carry

        for part in range(4):
            block(part, 0)
        rows = pl.ds(shot * 32 * MESSAGE, 32 * MESSAGE)
        pushes.append(pltpu.make_async_copy(cuts.at[rows], flat.at[rows], sem.at[shot]))
        pushes[-1].start()
    for push in pushes:
        push.wait()


def unpack_model(corners, window, buoy, modu, rho):
    s, g, h = place()
    corner_x = corner(corners, s, 0) + g * CX
    corner_y = corner(corners, s, 1) + h * CY
    wide_turn = lax.rem(8 - lax.rem(corner_y + 4, 8), 8)
    turn = lax.rem(8 - lax.rem(corner_y, 8), 8)
    sub = lax.broadcasted_iota(jnp.int32, (8, 128), 0)
    flat = window.reshape(128 * MESSAGE, 128)
    low_in = (h > 0) | (sub >= 4)
    high_in = (h < 7) | (sub < 4)
    for x in range(-4, CX + 3):
        start = lax.rem(corner_x + 16 + x, 16) * (8 * MESSAGE)
        base = (x + 4) * WIDE
        if 0 <= x < CX:
            for n in range(5):
                got = pltpu.roll(every(flat, start + 5 * (x // 16) + n, MESSAGE), wide_turn, 0)
                rho[base + n * 8 : base + n * 8 + 8, :] = got
                light = time_step * (1.0 / got)
                if n == 0:
                    light = jnp.where(low_in, light, 0.0)
                elif n == 4:
                    light = jnp.where(high_in, light, 0.0)
                buoy[base + n * 8 : base + n * 8 + 8, :] = light
            for n in range(4):
                got = every(flat, start + 14 + 4 * (x // 16) + n, MESSAGE)
                speed = pltpu.roll(got, turn, 0)
                at = x * CY + n * 8
                dens = rho[base + 4 + n * 8 : base + 12 + n * 8, :]
                modu[at : at + 8, :] = time_step * (dens * speed * speed)
        else:
            row_in = (g > 0) if x < 0 else (g < 3)
            for n in range(4):
                got = pltpu.roll(every(flat, start + 10 + n, MESSAGE), turn, 0)
                buoy[base + 4 + n * 8 : base + 12 + n * 8, :] = jnp.where(
                    row_in, time_step * (1.0 / got), 0.0
                )


def buoy_at(buoy, x, y, rows=8):
    return buoy[pl.ds((x + 4) * WIDE + 4 + y, rows), :]


def depth_kernel(mat_f, pres_from, grad_to, pres, grad_z, sem):
    pull = pltpu.make_async_copy(pres_from, pres, sem.at[0])
    pull.start()
    pull.wait()
    for chunk in range(8):
        rows = slice(chunk * 128, (chunk + 1) * 128)
        grad_z[rows, :] = depth_difference(pres[rows, :], mat_f)
    push = pltpu.make_async_copy(grad_z, grad_to, sem.at[1])
    push.start()
    push.wait()


def grad0_kernel(cells, amps, pres_from, gy_b, gy_a, gx_b, gx_a, x_from, y_from, *refs):
    outs, scratch = refs[:5], refs[5:]
    grad_x, grad_y, wide_x, wide_y, pres, padded, in_x, in_y, in_sem, out_sem = scratch
    for pull in pull_all(((pres_from, pres), (x_from, in_x), (y_from, in_y)), in_sem):
        pull.wait()
    s, g, h = place()
    end_x = (g == 0) | (g == 3)
    end_y = (h == 0) | (h == 7)
    for x in range(CX):
        at = (x + 8) * PAD + 8
        padded[at : at + 32, :] = pres[x * CY : (x + 1) * CY, :]
        wide_y[x * WIDE + 4 : x * WIDE + 36, :] = in_y[x * CY : (x + 1) * CY, :]
    wide_x[4 * CY : 36 * CY, :] = in_x[...]
    x_pair, y_pair = (gx_a, gx_b), (gy_a, gy_b)
    for which in range(2):
        low = odd(g) if which == 0 else jnp.logical_not(odd(g))
        start = jnp.where(low, -HALO, CX)
        for i in range(HALO):
            for part in range(4):
                at = pl.multiple_of((start + i + 8) * PAD + 8 + part * 8, 8)
                padded[pl.ds(at, 8), :] = received(x_pair, which, end_x, i * 32 + part * 8)
        start = jnp.where(low, 0, 36)
        for i in range(4):
            for part in range(4):
                at = pl.multiple_of((start + i) * CY + part * 8, 8)
                wide_x[pl.ds(at, 8), :] = received(x_pair, which, end_x, (HALO + i) * 32 + part * 8)
        low = odd(h) if which == 0 else jnp.logical_not(odd(h))
        start = jnp.where(low, -HALO, CY)
        for c in range(HALO):
            for part in range(4):
                at = (part * 8 + 8) * PAD + start + c + 8
                put_every(padded, at, PAD, received(y_pair, which, end_y, c * 32 + part * 8))
        start = jnp.where(low, 0, 36)
        for c in range(4):
            for part in range(4):
                value = received(y_pair, which, end_y, (HALO + c) * 32 + part * 8)
                put_every(wide_y, part * 8 * WIDE + start + c, WIDE, value)

    def along_x(chunk, carry):
        x0 = chunk * 4 - 4
        for n in range(4):
            taps = [
                padded[pl.ds(pl.multiple_of((x0 + d + 8) * PAD + 8 + n * 8, 8), 8), :]
                for d in range(-3, 8)
            ]
            for i in range(4):
                at = pl.multiple_of((x0 + i + 4) * CY + n * 8, 8)
                grad_x[pl.ds(at, 8), :] = forward(taps, i)
        return carry

    lax.fori_loop(0, 10, along_x, 0)

    def along_y(x, carry):
        taps = [every(padded, (x + 8) * PAD + 4 + d, 5) for d in range(-3, 9)]
        for j in range(5):
            put_every(grad_y, x * WIDE + j, 5, forward(taps, j))
        return carry

    lax.fori_loop(0, CX, along_y, 0)
    kick_source(0, cells, amps, pres)
    for push in pull_all(zip(scratch[:5], outs), out_sem):
        push.wait()


def kick_source(step, cells, amps, field):
    s, g, h = place()
    x = cells[s, 0] - g * CX
    y = cells[s, 1] - h * CY

    @pl.when((x >= 0) & (x < CX) & (y >= 0) & (y < CY))
    def _():
        at = x * CY + y
        lane = lax.broadcasted_iota(jnp.int32, (1, 128), 1)
        kick = time_step * amps[s, step]
        field[pl.ds(at, 1), :] = field[pl.ds(at, 1), :] + jnp.where(lane == cells[s, 2], kick, 0.0)


def step0_kernel(corners, mat_b, window, *refs):
    sources, outs, scratch = refs[:7], refs[7:17], refs[17:]
    new_p, wide_x, wide_y, new_z, buoy, modu, gy_b, gy_a, gx_b, gx_a = outs
    pres, in_x, in_y, in_z, grad_x, grad_y, grad_z, rho, spread, sem = scratch
    order = (6, 3, 4, 1, 0, 5, 2)
    pulls = pull_all([(sources[i], scratch[i]) for i in order], sem)
    unpack_model(corners, window, buoy, modu, rho)

    def wait(*which):
        for i in which:
            pulls[i].wait()

    def tiles(count, per):
        return [(x, n, (x * per + n) * 8) for x in range(count) for n in range(per)]

    wait(0, 1)
    for x, n, at in tiles(CX, 4):
        new_z[at : at + 8, :] = in_z[at : at + 8, :] - buoy_at(buoy, x, n * 8) * grad_z[at : at + 8, :]
    for chunk in range(8):
        rows = slice(chunk * 128, (chunk + 1) * 128)
        spread[rows, :] = depth_difference(new_z[rows, :], mat_b)
    wait(2, 3)
    for x, n, at in tiles(WIDE, 4):
        wide_x[at : at + 8, :] = (
            in_x[at : at + 8, :] - buoy_at(buoy, x - 4, n * 8) * grad_x[at : at + 8, :]
        )
    for x0 in range(0, CX, 4):
        for n in range(4):
            mid = (x0 + 4) * CY + n * 8
            taps = [wide_x[mid + d * CY : mid + d * CY + 8, :] for d in range(-4, 7)]
            for i in range(4):
                at = (x0 + i) * CY + n * 8
                spread[at : at + 8, :] = spread[at : at + 8, :] + backward(taps, i)
    wait(4, 5, 6)
    for x, n, at in tiles(CX, 5):
        wide_y[at : at + 8, :] = (
            in_y[at : at + 8, :] - buoy_at(buoy, x, n * 8 - 4) * grad_y[at : at + 8, :]
        )
    for x in range(CX):
        taps = [every(wide_y, x * WIDE + 4 + d, 4) for d in range(-4, 7)]
        for j in range(4):
            at = x * CY + j
            total = every(spread, at, 4) + backward(taps, j)
            put_every(new_p, at, 4, every(pres, at, 4) - every(modu, at, 4) * total)
    send_faces(new_p, (gx_a, gx_b), (gy_a, gy_b), 0, HALO)


def inner_kernel(step, cells, amps, mat_f, mat_b, pres, in_x, in_y, in_z, buoy, *outs):
    wide_x, wide_y, new_z, spread, kicked = outs
    kicked[...] = pres[...]
    kick_source(step, cells, amps, kicked)
    for chunk in range(8):
        rows = slice(chunk * 128, (chunk + 1) * 128)
        grad = depth_difference(pres[rows, :], mat_f)
        light = jnp.concatenate(
            [buoy_at(buoy, x, 0, 32) for x in range(chunk * 4, chunk * 4 + 4)], axis=0
        )
        new_z[rows, :] = in_z[rows, :] - light * grad

    def along_x(chunk, carry):
        x0 = chunk * 4 + 4
        for n in range(4):
            taps = [
                pres[pl.ds(pl.multiple_of((x0 + d) * CY + n * 8, 8), 8), :] for d in range(-3, 8)
            ]
            for i in range(4):
                at = pl.multiple_of((x0 + i + 4) * CY + n * 8, 8)
                wide_x[pl.ds(at, 8), :] = in_x[pl.ds(at, 8), :] - buoy_at(
                    buoy, x0 + i, n * 8
                ) * forward(taps, i)
        return carry

    lax.fori_loop(0, 6, along_x, 0)

    def along_y(x, carry):
        taps = [every(pres, x * CY + 4 + d, 3) for d in range(-3, 7)]
        for j in range(3):
            at = x * WIDE + 8 + j
            light = every(buoy, (x + 4) * WIDE + 8 + j, 3)
            put_every(wide_y, at, 3, every(in_y, at, 3) - light * forward(taps, j))
        return carry

    lax.fori_loop(0, CX, along_y, 0, unroll=4)
    wide_x[0 : 8 * CY, :] = in_x[0 : 8 * CY, :]
    wide_x[32 * CY : 40 * CY, :] = in_x[32 * CY : 40 * CY, :]
    for x in range(CX):
        wide_y[x * WIDE : x * WIDE + 8, :] = in_y[x * WIDE : x * WIDE + 8, :]
        wide_y[x * WIDE + 32 : x * WIDE + 40, :] = in_y[x * WIDE + 32 : x * WIDE + 40, :]
    for chunk in range(8):
        rows = slice(chunk * 128, (chunk + 1) * 128)
        spread[rows, :] = depth_difference(new_z[rows, :], mat_b)

    def across(chunk, carry):
        x0 = chunk * 4 + 8
        for n in range(4):
            taps = [
                wide_x[pl.ds(pl.multiple_of((x0 + d + 4) * CY + n * 8, 8), 8), :]
                for d in range(-4, 7)
            ]
            for i in range(4):
                at = pl.multiple_of((x0 + i) * CY + n * 8, 8)
                spread[pl.ds(at, 8), :] = spread[pl.ds(at, 8), :] + backward(taps, i)
        return carry

    lax.fori_loop(0, 4, across, 0)

    def along(x, carry):
        taps = [every(wide_y, x * WIDE + 12 + d, 2) for d in range(-4, 5)]
        for j in range(2):
            at = x * CY + 8 + j
            put_every(spread, at, 2, every(spread, at, 2) + backward(taps, j))
        return carry

    lax.fori_loop(0, CX, along, 0, unroll=4)


def edge_kernel(step, *refs):
    pres, gy_b, gy_a, gx_b, gx_a, in_x, in_y, buoy, modu, spread, kicked = refs[:11]
    last = step == STEPS - 1
    if last:
        p_to, x_to, y_to, rim_x, rim_y, wide_x, wide_y, new_p, out_y, sem = refs[11:]
        pushes = []

        def push(src, dst, rows):
            pushes.append(pltpu.make_async_copy(src, dst.at[rows], sem.at[len(pushes)]))
            pushes[-1].start()

    else:
        new_p, wide_x, wide_y, to_d, to_c, to_b, to_a, rim_x, rim_y = refs[11:]
    s, g, h = place()
    end_x = (g == 0) | (g == 3)
    end_y = (h == 0) | (h == 7)
    for which in range(2):
        low = odd(g) if which == 0 else jnp.logical_not(odd(g))
        start = jnp.where(low, 1, 24) * CY
        for i in range(HALO):
            for part in range(4):
                at = pl.multiple_of(start + (i * CY + part * 8), 8)
                rim_x[pl.ds(at, 8), :] = received((gx_a, gx_b), which, end_x, i * 32 + part * 8)
        low = odd(h) if which == 0 else jnp.logical_not(odd(h))
        start = jnp.where(low, 1, CX * STRIP + 8)
        for c in range(HALO):
            for part in range(4):
                value = received((gy_a, gy_b), which, end_y, c * 32 + part * 8)
                put_every(rim_y, start + (part * 8 * STRIP + c), STRIP, value)
    rim_x[8 * CY : 24 * CY, :] = jnp.concatenate([pres[0 : 8 * CY, :], pres[24 * CY : 32 * CY, :]], axis=0)
    for x in range(CX):
        rim_y[x * STRIP + 8 : x * STRIP + 16, :] = pres[x * CY : x * CY + 8, :]
        at = (CX + x) * STRIP
        rim_y[at : at + 8, :] = pres[x * CY + 24 : x * CY + 32, :]
    wide_x[8 * CY : 32 * CY, :] = in_x[8 * CY : 32 * CY, :]
    for x in range(CX):
        wide_y[x * WIDE + 8 : x * WIDE + 32, :] = in_y[x * WIDE + 8 : x * WIDE + 32, :]
    for rim, first in ((0, -4), (16, 28)):
        for half in range(2):
            for n in range(4):
                mid = (rim + half * 4 + 4) * CY + n * 8
                taps = [rim_x[mid + d * CY : mid + d * CY + 8, :] for d in range(-3, 8)]
                for i in range(4):
                    x = first + half * 4 + i
                    at = (x + 4) * CY + n * 8
                    wide_x[at : at + 8, :] = in_x[at : at + 8, :] - buoy_at(
                        buoy, x, n * 8
                    ) * forward(taps, i)

    if last:
        push(wide_x.at[pl.ds(4 * CY, CX * CY)], x_to, pl.ds(0, CX * CY))
    for x in range(CX):
        for rim, col in ((0, 0), (CX, 32)):
            mid = (rim + x) * STRIP + 4
            taps = [rim_y[mid + d : mid + d + 8, :] for d in range(-3, 5)]
            at = x * WIDE + col
            wide_y[at : at + 8, :] = in_y[at : at + 8, :] - buoy_at(buoy, x, col - 4) * forward(taps, 0)

    for first, count in ((0, 2), (24, 2), (8, 4)) if not last else ((0, 2), (24, 2), (8, 3), (20, 1)):
        for x0 in range(first, first + count * 4, 4):
            part_x = {}
            if first in (0, 24):
                for n in range(4):
                    taps = [
                        wide_x[(x0 + d + 4) * CY + n * 8 : (x0 + d + 4) * CY + n * 8 + 8, :]
                        for d in range(-4, 7)
                    ]
                    for i in range(4):
                        part_x[i, n] = backward(taps, i)
            for i in range(4):
                for n in range(4):
                    at = (x0 + i) * CY + n * 8
                    total = spread[at : at + 8, :]
                    if n in (0, 3):
                        mid = (x0 + i) * WIDE + 4 + n * 8
                        taps = [wide_y[mid + d : mid + d + 8, :] for d in range(-4, 4)]
                        total = total + backward(taps, 0)
                    if first in (0, 24):
                        total = total + part_x[i, n]
                    new_p[at : at + 8, :] = kicked[at : at + 8, :] - modu[at : at + 8, :] * total
        if last:
            for x in range(first, first + count * 4):
                out_y[x * CY : (x + 1) * CY, :] = wide_y[x * WIDE + 4 : x * WIDE + 36, :]
            part = pl.ds(first * CY, count * 4 * CY)
            push(new_p.at[part], p_to, part)
            push(out_y.at[part], y_to, part)
    if last:
        for copy in pushes:
            copy.wait()
    else:
        send_faces(new_p, (to_a, to_b), (to_c, to_d), 0, HALO)


def shape(rows, dtype=f32):
    return jax.ShapeDtypeStruct((rows, 128), dtype)


def vmem(rows):
    return pltpu.VMEM((rows, 128), f32)


def call(kernel, outs, args, scratch, name, smem=0, hbm=(), loose=(), to_hbm=(), cost=None):
    spaces = [
        pltpu.SMEM if i < smem else pltpu.HBM if i in hbm else pl.ANY if i in loose else pltpu.VMEM
        for i in range(len(args))
    ]
    to_hbm = range(len(outs)) if to_hbm is True else to_hbm
    outs = [pltpu.HBM(o.shape, o.dtype) if i in to_hbm else o for i, o in enumerate(outs)]
    places = [pltpu.HBM if i in to_hbm else pltpu.VMEM for i in range(len(outs))]
    specs = [pl.BlockSpec(memory_space=space) for space in spaces]
    args = [
        pltpu.with_memory_space_constraint(arg, pltpu.HBM) if i in hbm else arg
        for i, arg in enumerate(args)
    ]
    return pl.pallas_call(
        kernel,
        out_shape=outs,
        in_specs=specs,
        out_specs=[pl.BlockSpec(memory_space=place) for place in places],
        scratch_shapes=scratch,
        cost_estimate=cost,
        compiler_params=pltpu.CompilerParams(vmem_limit_bytes=24 * 1024 * 1024),
        name=name,
    )(*args)


GX, GY = 4, 8


def partners(match):
    out = []
    for s in range(4):
        for g in range(GX):
            for h in range(GY):
                to_s, to_g, to_h = match(s, g, h)
                out.append(((s * GX + g) * GY + h, (to_s * GX + to_g) * GY + to_h))
    return out


gx_near = partners(lambda s, g, h: (s, g ^ 1, h))
gx_far = partners(lambda s, g, h: (s ^ 1, g, h) if g in (0, GX - 1) else (s, 3 - g, h))
gy_near = partners(lambda s, g, h: (s, g, h ^ 1))
gy_far = partners(
    lambda s, g, h: (s ^ 1, g, h) if h in (0, GY - 1) else (s, g, ((h + 1) ^ 1) - 1)
)


def exchange(faces):
    gy_b = lax.ppermute(faces[0], DEVICES, gy_far)
    gx_b = lax.ppermute(faces[2], DEVICES, gx_far)
    gy_a = lax.ppermute(faces[1], DEVICES, gy_near)
    gx_a = lax.ppermute(faces[3], DEVICES, gx_near)
    return [gy_b, gy_a, gx_b, gx_a]


def shards(velocity, density, offsets, pressure, vel_x, vel_y, vel_z, source_cells, wavelet):
    mat_f, mat_b = (jnp.asarray(m) for m in depth_matrices())
    vel = velocity.reshape(16 * 64, 128)
    den = density.reshape(16 * 64, 128)
    pres = pressure.reshape(CX * CY, 128)
    flow_x = vel_x.reshape(CX * CY, 128)
    flow_y = vel_y.reshape(CX * CY, 128)
    flow_z = vel_z.reshape(CX * CY, 128)
    block = shape(CX * CY)
    wide = shape(WIDE * CY)
    face = shape(HALO * 32)
    cost = pl.CostEstimate(flops=20_000_000, bytes_accessed=8_000_000, transcendentals=0)
    long = pl.CostEstimate(flops=3 * 10**10, bytes_accessed=8_000_000, transcendentals=0)

    dma = pltpu.SemaphoreType.DMA
    (deal,) = call(
        pack_kernel,
        [shape(128 * 16)],
        [vel, den],
        [vmem(1024)] * 2 + [vmem(2048), dma((8,)), dma((4,))],
        "pack",
        hbm=range(2),
        to_hbm=True,
    )
    dealt = lax.all_to_all(deal.reshape(128, 16, 128), DEVICES, 0, 0, tiled=True)
    faces = call(
        face_kernel,
        [shape((HALO + 4) * 32)] * 4,
        [pres, flow_x, flow_y, deal],
        [vmem(1024)] * 3 + [dma((3,))],
        "first_faces",
        hbm=range(4),
        cost=cost,
    )
    faces = exchange(faces)
    (grad_z,) = call(
        depth_kernel,
        [block],
        [mat_f, pres],
        [vmem(CX * CY), vmem(CX * CY), dma((2,))],
        "step0_depth",
        hbm=(1,),
        to_hbm=True,
        cost=long,
    )
    (cut,) = call(
        cut_kernel,
        [jax.ShapeDtypeStruct((128, MESSAGE // 2, 2, 128), f32)],
        [dealt.reshape(128 * 16, 128), offsets, grad_z],
        [vmem(16 * LINE), vmem(16 * LINE), vmem(128 * MESSAGE), dma((4,))],
        "cut",
        hbm=(2,),
        to_hbm=True,
    )
    window = lax.all_to_all(cut, DEVICES, 0, 0, tiled=True)
    grad_x, grad_y, flow_x, flow_y, pres = call(
        grad0_kernel,
        [wide, wide, wide, wide, block],
        [source_cells, wavelet, pres, *faces, flow_x, flow_y],
        [vmem(WIDE * CY)] * 4 + [vmem(CX * CY)]
        + [vmem(PAD * PAD)] + [vmem(CX * CY)] * 2 + [dma((3,)), dma((5,))],
        "step0_gradients",
        smem=2,
        hbm=(2, 7, 8),
        to_hbm=True,
        cost=long,
    )
    pres, flow_x, flow_y, flow_z, buoy, modu, *faces = call(
        step0_kernel,
        [block, wide, wide, block, shape(WIDE * WIDE), block] + [face] * 4,
        [offsets, mat_b, window]
        + [pres, flow_x, flow_y, flow_z, grad_x, grad_y, grad_z],
        [vmem(CX * CY), vmem(WIDE * CY), vmem(WIDE * CY), vmem(CX * CY)]
        + [vmem(WIDE * CY), vmem(WIDE * CY), vmem(CX * CY)]
        + [vmem(WIDE * WIDE), vmem(CX * CY), dma((7,))],
        "step0",
        hbm=range(3, 10),
    )
    for step in range(1, STEPS):
        last = step == STEPS - 1
        faces = exchange(faces)
        flow_x, flow_y, flow_z, spread, kicked = call(
            functools.partial(inner_kernel, step),
            [wide, wide, block, block, block],
            [source_cells, wavelet, mat_f, mat_b, pres, flow_x, flow_y, flow_z, buoy],
            [],
            f"inner{step}",
            smem=2,
            cost=cost,
        )
        pres, flow_x, flow_y, *faces = call(
            functools.partial(edge_kernel, step),
            [block, block, block] if last else [block, wide, wide] + [face] * 4,
            [pres, *faces, flow_x, flow_y, buoy, modu, spread, kicked],
            [vmem(32 * CY), vmem(2 * CX * STRIP)]
            + ([vmem(WIDE * CY)] * 2 + [vmem(CX * CY)] * 2 + [dma((9,))] if last else []),
            f"edge{step}",
            to_hbm=last or (),
        )
    return tuple(a.reshape(1, CX, CY, 128) for a in (pres, flow_x, flow_y, flow_z))


def solution(mesh):
    return jax.shard_map(
        shards,
        mesh=mesh,
        in_specs=(
            P(("shot", "gx"), "gy", None),
            P(("shot", "gx"), "gy", None),
            P(),
            P("shot", "gx", "gy", None),
            P("shot", "gx", "gy", None),
            P("shot", "gx", "gy", None),
            P("shot", "gx", "gy", None),
            P(),
            P(),
        ),
        out_specs=(
            P("shot", "gx", "gy", None),
            P("shot", "gx", "gy", None),
            P("shot", "gx", "gy", None),
            P("shot", "gx", "gy", None),
        ),
        check_vma=False,
    )
```
